128 devices in a mesh: dp: 64 (over z_lo, y, x, core), mp: 2 (over z_hi).
Axes of the slice: x: 4, y: 4, z: 4 (z_hi: 2, z_lo: 2; z = z_hi * 2 + z_lo), core: 2. Of those that a mesh axis runs over, the one named last changes fastest.
Arguments:
- lowres_in: bfloat16 [384, 1, 24, 1024], P('dp'), may hold values from -6 to 6
- highres_in: bfloat16 [768, 1, 48, 1536], P('dp'), may hold values from -6 to 6
- image_sizes: int32 [16], replicated, may hold values from 24 to 48, as said below
- attn_gain: bfloat16 [1024], replicated, may hold values from 0.5 to 1.5
- query_weight: bfloat16 [1024, 1024], P('dp', 'mp'), may hold values from -0.1875 to 0.1875
- key_weight: bfloat16 [1024, 1024], P('dp', 'mp'), may hold values from -0.1875 to 0.1875
- value_weight: bfloat16 [1024, 1024], P('dp', 'mp'), may hold values from -0.1875 to 0.1875
- output_weight: bfloat16 [1024, 1024], P('mp', 'dp'), may hold values from -0.75 to 0.75
- mlp_gain: bfloat16 [1024], replicated, may hold values from 0.5 to 1.5
- up_weight: bfloat16 [1024, 4096], P('dp', 'mp'), may hold values from -0.1875 to 0.1875
- down_weight: bfloat16 [4096, 1024], P('mp', 'dp'), may hold values from -0.09375 to 0.09375
- depth_kernel: bfloat16 [49, 1536], replicated, may hold values from -0.875 to 0.875
- conv_gain: bfloat16 [1536], replicated, may hold values from 0.5 to 1.5
- expand_weight: bfloat16 [1536, 6144], P('dp', 'mp'), may hold values from -0.15625 to 0.15625
- shrink_weight: bfloat16 [6144, 1536], P('mp', 'dp'), may hold values from -0.078125 to 0.078125
- layer_scale: bfloat16 [1536], replicated, may hold values from 0.5 to 1.5
- adapter_weight: bfloat16 [1536, 1024], P('dp', 'mp'), may hold values from -0.15625 to 0.15625
- adapter_kernel: bfloat16 [9, 1024], P(None, 'mp'), may hold values from -2 to 2
- gate_vector: bfloat16 [1024], replicated, may hold values from -0.1875 to 0.1875
- out_cotangent: bfloat16 [384, 1, 24, 1024], P('dp', None, None, 'mp'), may hold values from -6 to 6
- map_cotangent: bfloat16 [768, 1, 48, 1536], P('dp'), may hold values from -6 to 6
Outputs:
- mixed_out: bfloat16 [384, 1, 24, 1024], P('dp', None, None, 'mp')
- map_out: bfloat16 [768, 1, 48, 1536], P('dp')
- lowres_grad: float32 [384, 1, 24, 1024], P('dp')
- highres_grad: float32 [768, 1, 48, 1536], P('dp')
- attn_gain_grad: float32 [1024], replicated
- query_weight_grad: float32 [1024, 1024], P('dp', 'mp')
- key_weight_grad: float32 [1024, 1024], P('dp', 'mp')
- value_weight_grad: float32 [1024, 1024], P('dp', 'mp')
- output_weight_grad: float32 [1024, 1024], P('mp', 'dp')
- mlp_gain_grad: float32 [1024], replicated
- up_weight_grad: float32 [1024, 4096], P('dp', 'mp')
- down_weight_grad: float32 [4096, 1024], P('mp', 'dp')
- depth_kernel_grad: float32 [49, 1536], replicated
- conv_gain_grad: float32 [1536], replicated
- expand_weight_grad: float32 [1536, 6144], P('dp', 'mp')
- shrink_weight_grad: float32 [6144, 1536], P('mp', 'dp')
- layer_scale_grad: float32 [1536], replicated
- adapter_weight_grad: float32 [1536, 1024], P('dp', 'mp')
- adapter_kernel_grad: float32 [9, 1024], P(None, 'mp')
- gate_vector_grad: float32 [1024], replicated
The draws below stay inside these ranges and needn't reach their ends.
Inputs may be any that keep to these rules, and one draw needn't show every extreme that they name: `image_sizes`: each image's valid side is 24, 32 or 48, and at least one image has 48.
All inputs are finite; a program needn't handle non-finite values.
Results may differ from the reference program's by a relative error of at most 0.018.
Values may be sent and summed in bfloat16 or wider, within the bound.
No kernel may reach another device: no remote copies, remote signals or barrier semaphores. Data moves between devices by JAX's collectives and lax.ppermute only.
A program may use at most 256 MiB of HBM per device.

```python
import jax
import jax.numpy as jnp
from jax import lax

D = 1024
HEADS = 16
HD = 64
FF = 4096
C = 1536
CF = 6144
GRID = 24
HR = 48
TILES = 4
IMG_GRP = 1
IMAGES = 16
LR_ROWS = 384
HR_ROWS = 768
N_DP = 64


def draw_image_sizes(key, part):
    key = jax.random.fold_in(key, 11)
    class_key, pick_key = jax.random.split(key)
    classes = jax.random.randint(class_key, (IMAGES,), 0, 3)
    extents = jnp.where(classes == 0, HR // 2, jnp.where(classes == 1, 2 * HR // 3, HR))
    chosen = jax.random.randint(pick_key, (), 0, IMAGES)
    return jnp.where(jnp.arange(IMAGES) == chosen, HR, extents).astype(jnp.int32)


def shard_levels(rng, shape, pieces, smallest, largest):
    gain, own = 1.0, jax.random.fold_in(rng, 6)
    for dim, shards_of in pieces:
        steps = jnp.exp(jax.random.uniform(jax.random.fold_in(own, dim), (shards_of,), jnp.float32, smallest / len(pieces), largest / len(pieces)))
        gain = gain * jnp.repeat(steps, shape[dim] // shards_of).reshape([-1 if axis == dim else 1 for axis in range(len(shape))])
    return gain


def normal_values(key, shape, deviation, reach, pieces=(), dtype=jnp.bfloat16):
    entries = deviation * jax.random.normal(key, shape, jnp.float32)
    if pieces:
        entries = entries * shard_levels(key, shape, pieces, -0.22, 0.18)
    return jnp.clip(entries, -reach, reach).astype(dtype)


def setup_inputs(seed: int = 0) -> dict:
    streams_of = jax.random.split(jax.random.key(seed), 22)
    lowres_in = normal_values(streams_of[0], (LR_ROWS, IMG_GRP, GRID, D), 1.0, 6.0, ((0, 64),))
    highres_in = normal_values(streams_of[1], (HR_ROWS, IMG_GRP, HR, C), 1.0, 6.0, ((0, 64),))
    image_sizes = draw_image_sizes(jax.random.fold_in(streams_of[21], 71), 0)
    attn_gain = jnp.clip(1.0 + 0.1 * jax.random.normal(streams_of[3], (D,), jnp.float32), 0.5, 1.5).astype(jnp.bfloat16)
    query_weight = normal_values(streams_of[4], (D, D), D ** -0.5, 0.1875, ((0, 64), (1, 2)))
    key_weight = normal_values(streams_of[5], (D, D), D ** -0.5, 0.1875, ((0, 64), (1, 2)))
    value_weight = normal_values(streams_of[6], (D, D), D ** -0.5, 0.1875, ((0, 64), (1, 2)))
    output_weight = normal_values(streams_of[7], (D, D), (D // 16) ** -0.5, 0.75, ((0, 2), (1, 64)))
    mlp_gain = jnp.clip(1.0 + 0.1 * jax.random.normal(streams_of[8], (D,), jnp.float32), 0.5, 1.5).astype(jnp.bfloat16)
    up_weight = normal_values(streams_of[9], (D, FF), D ** -0.5, 0.1875, ((0, 64), (1, 2)))
    down_weight = normal_values(streams_of[10], (FF, D), FF ** -0.5, 0.09375, ((0, 2), (1, 64)))
    depth_kernel = normal_values(streams_of[11], (49, C), 49 ** -0.5, 0.875)
    conv_gain = jnp.clip(1.0 + 0.1 * jax.random.normal(streams_of[12], (C,), jnp.float32), 0.5, 1.5).astype(jnp.bfloat16)
    expand_weight = normal_values(streams_of[13], (C, CF), C ** -0.5, 0.15625, ((0, 64), (1, 2)))
    shrink_weight = normal_values(streams_of[14], (CF, C), CF ** -0.5, 0.078125, ((0, 2), (1, 64)))
    layer_scale = jnp.clip(1.0 + 0.1 * jax.random.normal(streams_of[15], (C,), jnp.float32), 0.5, 1.5).astype(jnp.bfloat16)
    adapter_weight = normal_values(streams_of[16], (C, D), C ** -0.5, 0.15625, ((0, 64), (1, 2)))
    adapter_kernel = normal_values(streams_of[17], (9, D), 9 ** -0.5, 2.0, ((1, 2),))
    gate_vector = normal_values(streams_of[18], (D,), D ** -0.5, 0.1875)
    out_cotangent = normal_values(streams_of[19], (LR_ROWS, IMG_GRP, GRID, D), 1.0, 6.0, ((0, 64), (3, 2)))
    map_cotangent = normal_values(streams_of[20], (HR_ROWS, IMG_GRP, HR, C), 1.0, 6.0, ((0, 64),))
    return {"lowres_in": lowres_in, "highres_in": highres_in, "image_sizes": image_sizes, "attn_gain": attn_gain, "query_weight": query_weight, "key_weight": key_weight, "value_weight": value_weight, "output_weight": output_weight, "mlp_gain": mlp_gain, "up_weight": up_weight, "down_weight": down_weight, "depth_kernel": depth_kernel, "conv_gain": conv_gain, "expand_weight": expand_weight, "shrink_weight": shrink_weight, "layer_scale": layer_scale, "adapter_weight": adapter_weight, "adapter_kernel": adapter_kernel, "gate_vector": gate_vector, "out_cotangent": out_cotangent, "map_cotangent": map_cotangent}


@jax.custom_vjp
def low(v):
    return lax.optimization_barrier(v.astype(jnp.bfloat16)).astype(jnp.float32)

@jax.custom_vjp
def low_back(v):
    return v

def low_keep(v):
    return (low(v), None)

def low_pass(kept, grad):
    return (grad,)

def back_keep(v):
    return (v, None)

def back_low(kept, grad):
    return (low(grad),)
low.defvjp(low_keep, low_pass)
low_back.defvjp(back_keep, back_low)
norm_epsilon = 1e-06
highest = lax.Precision.HIGHEST

def layer_norm(values, scale_gain):
    average = lax.optimization_barrier(jnp.mean(values, axis=-1, keepdims=True))
    centred = values - average
    spread = lax.optimization_barrier(jnp.mean(centred * centred, axis=-1, keepdims=True))
    return centred * lax.rsqrt(spread + norm_epsilon) * scale_gain

def product(former, latter):
    return jnp.dot(former, latter, precision=highest)

def depthwise(picture, kernel, radius):
    height, breadth = (picture.shape[0], picture.shape[1])
    window = 2 * radius + 1
    padded = jnp.pad(picture, ((radius, radius), (radius, radius), (0, 0)))
    summed = jnp.zeros(picture.shape, jnp.float32)
    for row_shift in range(window):
        for across in range(window):
            summed = summed + padded[row_shift:row_shift + height, across:across + breadth] * kernel[row_shift * window + across]
    return summed

def to_images(values, stripe):
    groups = N_DP // TILES
    rolled = jnp.roll(values, 2 * stripe, axis=0)
    shaped = rolled.reshape(groups, TILES, stripe, IMG_GRP, values.shape[2], values.shape[3])
    return shaped.transpose(0, 3, 1, 2, 4, 5).reshape(groups * IMG_GRP, TILES * stripe, values.shape[2], values.shape[3])

def from_images(values, stripe):
    groups = N_DP // TILES
    shaped = values.reshape(groups, IMG_GRP, TILES, stripe, values.shape[2], values.shape[3])
    flat = shaped.transpose(0, 2, 3, 1, 4, 5).reshape(groups * TILES * stripe, IMG_GRP, values.shape[2], values.shape[3])
    return jnp.roll(flat, -2 * stripe, axis=0)

def image_layer(weights, lowres, highres, extent):
    attn_gain, query_weight, key_weight, value_weight, output_weight, mlp_gain, up_weight, down_weight, depth_kernel, conv_gain, expand_weight, shrink_weight, layer_scale, adapter_weight, adapter_kernel, gate_vector = weights
    patches = GRID * GRID
    token_rows = lowres.reshape(patches, D)
    normed = low(layer_norm(token_rows, attn_gain))
    queries = low_back(low(product(normed, query_weight))).reshape(patches, HEADS, HD)
    key_rows = low_back(low(product(normed, key_weight))).reshape(patches, HEADS, HD)
    values = low_back(low(product(normed, value_weight))).reshape(patches, HEADS, HD)
    scores = low_back(jnp.einsum('qhd,khd->hqk', queries, key_rows, precision=highest) * HD ** (-0.5))
    attention = jax.nn.softmax(scores, axis=-1)
    attended = jnp.einsum('hqk,khd->qhd', low(attention), values, precision=highest).reshape(patches, D)
    attended = low_back(low(attended))
    hidden = token_rows + low_back(product(attended, output_weight))
    normed_two = low(layer_norm(hidden, mlp_gain))
    expanded = low_back(product(normed_two, up_weight))
    activated = low(jax.nn.gelu(expanded, approximate=False))
    result = hidden + low_back(product(activated, down_weight))
    positions = jnp.arange(HR)
    inside = (positions < extent).astype(jnp.float32)
    valid_mask = (inside[:, None] * inside[None, :])[:, :, None]
    masked = highres * valid_mask
    convolved = low_back(depthwise(masked, depth_kernel, 3)).reshape(HR * HR, C)
    normed_map = low(layer_norm(convolved, conv_gain))
    widened = low_back(product(normed_map, expand_weight))
    widened_act = low(jax.nn.gelu(widened, approximate=False))
    narrowed = low_back(product(widened_act, shrink_weight)).reshape(HR, HR, C)
    mapped = valid_mask * (masked + layer_scale * narrowed)
    pooled = lax.optimization_barrier(jnp.mean(mapped.reshape(GRID, 2, GRID, 2, C), axis=(1, 3))).reshape(patches, C)
    lifted = low_back(product(low(pooled), adapter_weight))
    grid_rows = result.reshape(GRID, GRID, D)
    local_mix = low_back(depthwise(low(grid_rows), adapter_kernel, 1)).reshape(patches, D)
    gating = jax.nn.sigmoid(lax.optimization_barrier(jnp.sum(result * gate_vector, axis=-1, keepdims=True)))
    blended = result + local_mix + gating * lifted
    return (blended.reshape(GRID, GRID, D), mapped)

def reference(lowres_in, highres_in, image_sizes, attn_gain, query_weight, key_weight, value_weight, output_weight, mlp_gain, up_weight, down_weight, depth_kernel, conv_gain, expand_weight, shrink_weight, layer_scale, adapter_weight, adapter_kernel, gate_vector, out_cotangent, map_cotangent):
    weights = tuple((element.astype(jnp.float32) for element in (attn_gain, query_weight, key_weight, value_weight, output_weight, mlp_gain, up_weight, down_weight, depth_kernel, conv_gain, expand_weight, shrink_weight, layer_scale, adapter_weight, adapter_kernel, gate_vector)))
    low_stripe = GRID // TILES
    high_stripe = HR // TILES
    low_grid = to_images(lowres_in.astype(jnp.float32), low_stripe)
    high_grid = to_images(highres_in.astype(jnp.float32), high_stripe)
    per_image = jax.checkpoint(image_layer)

    def forward(low_grid, high_grid, weights):

        def apply_one(element):
            return per_image(weights, element[0], element[1], element[2])
        return lax.map(apply_one, (low_grid, high_grid, image_sizes))
    (blended, mapped), pullback = jax.vjp(forward, low_grid, high_grid, weights)
    low_slope, high_slope, slopes = pullback((to_images(out_cotangent.astype(jnp.float32), low_stripe), to_images(map_cotangent.astype(jnp.float32), high_stripe)))
    attn_gain_grad, query_weight_grad, key_weight_grad, value_weight_grad, output_weight_grad, mlp_gain_grad, up_weight_grad, down_weight_grad, depth_kernel_grad, conv_gain_grad, expand_weight_grad, shrink_weight_grad, layer_scale_grad, adapter_weight_grad, adapter_kernel_grad, gate_vector_grad = slopes
    return (from_images(blended, low_stripe).astype(jnp.bfloat16), from_images(mapped, high_stripe).astype(jnp.bfloat16), from_images(low_slope, low_stripe), from_images(high_slope, high_stripe), attn_gain_grad, query_weight_grad, key_weight_grad, value_weight_grad, output_weight_grad, mlp_gain_grad, up_weight_grad, down_weight_grad, depth_kernel_grad, conv_gain_grad, expand_weight_grad, shrink_weight_grad, layer_scale_grad, adapter_weight_grad, adapter_kernel_grad, gate_vector_grad)
```

```python
import functools

import jax
import jax.numpy as jnp
from jax import lax
from jax.experimental import pallas as pl
from jax.experimental.pallas import tpu as pltpu
from jax.sharding import PartitionSpec as P

HD = 64
TILES = 4
CHIPS = 32
CORE = 1
RINGS = (2, 6, 8, 24, 32)

norm_epsilon = 1e-06

LANES = 128
RADIUS = 3
WINDOW = 7
PAD = 8


def masked_rows(place, main_ref, low_ref, high_ref, wide, strip, side, bounded):
    first, extent = place[0], place[1]
    cols = lax.broadcasted_iota(jnp.int32, (side, LANES), 0)

    def put(slot, value):
        row = first + slot - RADIUS
        limit = extent if bounded else side
        keep = (cols < limit) & (row >= 0) & (row < limit)
        wide[slot] = jnp.where(keep, value.astype(jnp.float32), 0.0)

    for slot in range(RADIUS):
        put(slot, low_ref[slot])
        put(RADIUS + strip + slot, high_ref[slot])
    for slot in range(strip):
        put(RADIUS + slot, main_ref[slot])


def window_sum(wide, taps_ref, shifted, row, side, flipped):
    sums = [None] * WINDOW
    for a in range(WINDOW):
        line = wide[row + a]
        for b in range(WINDOW):
            tap = WINDOW * a + b
            if flipped:
                tap = WINDOW * WINDOW - 1 - tap
            term = line * taps_ref[tap : tap + 1]
            sums[b] = term if sums[b] is None else sums[b] + term
    total = sums[RADIUS]
    for b in range(WINDOW):
        if b != RADIUS:
            shifted[b, PAD : PAD + side] = sums[b]
    for b in range(WINDOW):
        if b != RADIUS:
            total = total + shifted[b, PAD + b - RADIUS : PAD + b - RADIUS + side]
    return total


def clear_edges(shifted, side):
    for b in range(WINDOW):
        shifted[b, 0:PAD] = jnp.zeros((PAD, LANES), jnp.float32)
        shifted[b, PAD + side : 2 * PAD + side] = jnp.zeros((PAD, LANES), jnp.float32)


def forward_kernel(place, main_ref, low_ref, high_ref, taps_in, out_ref, wide, taps, shifted):
    strip, side = main_ref.shape[0], main_ref.shape[1]
    masked_rows(place, main_ref, low_ref, high_ref, wide, strip, side, True)
    clear_edges(shifted, side)
    taps[...] = taps_in[...].astype(jnp.float32)

    def step(row, carry):
        out_ref[row] = window_sum(wide, taps, shifted, row, side, False)
        return carry

    lax.fori_loop(0, strip, step, 0)


def backward_kernel(place, main_ref, low_ref, high_ref, taps_in, add_ref, out_ref, wide, taps, shifted):
    strip, side = main_ref.shape[0], main_ref.shape[1]
    masked_rows(place, main_ref, low_ref, high_ref, wide, strip, side, False)
    clear_edges(shifted, side)
    taps[...] = taps_in[...].astype(jnp.float32)
    cols = lax.broadcasted_iota(jnp.int32, (side, LANES), 0)

    def step(row, carry):
        total = window_sum(wide, taps, shifted, row, side, True) + add_ref[row]
        keep = (cols < place[1]) & (place[0] + row < place[1])
        out_ref[row] = jnp.where(keep, total, 0.0)
        return carry

    lax.fori_loop(0, strip, step, 0)


def slope_kernel(place, main_ref, low_ref, high_ref, grad_ref, out_ref, wide, padded):
    strip, side = main_ref.shape[0], main_ref.shape[1]
    masked_rows(place, main_ref, low_ref, high_ref, wide, strip, side, True)
    edge = jnp.zeros((PAD, LANES), jnp.float32)
    for row in range(strip):
        padded[row, 0:PAD] = edge
        padded[row, PAD : PAD + side] = grad_ref[row].astype(jnp.float32)
        padded[row, PAD + side : 2 * PAD + side] = edge
    for group in ((0, 1, 2, 3), (4, 5, 6)):

        def step(row, sums):
            lines = [wide[row + a] for a in group]
            fresh = list(sums)
            for b in range(WINDOW):
                start = PAD + RADIUS - b
                part = padded[row, start : start + side]
                for i in range(len(group)):
                    term = (lines[i] * part).reshape(side // 8, 8, LANES)
                    fresh[i * WINDOW + b] = fresh[i * WINDOW + b] + jnp.sum(term, axis=0)
            return tuple(fresh)

        start = tuple(jnp.zeros((8, LANES), jnp.float32) for _ in range(len(group) * WINDOW))
        sums = lax.fori_loop(0, strip, step, start)
        for i, a in enumerate(group):
            for b in range(WINDOW):
                tap = a * WINDOW + b
                out_ref[tap : tap + 1] = jnp.sum(sums[i * WINDOW + b], axis=0, keepdims=True)


def block3(rows, side):
    return pl.BlockSpec((rows, side, LANES), lambda i: (0, 0, i))


SCALARS = pl.BlockSpec(memory_space=pltpu.SMEM)


def map_conv(place, main, low, high, taps, added=None):
    strip, side, channels = main.shape
    count = taps.shape[0]
    tap_spec = pl.BlockSpec((count, LANES), lambda i: (0, i))
    specs = [SCALARS, block3(strip, side), block3(RADIUS, side), block3(RADIUS, side), tap_spec]
    args = [place, main, low, high, taps]
    if added is not None:
        specs.append(block3(strip, side))
        args.append(added)
    work = strip * side * channels
    return pl.pallas_call(
        forward_kernel if added is None else backward_kernel,
        grid=(channels // LANES,),
        in_specs=specs,
        out_specs=block3(strip, side),
        out_shape=jax.ShapeDtypeStruct((strip, side, channels), jnp.float32),
        scratch_shapes=[
            pltpu.VMEM((strip + 2 * RADIUS, side, LANES), jnp.float32),
            pltpu.VMEM((count, LANES), jnp.float32),
            pltpu.VMEM((WINDOW, side + 2 * PAD, LANES), jnp.float32),
        ],
        compiler_params=pltpu.CompilerParams(vmem_limit_bytes=24 * 1024 * 1024),
        cost_estimate=pl.CostEstimate(flops=2 * count * work, bytes_accessed=8 * work, transcendentals=0),
    )(*args)


def map_slopes(place, main, low, high, grad):
    strip, side, channels = main.shape
    count = WINDOW * WINDOW
    work = strip * side * channels
    return pl.pallas_call(
        slope_kernel,
        grid=(channels // LANES,),
        in_specs=[SCALARS, block3(strip, side), block3(RADIUS, side), block3(RADIUS, side), block3(strip, side)],
        out_specs=pl.BlockSpec((count, LANES), lambda i: (0, i)),
        out_shape=jax.ShapeDtypeStruct((count, channels), jnp.float32),
        scratch_shapes=[
            pltpu.VMEM((strip + 2 * RADIUS, side, LANES), jnp.float32),
            pltpu.VMEM((strip, side + 2 * PAD, LANES), jnp.float32),
        ],
        compiler_params=pltpu.CompilerParams(vmem_limit_bytes=24 * 1024 * 1024),
        cost_estimate=pl.CostEstimate(flops=2 * count * work, bytes_accessed=4 * work, transcendentals=0),
    )(place, main, low, high, grad)


def rotated(start):
    return tuple(RINGS[(start + i) % len(RINGS)] for i in range(len(RINGS)))


def xor_swap(values, mask):
    count = lax.axis_size("dp")
    return lax.ppermute(values, "dp", [(i, i ^ mask) for i in range(count)])


def chip_steps(offset):
    x, y, z = offset & 3, (offset >> 2) & 3, offset >> 4
    return {2: (x ^ (x >> 1)) & 1, 6: x >> 1, 8: (y ^ (y >> 1)) & 1, 24: y >> 1, 32: z}


def gather_place(offset, order):
    steps = chip_steps(offset)
    place = steps[order[0]]
    for k in range(1, len(order)):
        place = place + (steps[order[k]] << k)
    return place


def scatter_place(offset, order):
    return gather_place(offset, order[::-1])


def gathered_part(block, order):
    held = block[None]
    for mask in order:
        held = jnp.concatenate([held, xor_swap(held, mask)], axis=0)
    return held


def scattered_part(held, order):
    for mask in order:
        half = held.shape[0] // 2
        kept, given = held[:half], held[half:]
        summed = kept.astype(jnp.float32) + xor_swap(given, mask).astype(jnp.float32)
        held = summed if half == 1 else summed.astype(jnp.bfloat16)
    return held[0]


def route_kernel(moves, n_in, n_out, place, *refs):
    ins, outs = refs[:n_in], refs[n_in : n_in + n_out]
    held = refs[n_in + n_out : n_in + 2 * n_out]
    sems = refs[n_in + 2 * n_out]
    device = place[0]
    chip, core = device >> 1, device & 1

    for target in range(n_out):

        def step(offset, carry):
            for source, take, goal, put, source_box, target_box in moves:
                if goal == target:
                    pltpu.make_async_copy(
                        ins[source].at[(take(chip, core, offset),) + source_box],
                        held[goal].at[(put(chip, core, offset),) + target_box],
                        sems.at[goal],
                    ).start()
            return carry

        lax.fori_loop(0, CHIPS, step, 0)
    for target in range(n_out):
        pltpu.make_async_copy(held[target], held[target], sems.at[target]).wait()
        pltpu.make_async_copy(held[target], outs[target], sems.at[target]).start()
    for target in range(n_out):
        pltpu.make_async_copy(held[target], outs[target], sems.at[target]).wait()


def route(moves, place, arrays, shapes):
    anywhere = pl.BlockSpec(memory_space=pl.ANY)
    volume = sum(2 * a.size for a in arrays)
    return pl.pallas_call(
        functools.partial(route_kernel, moves, len(arrays), len(shapes)),
        in_specs=[SCALARS] + [anywhere] * len(arrays),
        out_specs=[anywhere] * len(shapes),
        out_shape=[jax.ShapeDtypeStruct(s, jnp.bfloat16) for s in shapes],
        scratch_shapes=[pltpu.VMEM(s, jnp.bfloat16) for s in shapes]
        + [pltpu.SemaphoreType.DMA((len(shapes),))],
        compiler_params=pltpu.CompilerParams(vmem_limit_bytes=volume + volume // 4 + (4 << 20)),
        cost_estimate=pl.CostEstimate(flops=0, bytes_accessed=2 * volume, transcendentals=0),
    )(place, *arrays)


def box(rows, cols):
    return (pl.ds(rows[0], rows[1] - rows[0]), pl.ds(cols[0], cols[1] - cols[0]))


def overlap(first, second):
    low, high = max(first[0], second[0]), min(first[1], second[1])
    return (low, high) if low < high else None


def shifted_span(span, base):
    return (span[0] - base, span[1] - base)


def core_swap(values):
    return xor_swap(values, CORE)


def exchange(values):
    low = values.astype(jnp.bfloat16)
    other = lax.ppermute(low, "mp", [(0, 1), (1, 0)])
    return low.astype(jnp.float32) + other.astype(jnp.float32)


def halo_rows(block, width):
    count = lax.axis_size("dp")
    forward = [(i, (i + 1) % count) for i in range(count)]
    backward = [((i + 1) % count, i) for i in range(count)]
    low = lax.ppermute(block[block.shape[0] - width :], "dp", forward)
    high = lax.ppermute(block[:width], "dp", backward)
    return low, high


def normalize(values, scale_gain):
    average = jnp.mean(values, axis=-1, keepdims=True)
    centred = values - average
    spread = jnp.mean(centred * centred, axis=-1, keepdims=True)
    return centred * lax.rsqrt(spread + norm_epsilon) * scale_gain


def gelu_exact(values):
    return jax.nn.gelu(values, approximate=False)


def matmul(former, latter):
    return jnp.dot(former, latter, preferred_element_type=jnp.float32)


def matmul_nt(former, latter):
    return lax.dot_general(
        former, latter, (((1,), (1,)), ((), ())), preferred_element_type=jnp.float32
    )


def matmul_tn(former, latter):
    return lax.dot_general(
        former, latter, (((0,), (0,)), ((), ())), preferred_element_type=jnp.float32
    )


def pair_swap(values):
    chips = lax.axis_size("dp") // 2
    pairs = []
    for chip in range(chips):
        other = (chip + 1) % chips if chip % 2 else (chip - 1) % chips
        pairs += [(2 * chip + core, 2 * other + core) for core in range(2)]
    return lax.ppermute(values, "dp", pairs)


def with_edges(block, position):
    low, high = halo_rows(block, 1)
    low = jnp.where(position != 0, low, jnp.zeros_like(low))
    high = jnp.where(position != TILES - 1, high, jnp.zeros_like(high))
    return jnp.concatenate([low, block, high], axis=0).astype(jnp.float32)


def depth_apply(padded, kernel, radius):
    height = padded.shape[0] - 2 * radius
    breadth = padded.shape[1]
    window = 2 * radius + 1
    widened = jnp.pad(padded, ((0, 0), (radius, radius), (0, 0)))
    summed = jnp.zeros((height,) + padded.shape[1:], jnp.float32)
    for row_shift in range(window):
        for col_shift in range(window):
            summed = (
                summed
                + widened[row_shift : row_shift + height, col_shift : col_shift + breadth]
                * kernel[row_shift * window + col_shift]
            )
    return summed


def kernel_slopes(padded, gradient, radius):
    height, breadth = gradient.shape[0], gradient.shape[1]
    window = 2 * radius + 1
    widened = jnp.pad(padded, ((0, 0), (radius, radius), (0, 0)))
    columns = []
    for row_shift in range(window):
        for col_shift in range(window):
            columns.append(
                jnp.sum(
                    widened[row_shift : row_shift + height, col_shift : col_shift + breadth]
                    * gradient,
                    axis=(0, 1),
                )
            )
    return jnp.stack(columns, 0)


def own_half(first, core, axis, other=False):
    size = first.shape[axis] // 2
    low = lax.slice_in_dim(first, 0, size, axis=axis)
    high = lax.slice_in_dim(first, size, 2 * size, axis=axis)
    return jnp.where((core == 0) != other, low, high)


def in_core_order(own, other, core, axis):
    return jnp.where(
        core == 0,
        jnp.concatenate([own, other], axis=axis),
        jnp.concatenate([other, own], axis=axis),
    )


def all_weights(place, core, small_rows, adapter_weight, expand_weight, shrink_rows):
    depth = small_rows[0].shape[0]
    fine = expand_weight.shape[0]
    whole = jnp.concatenate(small_rows[:4], axis=1)
    wide = whole.shape[1]
    split = 3 * small_rows[0].shape[1]
    adapter_half = adapter_weight.shape[1] // 2
    private = jnp.concatenate(
        [
            jnp.concatenate([whole, small_rows[4], small_rows[5]], axis=0),
            jnp.concatenate([adapter_weight[:, :adapter_half], adapter_weight[:, adapter_half:]], axis=0),
        ],
        axis=1,
    )
    kept = jnp.concatenate([own_half(expand_weight, core, 1), own_half(shrink_rows, core, 1)], axis=1)
    given = jnp.concatenate(
        [own_half(expand_weight, core, 1, True), own_half(shrink_rows, core, 1, True)], axis=1
    )
    common = in_core_order(kept, core_swap(given), core, 0)
    hidden = common.shape[1] // 2
    rows = common.shape[0]
    middle = private.shape[1] // 2
    third = common.shape[1] // 3
    spans = [(0, middle), (middle, 2 * middle)] + [(i * third, (i + 1) * third) for i in range(3)]
    orders = [rotated(i) for i in range(5)]
    parts = [
        gathered_part((private if i < 2 else common)[:, low:high], orders[i])
        for i, (low, high) in enumerate(spans)
    ]
    arrays = [parts[0], core_swap(parts[0]), parts[1], core_swap(parts[1])] + parts[2:]
    shapes = [
        (2 * CHIPS, depth, split),
        (2 * CHIPS, depth, wide - split),
        (2 * CHIPS, depth, wide),
        (2 * CHIPS, depth, wide),
        (2 * CHIPS, rows, adapter_half),
        (CHIPS, rows, hidden),
        (CHIPS, rows, hidden),
    ]
    moves = []

    def add(source, order, target, rows_span, cols_span, part_span, out_span, plane):
        common_cols = overlap(cols_span, part_span)
        if common_cols is None:
            return
        take = lambda chip, core, offset: gather_place(offset, order)
        if plane is None:
            put = lambda chip, core, offset: chip ^ offset
        else:
            put = lambda chip, core, offset: 2 * (chip ^ offset) + (core ^ plane)
        moves.append(
            (
                source,
                take,
                target,
                put,
                box(rows_span, shifted_span(common_cols, part_span[0])),
                box(out_span, shifted_span(common_cols, cols_span[0])),
            )
        )

    for i in range(2):
        for plane in range(2):
            source = 2 * i + plane
            everything = ((0, (0, depth), (0, split)), (1, (0, depth), (split, wide)))
            for target, rows_span, cols_span in everything:
                add(source, orders[i], target, rows_span, cols_span, spans[i], (0, depth), plane)
            for target in (2, 3):
                rows_span = ((target - 1) * depth, target * depth)
                add(source, orders[i], target, rows_span, (0, wide), spans[i], (0, depth), plane)
            add(source, orders[i], 4, (0, rows), (wide, 2 * middle), spans[i], (0, rows), plane)
    for i in range(2, 5):
        for target in (5, 6):
            cols_span = ((target - 5) * hidden, (target - 4) * hidden)
            add(i + 2, orders[i], target, (0, rows), cols_span, spans[i], (0, rows), None)
    qkv, out, up, down, adapter, expand, shrink = route(moves, place, arrays, shapes)
    adapter = adapter.reshape(2 * CHIPS, 2, fine, adapter_half).transpose(0, 2, 1, 3)
    return (
        qkv.reshape(2 * CHIPS * depth, split),
        out.reshape(2 * CHIPS * depth, wide - split),
        up.reshape(2 * CHIPS * depth, wide),
        down.reshape(2 * CHIPS * depth, wide),
        adapter.reshape(2 * CHIPS * fine, 2 * adapter_half),
        expand.reshape(CHIPS * rows, hidden),
        shrink.reshape(CHIPS * rows, hidden),
    )


def reduced_map_slopes(place, core, expand_slope, shrink_slope):
    hidden = expand_slope.shape[1]
    rows = expand_slope.shape[0] // CHIPS
    arrays = [expand_slope.reshape(CHIPS, rows, hidden), shrink_slope.reshape(CHIPS, rows, hidden)]
    tiles = 2 * hidden // LANES
    edges = [LANES * ((tiles * i + 4) // 5) for i in range(6)]
    spans = [(edges[i], edges[i + 1]) for i in range(5)]
    orders = [rotated(i) for i in range(5)]
    moves = []
    for i, span in enumerate(spans):
        for source in range(2):
            cols_span = (source * hidden, (source + 1) * hidden)
            shared = overlap(cols_span, span)
            if shared is None:
                continue
            moves.append(
                (
                    source,
                    lambda chip, core, offset: chip ^ offset,
                    i,
                    lambda chip, core, offset, order=orders[i]: scatter_place(offset, order),
                    box((0, rows), shifted_span(shared, cols_span[0])),
                    box((0, rows), shifted_span(shared, span[0])),
                )
            )
    packed = route(moves, place, arrays, [(CHIPS, rows, high - low) for low, high in spans])
    block = jnp.concatenate(
        [scattered_part(packed[i], orders[i]) for i in range(5)], axis=1
    )
    kept = own_half(block, core, 0)
    given = own_half(block, core, 0, True)
    got = core_swap(given.astype(jnp.bfloat16)).astype(jnp.float32)
    return tuple(
        in_core_order(
            kept[:, i * hidden : (i + 1) * hidden], got[:, i * hidden : (i + 1) * hidden], core, 1
        )
        for i in range(2)
    )


def reduced_other_slopes(place, core, qkv, out, up, down, adapter, minor):
    fine = adapter.shape[0] // (2 * CHIPS)
    depth = qkv.shape[0] // (2 * CHIPS)
    split, wide = qkv.shape[1], up.shape[1]
    adapter_half = adapter.shape[1] // 2
    rows = 3 * depth
    adapter = (
        adapter.reshape(2 * CHIPS, fine, 2, adapter_half)
        .transpose(0, 2, 1, 3)
        .reshape(2 * CHIPS, rows, adapter_half)
    )
    arrays = [
        qkv.reshape(2 * CHIPS, depth, split),
        out.reshape(2 * CHIPS, depth, wide - split),
        up.reshape(2 * CHIPS, depth, wide),
        down.reshape(2 * CHIPS, depth, wide),
        adapter,
        minor,
    ]
    quarter = wide // 4
    orders = [rotated(i) for i in range(5)]
    moves = []

    def add(source, source_cols, target, rows_span, target_cols):
        order = orders[target]
        size = rows_span[1] - rows_span[0]

        def put(chip, core, offset, plane):
            return CHIPS * plane + scatter_place(offset, order)

        for plane in range(2):
            moves.append(
                (
                    source,
                    lambda chip, core, offset, plane=plane: 2 * (chip ^ offset) + (core ^ plane),
                    target,
                    functools.partial(put, plane=plane),
                    box((0, size), source_cols),
                    box(rows_span, target_cols),
                )
            )

    for i in range(4):
        cols = (i * quarter, (i + 1) * quarter)
        first = 0 if cols[1] <= split else 1
        add(first, shifted_span(cols, first * split), i, (0, depth), (0, quarter))
        add(2, cols, i, (depth, 2 * depth), (0, quarter))
        add(3, cols, i, (2 * depth, rows), (0, quarter))
    minor_width = minor.shape[2]
    add(4, (0, adapter_half), 4, (0, rows), (0, adapter_half))
    add(5, (0, minor_width), 4, (0, rows), (adapter_half, adapter_half + minor_width))
    shapes = [(2 * CHIPS, rows, quarter)] * 4 + [(2 * CHIPS, rows, adapter_half + minor_width)]
    packed = route(moves, place, arrays, shapes)
    blocks = [scattered_part(packed[i], (CORE,) + orders[i]) for i in range(5)]
    whole = jnp.concatenate(blocks[:4], axis=1)
    last = blocks[4]
    adapter_own = jnp.concatenate(
        [last[:fine, :adapter_half], last[fine:, :adapter_half]], axis=1
    )
    return (
        [blocks[i][:depth] for i in range(4)],
        whole[depth : 2 * depth],
        whole[2 * depth :],
        adapter_own,
        last[:, adapter_half:],
    )


def gathered_rows(row, device):
    held = row[None]
    count = lax.axis_size("dp")
    step = 1
    while step < count:
        other = xor_swap(held, step)
        held = jnp.where(
            (device & step) != 0,
            jnp.concatenate([other, held], axis=0),
            jnp.concatenate([held, other], axis=0),
        )
        step *= 2
    return held


def on_device(
    lowres_in,
    highres_in,
    image_sizes,
    attn_gain,
    query_weight,
    key_weight,
    value_weight,
    output_weight,
    mlp_gain,
    up_weight,
    down_weight,
    depth_kernel,
    conv_gain,
    expand_weight,
    shrink_weight,
    layer_scale,
    adapter_weight,
    adapter_kernel,
    gate_vector,
    out_cotangent,
    map_cotangent,
):
    device = lax.axis_index("dp")
    core = device & 1
    place = device.reshape(1).astype(jnp.int32)
    group_count = lax.axis_size("dp") // TILES
    position = (device + 2) % TILES
    group_id = (device + 2) // TILES % group_count
    model_half = lax.axis_index("mp")
    low_strip, _, grid_side, width = lowres_in.shape
    high_strip, _, high_side, channels = highres_in.shape
    own_width = adapter_kernel.shape[1]
    local_width = query_weight.shape[1]
    local_heads = local_width // HD
    scaling = HD ** (-0.5)
    token_count = low_strip * grid_side
    pixel_count = high_strip * high_side

    high_map = highres_in.reshape(high_strip, high_side, channels)
    map_low, map_high = halo_rows(high_map, RADIUS)

    qkv_full, output_full, up_full, down_full, adapter_full, expand_full, shrink_full = all_weights(
        place,
        core,
        (query_weight, key_weight, value_weight, output_weight.T, up_weight, down_weight.T),
        adapter_weight,
        expand_weight,
        shrink_weight.T,
    )

    table_ids = jnp.arange(image_sizes.shape[0])
    extent = jnp.sum(jnp.where(table_ids == group_id, image_sizes, 0))
    first_row = position * high_strip
    map_place = jnp.stack([first_row, extent]).astype(jnp.int32)
    row_ids = first_row + jnp.arange(high_strip)
    col_ids = jnp.arange(high_side)
    valid_mask = (
        ((row_ids < extent)[:, None] & (col_ids < extent)[None, :])
        .astype(jnp.float32)[..., None]
    )

    convolved = map_conv(map_place, high_map, map_low, map_high, depth_kernel).reshape(
        pixel_count, channels
    )
    normed_map, conv_norm_back = jax.vjp(normalize, convolved, conv_gain.astype(jnp.float32))
    normed_map_low = normed_map.astype(jnp.bfloat16)
    normed_map_pair = jnp.concatenate([normed_map_low, core_swap(normed_map_low)], axis=0)

    token_rows = lowres_in.astype(jnp.float32).reshape(token_count, width)
    normed, attn_norm_back = jax.vjp(normalize, token_rows, attn_gain.astype(jnp.float32))
    normed_low = normed.astype(jnp.bfloat16)
    qkv_rows = matmul(normed_low, qkv_full).astype(jnp.bfloat16)
    queries = qkv_rows[:, :local_width]
    pair = qkv_rows[:, local_width:]
    pair = jnp.concatenate([pair, core_swap(pair)], axis=0)
    pair = jnp.concatenate([pair, pair_swap(pair)], axis=0)
    key_all = pair[:, :local_width].reshape(-1, local_heads, HD)
    value_all = pair[:, local_width:].reshape(-1, local_heads, HD)
    query_heads = queries.reshape(token_count, local_heads, HD)
    scores = (
        jnp.einsum("qhd,khd->hqk", query_heads, key_all, preferred_element_type=jnp.float32)
        * scaling
    )
    top_score = jnp.max(scores, axis=-1, keepdims=True)
    log_total = top_score + jnp.log(jnp.sum(jnp.exp(scores - top_score), axis=-1, keepdims=True))
    attention_low = jnp.exp(scores - log_total).astype(jnp.bfloat16)
    attended = jnp.einsum(
        "hqk,khd->qhd", attention_low, value_all, preferred_element_type=jnp.float32
    )
    attended_low = attended.reshape(token_count, local_width).astype(jnp.bfloat16)
    hidden_rows = token_rows + exchange(matmul_nt(attended_low, output_full))
    normed_two, mlp_norm_back = jax.vjp(normalize, hidden_rows, mlp_gain.astype(jnp.float32))
    normed_two_low = normed_two.astype(jnp.bfloat16)
    expanded = matmul(normed_two_low, up_full)
    activated, up_gelu_back = jax.vjp(gelu_exact, expanded)
    activated_low = activated.astype(jnp.bfloat16)
    result_rows = hidden_rows + exchange(matmul_nt(activated_low, down_full))

    widened = matmul(normed_map_pair, expand_full)
    widened_act, wide_gelu_back = jax.vjp(gelu_exact, widened)
    widened_low = widened_act.astype(jnp.bfloat16)
    narrowed_part = matmul_nt(widened_low, shrink_full)
    narrowed_part = narrowed_part[:pixel_count] + core_swap(
        narrowed_part[pixel_count:].astype(jnp.bfloat16)
    ).astype(jnp.float32)
    narrowed = exchange(narrowed_part).reshape(high_strip, high_side, channels)
    scale_wide = layer_scale.astype(jnp.float32)
    masked_map = high_map.astype(jnp.float32) * valid_mask
    mapped = valid_mask * (masked_map + scale_wide * narrowed)
    pooled = (
        jnp.sum(mapped.reshape(low_strip, 2, grid_side, 2, channels), axis=(1, 3)) * 0.25
    )
    pooled_low = pooled.reshape(token_count, channels).astype(jnp.bfloat16)
    lifted = matmul(pooled_low, adapter_full).reshape(low_strip, grid_side, own_width)

    result_grid = result_rows.reshape(low_strip, grid_side, width)
    own_result = lax.dynamic_slice_in_dim(result_grid, model_half * own_width, own_width, 2)
    own_padded = with_edges(own_result.astype(jnp.bfloat16), position)
    adapter_wide = adapter_kernel.astype(jnp.float32)
    local_mix = depth_apply(own_padded, adapter_wide, 1)
    gate_wide = gate_vector.astype(jnp.float32)
    gating = jax.nn.sigmoid(jnp.sum(result_grid * gate_wide, axis=-1, keepdims=True))
    blended = own_result + local_mix + gating * lifted

    local_grad_low = out_cotangent.reshape(low_strip, grid_side, own_width)
    out_grad = local_grad_low.astype(jnp.float32)
    lifted_grad_low = (out_grad * gating).reshape(token_count, own_width).astype(jnp.bfloat16)
    gate_part = jnp.sum(out_grad * lifted, axis=-1, keepdims=True)
    pooled_part = matmul_nt(lifted_grad_low, adapter_full)
    pooled_grad = exchange(pooled_part)
    gate_grad = exchange(gate_part)
    adapter_weight_slope = matmul_tn(pooled_low, lifted_grad_low).astype(jnp.bfloat16)
    local_padded = with_edges(local_grad_low, position)
    own_grad = out_grad + depth_apply(local_padded, adapter_wide[::-1], 1)
    adapter_kernel_slope = kernel_slopes(own_padded, out_grad, 1)
    own_grad_low = own_grad.astype(jnp.bfloat16)
    other_grad = lax.ppermute(own_grad_low, "mp", [(0, 1), (1, 0)])
    result_grad = in_core_order(own_grad_low, other_grad, model_half, 2).astype(jnp.float32)
    gate_slope = gate_grad * gating * (1.0 - gating)
    gate_vector_slope = jnp.sum((gate_slope * result_grid).reshape(token_count, width), axis=0)
    result_grad = (result_grad + gate_slope * gate_wide).reshape(token_count, width)

    pooled_spread = jnp.broadcast_to(
        (pooled_grad * 0.25).reshape(low_strip, 1, grid_side, 1, channels),
        (low_strip, 2, grid_side, 2, channels),
    ).reshape(high_strip, high_side, channels)
    map_grad = (
        map_cotangent.reshape(high_strip, high_side, channels).astype(jnp.float32) + pooled_spread
    ) * valid_mask
    narrowed_grad_low = (map_grad * scale_wide).reshape(pixel_count, channels).astype(jnp.bfloat16)
    layer_scale_slope = jnp.sum((map_grad * narrowed).reshape(pixel_count, channels), axis=0)
    narrowed_grad_pair = jnp.concatenate([narrowed_grad_low, core_swap(narrowed_grad_low)], axis=0)
    widened_grad = matmul(narrowed_grad_pair, shrink_full)
    widened_grad_low = wide_gelu_back(widened_grad)[0].astype(jnp.bfloat16)
    normed_map_part = matmul_nt(widened_grad_low, expand_full)
    normed_map_part = normed_map_part[:pixel_count] + core_swap(
        normed_map_part[pixel_count:].astype(jnp.bfloat16)
    ).astype(jnp.float32)
    normed_map_grad = exchange(normed_map_part)
    shrink_weight_slope = matmul_tn(narrowed_grad_pair, widened_low).astype(jnp.bfloat16)
    expand_weight_slope = matmul_tn(normed_map_pair, widened_grad_low).astype(jnp.bfloat16)
    expand_own, shrink_own = reduced_map_slopes(
        place, core, expand_weight_slope, shrink_weight_slope
    )

    result_low = result_grad.astype(jnp.bfloat16)
    activated_grad = matmul(result_low, down_full)
    down_weight_slope = matmul_tn(result_low, activated_low).astype(jnp.bfloat16)
    expanded_grad_low = up_gelu_back(activated_grad)[0].astype(jnp.bfloat16)
    up_weight_slope = matmul_tn(normed_two_low, expanded_grad_low).astype(jnp.bfloat16)
    normed_two_grad = exchange(matmul_nt(expanded_grad_low, up_full))
    hidden_part, mlp_gain_slope = mlp_norm_back(normed_two_grad)
    hidden_grad = result_grad + hidden_part
    hidden_low = hidden_grad.astype(jnp.bfloat16)
    attended_grad_low = matmul(hidden_low, output_full).astype(jnp.bfloat16)
    output_weight_slope = matmul_tn(hidden_low, attended_low).astype(jnp.bfloat16)
    attended_heads_grad = attended_grad_low.reshape(token_count, local_heads, HD)
    scores_again = (
        jnp.einsum("qhd,khd->hqk", query_heads, key_all, preferred_element_type=jnp.float32)
        * scaling
    )
    attention_again = jnp.exp(scores_again - log_total)
    attention_again_low = attention_again.astype(jnp.bfloat16)
    attention_grad = jnp.einsum(
        "qhd,khd->hqk", attended_heads_grad, value_all, preferred_element_type=jnp.float32
    )
    row_dot = jnp.sum(attention_again * attention_grad, axis=-1, keepdims=True)
    score_grad_low = (attention_again * (attention_grad - row_dot)).astype(jnp.bfloat16)
    query_grad_rows = (
        jnp.einsum("hqk,khd->qhd", score_grad_low, key_all, preferred_element_type=jnp.float32)
        * scaling
    ).astype(jnp.bfloat16).reshape(token_count, local_width)
    key_grad_all = (
        jnp.einsum("hqk,qhd->khd", score_grad_low, query_heads, preferred_element_type=jnp.float32)
        * scaling
    )
    value_grad_all = jnp.einsum(
        "hqk,qhd->khd", attention_again_low, attended_heads_grad, preferred_element_type=jnp.float32
    )
    pair_back = jnp.concatenate(
        [key_grad_all.reshape(-1, local_width), value_grad_all.reshape(-1, local_width)], axis=1
    )
    pair_back = pair_back[: 2 * token_count] + pair_swap(
        pair_back[2 * token_count :].astype(jnp.bfloat16)
    ).astype(jnp.float32)
    pair_back = pair_back[:token_count] + core_swap(
        pair_back[token_count:].astype(jnp.bfloat16)
    ).astype(jnp.float32)
    qkv_grad = jnp.concatenate([query_grad_rows, pair_back.astype(jnp.bfloat16)], axis=1)
    normed_grad = exchange(matmul_nt(qkv_grad, qkv_full))
    qkv_slope = matmul_tn(normed_low, qkv_grad).astype(jnp.bfloat16)
    input_part, attn_gain_slope = attn_norm_back(normed_grad)
    lowres_grad = (hidden_grad + input_part).reshape(low_strip, 1, grid_side, width)

    convolved_grad, conv_gain_slope = conv_norm_back(normed_map_grad)
    convolved_grad_low = convolved_grad.reshape(high_strip, high_side, channels).astype(
        jnp.bfloat16
    )
    grad_low, grad_high = halo_rows(convolved_grad_low, RADIUS)
    depth_kernel_slope = map_slopes(map_place, high_map, map_low, map_high, convolved_grad_low)
    highres_grad = map_conv(
        map_place, convolved_grad_low, grad_low, grad_high, depth_kernel, map_grad
    )

    def as_rows(values):
        return jnp.pad(values, ((0, 0), (0, channels - values.shape[1])))

    minor_rows = jnp.concatenate(
        [
            depth_kernel_slope,
            conv_gain_slope[None],
            layer_scale_slope[None],
            as_rows(jnp.stack([attn_gain_slope, mlp_gain_slope, gate_vector_slope], 0)),
            as_rows(adapter_kernel_slope),
        ],
        axis=0,
    )
    minor_used = minor_rows.shape[0]
    lines = channels // LANES
    minor = jnp.pad(
        minor_rows.astype(jnp.bfloat16).reshape(minor_used, lines, LANES),
        ((0, 2 * CHIPS - minor_used), (0, 3 * query_weight.shape[0] - lines), (0, 0)),
    )
    firsts, up_own, down_own, adapter_own, minor_own = reduced_other_slopes(
        place,
        core,
        qkv_slope,
        output_weight_slope,
        up_weight_slope,
        down_weight_slope,
        adapter_weight_slope,
        minor,
    )
    minor_all = gathered_rows(minor_own[:lines], device).reshape(2 * CHIPS, channels)
    taps = depth_kernel.shape[0]
    side_taps = adapter_kernel.shape[0]
    return (
        blended.astype(jnp.bfloat16)[:, None],
        mapped.astype(jnp.bfloat16)[:, None],
        lowres_grad,
        highres_grad[:, None],
        minor_all[taps + 2, :width],
        firsts[0],
        firsts[1],
        firsts[2],
        firsts[3].T,
        minor_all[taps + 3, :width],
        up_own,
        down_own.T,
        minor_all[:taps],
        minor_all[taps],
        expand_own,
        shrink_own.T,
        minor_all[taps + 1],
        adapter_own,
        minor_all[taps + 5 : taps + 5 + side_taps, :own_width],
        minor_all[taps + 4, :width],
    )


def solution(mesh):
    in_specs = (
        P("dp", None, None, None),
        P("dp", None, None, None),
        P(),
        P(),
        P("dp", "mp"),
        P("dp", "mp"),
        P("dp", "mp"),
        P("mp", "dp"),
        P(),
        P("dp", "mp"),
        P("mp", "dp"),
        P(),
        P(),
        P("dp", "mp"),
        P("mp", "dp"),
        P(),
        P("dp", "mp"),
        P(None, "mp"),
        P(),
        P("dp", None, None, "mp"),
        P("dp", None, None, None),
    )
    out_specs = (
        P("dp", None, None, "mp"),
        P("dp", None, None, None),
        P("dp", None, None, None),
        P("dp", None, None, None),
        P(),
        P("dp", "mp"),
        P("dp", "mp"),
        P("dp", "mp"),
        P("mp", "dp"),
        P(),
        P("dp", "mp"),
        P("mp", "dp"),
        P(),
        P(),
        P("dp", "mp"),
        P("mp", "dp"),
        P(),
        P("dp", "mp"),
        P(None, "mp"),
        P(),
    )
    return jax.shard_map(
        on_device, mesh=mesh, in_specs=in_specs, out_specs=out_specs, check_vma=False
    )
```

```python
import functools

import jax
import jax.numpy as jnp
from jax import lax
from jax.experimental import pallas as pl
from jax.experimental.pallas import tpu as pltpu
from jax.sharding import PartitionSpec as P

HD = 64
TILES = 4
CHIPS = 32
CORE = 1
RINGS = (2, 6, 8, 24, 32)

norm_epsilon = 1e-06

LANES = 128
RADIUS = 3
WINDOW = 7
PAD = 8


def masked_rows(place, main_ref, low_ref, high_ref, wide, strip, side, bounded):
    first, extent = place[0], place[1]
    cols = lax.broadcasted_iota(jnp.int32, (side, LANES), 0)

    def put(slot, value):
        row = first + slot - RADIUS
        limit = extent if bounded else side
        keep = (cols < limit) & (row >= 0) & (row < limit)
        wide[slot] = jnp.where(keep, value.astype(jnp.float32), 0.0)

    for slot in range(RADIUS):
        put(slot, low_ref[slot])
        put(RADIUS + strip + slot, high_ref[slot])
    for slot in range(strip):
        put(RADIUS + slot, main_ref[slot])


def window_sum(wide, taps_ref, shifted, row, side, flipped):
    sums = [None] * WINDOW
    for a in range(WINDOW):
        line = wide[row + a]
        for b in range(WINDOW):
            tap = WINDOW * a + b
            if flipped:
                tap = WINDOW * WINDOW - 1 - tap
            term = line * taps_ref[tap : tap + 1]
            sums[b] = term if sums[b] is None else sums[b] + term
    total = sums[RADIUS]
    for b in range(WINDOW):
        if b != RADIUS:
            shifted[b, PAD : PAD + side] = sums[b]
    for b in range(WINDOW):
        if b != RADIUS:
            total = total + shifted[b, PAD + b - RADIUS : PAD + b - RADIUS + side]
    return total


def clear_edges(shifted, side):
    for b in range(WINDOW):
        shifted[b, 0:PAD] = jnp.zeros((PAD, LANES), jnp.float32)
        shifted[b, PAD + side : 2 * PAD + side] = jnp.zeros((PAD, LANES), jnp.float32)


def forward_kernel(place, main_ref, low_ref, high_ref, taps_in, out_ref, wide, taps, shifted):
    strip, side = main_ref.shape[0], main_ref.shape[1]
    masked_rows(place, main_ref, low_ref, high_ref, wide, strip, side, True)
    clear_edges(shifted, side)
    taps[...] = taps_in[...].astype(jnp.float32)

    def step(row, carry):
        out_ref[row] = window_sum(wide, taps, shifted, row, side, False)
        return carry

    lax.fori_loop(0, strip, step, 0)


def backward_kernel(place, main_ref, low_ref, high_ref, taps_in, add_ref, out_ref, wide, taps, shifted):
    strip, side = main_ref.shape[0], main_ref.shape[1]
    masked_rows(place, main_ref, low_ref, high_ref, wide, strip, side, False)
    clear_edges(shifted, side)
    taps[...] = taps_in[...].astype(jnp.float32)
    cols = lax.broadcasted_iota(jnp.int32, (side, LANES), 0)

    def step(row, carry):
        total = window_sum(wide, taps, shifted, row, side, True) + add_ref[row]
        keep = (cols < place[1]) & (place[0] + row < place[1])
        out_ref[row] = jnp.where(keep, total, 0.0)
        return carry

    lax.fori_loop(0, strip, step, 0)


def slope_kernel(place, main_ref, low_ref, high_ref, grad_ref, out_ref, wide, padded):
    strip, side = main_ref.shape[0], main_ref.shape[1]
    masked_rows(place, main_ref, low_ref, high_ref, wide, strip, side, True)
    edge = jnp.zeros((PAD, LANES), jnp.float32)
    for row in range(strip):
        padded[row, 0:PAD] = edge
        padded[row, PAD : PAD + side] = grad_ref[row].astype(jnp.float32)
        padded[row, PAD + side : 2 * PAD + side] = edge
    for group in ((0, 1, 2, 3), (4, 5, 6)):

        def step(row, sums):
            lines = [wide[row + a] for a in group]
            fresh = list(sums)
            for b in range(WINDOW):
                start = PAD + RADIUS - b
                part = padded[row, start : start + side]
                for i in range(len(group)):
                    term = (lines[i] * part).reshape(side // 8, 8, LANES)
                    fresh[i * WINDOW + b] = fresh[i * WINDOW + b] + jnp.sum(term, axis=0)
            return tuple(fresh)

        start = tuple(jnp.zeros((8, LANES), jnp.float32) for _ in range(len(group) * WINDOW))
        sums = lax.fori_loop(0, strip, step, start)
        for i, a in enumerate(group):
            for b in range(WINDOW):
                tap = a * WINDOW + b
                out_ref[tap : tap + 1] = jnp.sum(sums[i * WINDOW + b], axis=0, keepdims=True)


def block3(rows, side):
    return pl.BlockSpec((rows, side, LANES), lambda i: (0, 0, i))


SCALARS = pl.BlockSpec(memory_space=pltpu.SMEM)


def map_conv(place, main, low, high, taps, added=None):
    strip, side, channels = main.shape
    count = taps.shape[0]
    tap_spec = pl.BlockSpec((count, LANES), lambda i: (0, i))
    specs = [SCALARS, block3(strip, side), block3(RADIUS, side), block3(RADIUS, side), tap_spec]
    args = [place, main, low, high, taps]
    if added is not None:
        specs.append(block3(strip, side))
        args.append(added)
    work = strip * side * channels
    return pl.pallas_call(
        forward_kernel if added is None else backward_kernel,
        grid=(channels // LANES,),
        in_specs=specs,
        out_specs=block3(strip, side),
        out_shape=jax.ShapeDtypeStruct((strip, side, channels), jnp.float32),
        scratch_shapes=[
            pltpu.VMEM((strip + 2 * RADIUS, side, LANES), jnp.float32),
            pltpu.VMEM((count, LANES), jnp.float32),
            pltpu.VMEM((WINDOW, side + 2 * PAD, LANES), jnp.float32),
        ],
        compiler_params=pltpu.CompilerParams(vmem_limit_bytes=24 * 1024 * 1024),
        cost_estimate=pl.CostEstimate(flops=0, bytes_accessed=work // 8, transcendentals=0),
    )(*args)


def map_slopes(place, main, low, high, grad):
    strip, side, channels = main.shape
    count = WINDOW * WINDOW
    work = strip * side * channels
    return pl.pallas_call(
        slope_kernel,
        grid=(channels // LANES,),
        in_specs=[SCALARS, block3(strip, side), block3(RADIUS, side), block3(RADIUS, side), block3(strip, side)],
        out_specs=pl.BlockSpec((count, LANES), lambda i: (0, i)),
        out_shape=jax.ShapeDtypeStruct((count, channels), jnp.float32),
        scratch_shapes=[
            pltpu.VMEM((strip + 2 * RADIUS, side, LANES), jnp.float32),
            pltpu.VMEM((strip, side + 2 * PAD, LANES), jnp.float32),
        ],
        compiler_params=pltpu.CompilerParams(vmem_limit_bytes=24 * 1024 * 1024),
        cost_estimate=pl.CostEstimate(flops=0, bytes_accessed=work // 8, transcendentals=0),
    )(place, main, low, high, grad)


WIDE = 384


def inside(place, row, side):
    cols = lax.broadcasted_iota(jnp.int32, (side, LANES), 0)
    return (cols < place[1]) & (place[0] + row < place[1])


def blend_kernel(
    place, own_ref, other_ref, map_ref, scale_ref, grad_ref, out_ref, pool_ref, slope_ref, line
):
    strip, side = map_ref.shape[0], map_ref.shape[1]
    half = side // 2
    for part in range(map_ref.shape[2] // LANES):
        lanes = slice(part * LANES, (part + 1) * LANES)
        scale = scale_ref[:, lanes].astype(jnp.float32)

        def step(pair, slope):
            total = None
            for i in range(2):
                row = 2 * pair + i
                narrow = own_ref[row, :, lanes].astype(jnp.float32) + other_ref[
                    row, :, lanes
                ].astype(jnp.float32)
                value = map_ref[row, :, lanes].astype(jnp.float32) + scale * narrow
                value = jnp.where(inside(place, row, side), value, 0.0)
                out_ref[row, :, lanes] = value.astype(out_ref.dtype)
                total = value if total is None else total + value
                product = grad_ref[row, :, lanes] * narrow
                slope = slope + jnp.sum(product.reshape(side // 8, 8, LANES), axis=0)
            line[...] = total
            pooled = line[pl.ds(0, half, 2), :] + line[pl.ds(1, half, 2), :]
            pool_ref[pair, :, lanes] = (pooled * 0.25).astype(pool_ref.dtype)
            return slope

        slope = lax.fori_loop(0, strip // 2, step, jnp.zeros((8, LANES), jnp.float32))
        slope_ref[:, lanes] = jnp.sum(slope, axis=0, keepdims=True)


def spread_kernel(place, pool_ref, pool_other_ref, cot_ref, scale_ref, grad_ref, low_ref, line):
    strip, side = cot_ref.shape[0], cot_ref.shape[1]
    half = side // 2
    for part in range(cot_ref.shape[2] // LANES):
        lanes = slice(part * LANES, (part + 1) * LANES)
        scale = scale_ref[:, lanes].astype(jnp.float32)

        def step(pair, carry):
            pooled = pool_ref[pair, :, lanes].astype(jnp.float32) + pool_other_ref[
                pair, :, lanes
            ].astype(jnp.float32)
            pooled = pooled * 0.25
            line[pl.ds(0, half, 2), :] = pooled
            line[pl.ds(1, half, 2), :] = pooled
            spread = line[...]
            for i in range(2):
                row = 2 * pair + i
                value = cot_ref[row, :, lanes].astype(jnp.float32) + spread
                value = jnp.where(inside(place, row, side), value, 0.0)
                grad_ref[row, :, lanes] = value
                low_ref[row, :, lanes] = (value * scale).astype(low_ref.dtype)
            return carry

        lax.fori_loop(0, strip // 2, step, 0)


def wide_block(*lead):
    return pl.BlockSpec(lead + (WIDE,), lambda i: (0,) * len(lead) + (i,))


def blend_map(place, own, other, main, scale, grad):
    strip, side, channels = main.shape
    full = wide_block(strip, side)
    pool = (strip // 2, side // 2)
    return pl.pallas_call(
        blend_kernel,
        grid=(channels // WIDE,),
        in_specs=[SCALARS, full, full, full, wide_block(1), full],
        out_specs=[full, wide_block(*pool), wide_block(1)],
        out_shape=[
            jax.ShapeDtypeStruct(main.shape, jnp.bfloat16),
            jax.ShapeDtypeStruct(pool + (channels,), jnp.bfloat16),
            jax.ShapeDtypeStruct((1, channels), jnp.float32),
        ],
        scratch_shapes=[pltpu.VMEM((side, LANES), jnp.float32)],
        compiler_params=pltpu.CompilerParams(vmem_limit_bytes=24 * 1024 * 1024),
        cost_estimate=pl.CostEstimate(flops=0, bytes_accessed=1 << 20, transcendentals=0),
    )(place, own, other, main, scale, grad)


def spread_map(place, pool, pool_other, cot, scale):
    strip, side, channels = cot.shape
    full = wide_block(strip, side)
    pooled = wide_block(strip // 2, side // 2)
    return pl.pallas_call(
        spread_kernel,
        grid=(channels // WIDE,),
        in_specs=[SCALARS, pooled, pooled, full, wide_block(1)],
        out_specs=[full, full],
        out_shape=[
            jax.ShapeDtypeStruct(cot.shape, jnp.float32),
            jax.ShapeDtypeStruct(cot.shape, jnp.bfloat16),
        ],
        scratch_shapes=[pltpu.VMEM((side, LANES), jnp.float32)],
        compiler_params=pltpu.CompilerParams(vmem_limit_bytes=24 * 1024 * 1024),
        cost_estimate=pl.CostEstimate(flops=0, bytes_accessed=1 << 20, transcendentals=0),
    )(place, pool, pool_other, cot, scale)


def head_lanes(rows, head):
    lanes = lax.broadcasted_iota(jnp.int32, (rows, LANES), 1)
    return (lanes >= head * HD) & (lanes < (head + 1) * HD)


def nt(former, latter):
    return lax.dot_general(
        former, latter, (((1,), (1,)), ((), ())), preferred_element_type=jnp.float32
    )


def tn(former, latter):
    return lax.dot_general(
        former, latter, (((0,), (0,)), ((), ())), preferred_element_type=jnp.float32
    )


def softmax_rows(scores):
    top = jnp.max(scores, axis=-1, keepdims=True)
    raised = jnp.exp(scores - top)
    return raised * (1.0 / jnp.sum(raised, axis=-1, keepdims=True))


def attend_kernel(query_ref, key_ref, value_ref, out_ref):
    rows = query_ref.shape[0]
    query, key, value = query_ref[...], key_ref[...], value_ref[...]
    total = jnp.zeros((rows, LANES), jnp.float32)
    for head in range(LANES // HD):
        mine = head_lanes(rows, head)
        scores = nt(jnp.where(mine, query, jnp.zeros_like(query)), key) * HD ** (-0.5)
        weights = softmax_rows(scores).astype(jnp.bfloat16)
        part = jnp.dot(weights, value, preferred_element_type=jnp.float32)
        total = jnp.where(mine, part, total)
    out_ref[...] = total.astype(out_ref.dtype)


def attend_back_kernel(
    query_ref, key_ref, value_ref, grad_ref, query_out, key_out, value_out
):
    rows = query_ref.shape[0]
    query, key, value, grad = query_ref[...], key_ref[...], value_ref[...], grad_ref[...]
    none = jnp.zeros_like(query)
    query_grad = jnp.zeros((rows, LANES), jnp.float32)
    key_grad, value_grad = None, None
    for head in range(LANES // HD):
        mine = head_lanes(rows, head)
        query_own = jnp.where(mine, query, none)
        grad_own = jnp.where(mine, grad, none)
        weights = softmax_rows(nt(query_own, key) * HD ** (-0.5))
        weight_grad = nt(grad_own, value)
        row_dot = jnp.sum(weights * weight_grad, axis=-1, keepdims=True)
        score_grad = (weights * (weight_grad - row_dot)).astype(jnp.bfloat16)
        part = jnp.dot(score_grad, key, preferred_element_type=jnp.float32)
        query_grad = jnp.where(mine, part, query_grad)
        key_part = tn(score_grad, query_own)
        value_part = tn(weights.astype(jnp.bfloat16), grad_own)
        key_grad = key_part if key_grad is None else key_grad + key_part
        value_grad = value_part if value_grad is None else value_grad + value_part
    query_out[...] = (query_grad * HD ** (-0.5)).astype(query_out.dtype)
    key_out[...] = key_grad * HD ** (-0.5)
    value_out[...] = value_grad


def lane_block(rows, shift=0):
    return pl.BlockSpec((rows, LANES), lambda i: (0, i + shift))


def attend(rows, pair):
    count, keys = rows.shape[0], pair.shape[0]
    width = pair.shape[1] // 2
    steps = width // LANES
    work = 4 * count * keys * width
    return pl.pallas_call(
        attend_kernel,
        grid=(steps,),
        in_specs=[lane_block(count), lane_block(keys), lane_block(keys, steps)],
        out_specs=lane_block(count),
        out_shape=jax.ShapeDtypeStruct((count, width), jnp.bfloat16),
        compiler_params=pltpu.CompilerParams(vmem_limit_bytes=24 * 1024 * 1024),
        cost_estimate=pl.CostEstimate(flops=0, bytes_accessed=1 << 20, transcendentals=0),
    )(rows, pair, pair)


def attend_back(rows, pair, grad):
    count, keys = rows.shape[0], pair.shape[0]
    width = pair.shape[1] // 2
    steps = width // LANES
    work = 10 * count * keys * width
    return pl.pallas_call(
        attend_back_kernel,
        grid=(steps,),
        in_specs=[
            lane_block(count),
            lane_block(keys),
            lane_block(keys, steps),
            lane_block(count),
        ],
        out_specs=[lane_block(count), lane_block(keys), lane_block(keys)],
        out_shape=[
            jax.ShapeDtypeStruct((count, width), jnp.bfloat16),
            jax.ShapeDtypeStruct((keys, width), jnp.float32),
            jax.ShapeDtypeStruct((keys, width), jnp.float32),
        ],
        compiler_params=pltpu.CompilerParams(vmem_limit_bytes=24 * 1024 * 1024),
        cost_estimate=pl.CostEstimate(flops=0, bytes_accessed=1 << 20, transcendentals=0),
    )(rows, pair, pair, grad)


def slopes_kernel(ends, *refs):
    count = len(ends)
    lefts, rights = refs[:count], refs[count : 2 * count]
    near_ref, far_ref = refs[2 * count :]
    half = near_ref.shape[0]
    step = pl.program_id(0)
    first = 0
    for left, right, end in zip(lefts, rights, ends):

        @pl.when((step >= first) & (step < end))
        def _(left=left, right=right):
            near_ref[...] = tn(left[:, :half], right[...]).astype(near_ref.dtype)
            far_ref[...] = tn(left[:, half:], right[...]).astype(far_ref.dtype)

        first = end


def paired_slopes(lefts, rights):
    tile = 512
    rows, depth = lefts[0].shape
    half = depth // 2
    starts, ends = [], []
    total = 0
    for right in rights:
        starts.append(total)
        total += right.shape[1] // tile
        ends.append(total)

    def column(start, end):
        return lambda i: (0, jnp.clip(i - start, 0, end - start - 1))

    whole = pl.BlockSpec((rows, depth), lambda i: (0, 0))
    out = pl.BlockSpec((half, tile), lambda i: (0, i))
    shape = jax.ShapeDtypeStruct((half, total * tile), jnp.bfloat16)
    near, far = pl.pallas_call(
        functools.partial(slopes_kernel, tuple(ends)),
        grid=(total,),
        in_specs=[whole] * len(lefts)
        + [pl.BlockSpec((rows, tile), column(a, b)) for a, b in zip(starts, ends)],
        out_specs=[out, out],
        out_shape=[shape, shape],
        compiler_params=pltpu.CompilerParams(vmem_limit_bytes=24 * 1024 * 1024),
        cost_estimate=pl.CostEstimate(
            flops=0,
            bytes_accessed=1 << 20,
            transcendentals=0,
        ),
    )(*lefts, *rights)
    return near, far


def split_rows(pair):
    return [part.reshape(CHIPS, part.shape[0] // CHIPS, part.shape[1]) for part in pair]


def dense_kernel(flipped, scaled, halves, left_ref, right_ref, *refs):
    scale_ref, outs = (refs[0], refs[1:]) if scaled else (None, refs)
    rows = left_ref.shape[0]
    chunk = rows // 6
    for part in range(6):
        lines = slice(part * chunk, (part + 1) * chunk)
        product = nt if flipped else functools.partial(jnp.dot, preferred_element_type=jnp.float32)
        value = product(left_ref[lines, :], right_ref[...])
        if scaled:
            value = value * scale_ref[lines, :].astype(jnp.float32)
        if halves:
            out, first = (outs[0], 0) if part < 3 else (outs[1], rows // 2)
            out[part * chunk - first : (part + 1) * chunk - first, :] = value.astype(out.dtype)
        else:
            outs[0][lines, :] = value.astype(outs[0].dtype)


def dense(left, right, flipped, scale=None, halves=False):
    rows, depth = left.shape
    count = right.shape[0] if flipped else right.shape[1]
    tile = 512
    specs = [
        pl.BlockSpec((rows, depth), lambda i: (0, 0), pipeline_mode=pl.Buffered(1)),
        pl.BlockSpec((tile, depth), lambda i: (i, 0))
        if flipped
        else pl.BlockSpec((depth, tile), lambda i: (0, i)),
    ]
    args = [left, right]
    if scale is not None:
        specs.append(pl.BlockSpec((rows, tile), lambda i: (0, i)))
        args.append(scale)
    if halves:
        kinds = [(rows // 2, jnp.float32), (rows // 2, jnp.bfloat16)]
    else:
        kinds = [(rows, jnp.bfloat16)]
    return pl.pallas_call(
        functools.partial(dense_kernel, flipped, scale is not None, halves),
        grid=(count // tile,),
        in_specs=specs,
        out_specs=[pl.BlockSpec((size, tile), lambda i: (0, i)) for size, _ in kinds],
        out_shape=[jax.ShapeDtypeStruct((size, count), kind) for size, kind in kinds],
        compiler_params=pltpu.CompilerParams(vmem_limit_bytes=24 * 1024 * 1024),
        cost_estimate=pl.CostEstimate(flops=0, bytes_accessed=1 << 20, transcendentals=0),
    )(*args)


def mix_kernel(place, main_ref, low_ref, high_ref, taps_ref, mix_ref, back_ref, slope_ref, wide):
    strip, side, width = mix_ref.shape
    top, bottom = place[0] > 0, place[0] + strip < place[1]
    blank = jnp.zeros((PAD, LANES), jnp.float32)
    for first in range(0, width, LANES):
        for kind in range(2):
            lanes = slice(kind * width + first, kind * width + first + LANES)
            for slot in range(strip + 2):
                if slot == 0:
                    value = jnp.where(top, low_ref[0, :, lanes].astype(jnp.float32), 0.0)
                elif slot == strip + 1:
                    value = jnp.where(bottom, high_ref[0, :, lanes].astype(jnp.float32), 0.0)
                else:
                    value = main_ref[slot - 1, :, lanes].astype(jnp.float32)
                wide[kind, slot, 0:PAD] = blank
                wide[kind, slot, PAD : PAD + side] = value
                wide[kind, slot, PAD + side : 2 * PAD + side] = blank
        own = slice(first, first + LANES)
        taps = taps_ref[:, own].astype(jnp.float32)
        sums = [jnp.zeros((side, LANES), jnp.float32) for _ in range(9)]
        for row in range(strip):
            grad = wide[1, row + 1, PAD : PAD + side]
            mixed = jnp.zeros((side, LANES), jnp.float32)
            back = jnp.zeros((side, LANES), jnp.float32)
            for a in range(3):
                for b in range(3):
                    tap = 3 * a + b
                    span = slice(PAD + b - 1, PAD + b - 1 + side)
                    value = wide[0, row + a, span]
                    mixed = mixed + value * taps[tap : tap + 1]
                    back = back + wide[1, row + a, span] * taps[8 - tap : 9 - tap]
                    sums[tap] = sums[tap] + value * grad
            mix_ref[row, :, own] = mixed
            back_ref[row, :, own] = back
        for tap in range(9):
            slope_ref[tap : tap + 1, own] = jnp.sum(sums[tap], axis=0, keepdims=True)


def mix(place, both, low, high, taps):
    strip, side, double = both.shape
    width = double // 2
    grid = jax.ShapeDtypeStruct((strip, side, width), jnp.float32)
    return pl.pallas_call(
        mix_kernel,
        in_specs=[SCALARS] + [pl.BlockSpec(memory_space=pltpu.VMEM)] * 4,
        out_specs=[pl.BlockSpec(memory_space=pltpu.VMEM)] * 3,
        out_shape=[grid, grid, jax.ShapeDtypeStruct(taps.shape, jnp.float32)],
        scratch_shapes=[pltpu.VMEM((2, strip + 2, side + 2 * PAD, LANES), jnp.float32)],
        compiler_params=pltpu.CompilerParams(vmem_limit_bytes=16 * 1024 * 1024),
        cost_estimate=pl.CostEstimate(flops=0, bytes_accessed=1 << 20, transcendentals=0),
    )(place, both, low, high, taps)


def rotated(start):
    return tuple(RINGS[(start + i) % len(RINGS)] for i in range(len(RINGS)))


def xor_swap(values, mask):
    count = lax.axis_size("dp")
    return lax.ppermute(values, "dp", [(i, i ^ mask) for i in range(count)])


def chip_offset(place, order, low_first):
    offset = 0
    for k, mask in enumerate(order):
        bit = k if low_first else len(order) - 1 - k
        offset = offset ^ (((place >> bit) & 1) * (mask >> 1))
    return offset


def together(values):
    return list(lax.optimization_barrier(tuple(values)))


def after(value, *others):
    return lax.optimization_barrier((value,) + others)[0]


def gathered_parts(blocks, orders, early, work):
    held = [block[None] for block in blocks]
    count, last = len(blocks), len(RINGS) - 1
    for step in range(last):
        other = [xor_swap(part, order[step]) for part, order in zip(held, orders)]
        held = [jnp.concatenate([a, b], axis=0) for a, b in zip(held, other)]
        done = together(held + (early if step == last - 1 else []))
        held = done[:count]
    other = [xor_swap(part, order[last]) for part, order in zip(held, orders)]
    done = together(other + work(*done[count:]))
    return held, done[:count], done[count:]


def split_sum(kept, other):
    half = kept.shape[0] // 2
    if half == 0:
        return kept.astype(jnp.float32) + other.astype(jnp.float32), None
    return kept[:half] + other[:half], kept[half:] + other[half:]


class Scatter:
    def __init__(self, kept, given, orders):
        self.kept, self.given, self.orders = list(kept), list(given), orders
        self.step = 0

    def advance(self, *tied):
        other = [
            xor_swap(part, order[self.step]) for part, order in zip(self.given, self.orders)
        ]
        done = together(other + list(tied))
        sums = [split_sum(own, got) for own, got in zip(self.kept, done)]
        self.kept, self.given = [low for low, _ in sums], [high for _, high in sums]
        self.step += 1
        return done[len(other) :]

    def result(self):
        return [part[0] for part in self.kept]


def route_kernel(moves, steps, n_in, n_out, place, *refs):
    ins, outs = refs[:n_in], refs[n_in : n_in + n_out]
    held = refs[n_in + n_out : n_in + 2 * n_out]
    sems = refs[n_in + 2 * n_out]
    device = place[0]
    chip, core = device >> 1, device & 1

    for target in range(n_out):

        def step(index, carry):
            for source, take, goal, put, source_box, target_box in moves:
                if goal == target:
                    pltpu.make_async_copy(
                        ins[source].at[(take(chip, core, index),) + source_box],
                        held[goal].at[(put(chip, core, index),) + target_box],
                        sems.at[goal],
                    ).start()
            return carry

        lax.fori_loop(0, steps, step, 0)
    for target in range(n_out):
        pltpu.make_async_copy(held[target], held[target], sems.at[target]).wait()
        pltpu.make_async_copy(held[target], outs[target], sems.at[target]).start()
    for target in range(n_out):
        pltpu.make_async_copy(held[target], outs[target], sems.at[target]).wait()


def route(moves, steps, place, arrays, shapes):
    anywhere = pl.BlockSpec(memory_space=pl.ANY)
    volume = sum(2 * a.size for a in arrays)
    return pl.pallas_call(
        functools.partial(route_kernel, moves, steps, len(arrays), len(shapes)),
        in_specs=[SCALARS] + [anywhere] * len(arrays),
        out_specs=[anywhere] * len(shapes),
        out_shape=[jax.ShapeDtypeStruct(s, jnp.bfloat16) for s in shapes],
        scratch_shapes=[pltpu.VMEM(s, jnp.bfloat16) for s in shapes]
        + [pltpu.SemaphoreType.DMA((len(shapes),))],
        compiler_params=pltpu.CompilerParams(vmem_limit_bytes=volume + volume // 4 + (4 << 20)),
        cost_estimate=pl.CostEstimate(flops=0, bytes_accessed=2 * volume, transcendentals=0),
    )(place, *arrays)


def box(rows, cols):
    return (pl.ds(rows[0], rows[1] - rows[0]), pl.ds(cols[0], cols[1] - cols[0]))


def overlap(first, second):
    low, high = max(first[0], second[0]), min(first[1], second[1])
    return (low, high) if low < high else None


def shifted_span(span, base):
    return (span[0] - base, span[1] - base)


def core_swap(values):
    return xor_swap(values, CORE)


def model_swap(values):
    return lax.ppermute(values, "mp", [(0, 1), (1, 0)])


def exchange(values):
    low = values.astype(jnp.bfloat16)
    other = model_swap(low)
    return low.astype(jnp.float32) + other.astype(jnp.float32)


def halo_rows(block, width):
    count = lax.axis_size("dp")
    forward = [(i, (i + 1) % count) for i in range(count)]
    backward = [((i + 1) % count, i) for i in range(count)]
    low = lax.ppermute(block[block.shape[0] - width :], "dp", forward)
    high = lax.ppermute(block[:width], "dp", backward)
    return low, high


def normalize(values, scale_gain):
    average = jnp.mean(values, axis=-1, keepdims=True)
    centred = values - average
    spread = jnp.mean(centred * centred, axis=-1, keepdims=True)
    return centred * lax.rsqrt(spread + norm_epsilon) * scale_gain


def gelu_pair(values):
    below = 0.5 * (1.0 + lax.erf(values * 0.5**0.5))
    slope = below + values * (jnp.exp(-0.5 * values * values) * (2.0 * jnp.pi) ** -0.5)
    return (values * below).astype(jnp.bfloat16), slope.astype(jnp.bfloat16)


def matmul(former, latter):
    return jnp.dot(former, latter, preferred_element_type=jnp.float32)


def matmul_nt(former, latter):
    return lax.dot_general(
        former, latter, (((1,), (1,)), ((), ())), preferred_element_type=jnp.float32
    )


def matmul_tn(former, latter):
    return lax.dot_general(
        former, latter, (((0,), (0,)), ((), ())), preferred_element_type=jnp.float32
    )


def pair_swap(values):
    chips = lax.axis_size("dp") // 2
    pairs = []
    for chip in range(chips):
        other = (chip + 1) % chips if chip % 2 else (chip - 1) % chips
        pairs += [(2 * chip + core, 2 * other + core) for core in range(2)]
    return lax.ppermute(values, "dp", pairs)


def own_half(first, core, axis, other=False):
    size = first.shape[axis] // 2
    low = lax.slice_in_dim(first, 0, size, axis=axis)
    high = lax.slice_in_dim(first, size, 2 * size, axis=axis)
    return jnp.where((core == 0) != other, low, high)


def in_core_order(own, other, core, axis):
    return jnp.where(
        core == 0,
        jnp.concatenate([own, other], axis=axis),
        jnp.concatenate([other, own], axis=axis),
    )


def row_places(device, order, depth):
    chip, core = device >> 1, device & 1
    place = jnp.arange(2 * CHIPS * depth)
    block, line = place // depth, place % depth
    owner = 2 * (chip ^ chip_offset(block % CHIPS, order, True)) + (core ^ (block // CHIPS))
    return owner * depth + line


def row_picker(device, order, depth):
    places = row_places(device, order, depth)
    rows = lax.broadcasted_iota(jnp.int32, (places.shape[0], places.shape[0]), 0)
    return (rows == places[None, :]).astype(jnp.bfloat16)


def all_weights(place, core, small_rows, common_rows, *ties):
    middle = small_rows[4].shape[1] // 2
    first = jnp.concatenate(small_rows[:4] + (small_rows[4][:, :middle],), axis=1)
    second = jnp.concatenate([small_rows[4][:, middle:], small_rows[5]], axis=1)
    kept = jnp.concatenate([own_half(rows, core, 1) for rows in common_rows], axis=1)
    given = jnp.concatenate([own_half(rows, core, 1, True) for rows in common_rows], axis=1)
    common = in_core_order(kept, core_swap(given), core, 0)
    rows = common.shape[0]
    widths = [block.shape[1] // 2 for block in common_rows]
    spans = even_edges(common.shape[1], 3)
    orders = [rotated(i) for i in range(5)]
    held, other, extra = gathered_parts(
        [first, second] + [common[:, low:high] for low, high in spans], orders, *ties
    )
    near = [jnp.concatenate([a, b], axis=0) for a, b in zip(held[:2], other[:2])]
    far = [core_swap(part) for part in near]
    small = [
        tuple(part.reshape(-1, part.shape[2]) for part in pair) for pair in zip(near, far)
    ]
    starts = [0]
    for width in widths:
        starts.append(starts[-1] + width)
    moves = []
    half = CHIPS // 2
    for i, span in enumerate(spans):
        order = orders[i + 2]
        for target in range(len(widths)):
            cols_span = (starts[target], starts[target + 1])
            shared = overlap(cols_span, span)
            if shared is None:
                continue
            for side in range(2):

                def put(chip, core, index, side=side, order=order):
                    return chip ^ chip_offset(index + side * half, order, True)

                moves.append(
                    (
                        2 * i + side,
                        lambda chip, core, index: index,
                        target,
                        put,
                        box((0, rows), shifted_span(shared, span[0])),
                        box((0, rows), shifted_span(shared, cols_span[0])),
                    )
                )
    arrays = [part for pair in zip(held[2:], other[2:]) for part in pair]
    large = route(moves, half, place, arrays, [(CHIPS, rows, width) for width in widths])
    expand, shrink, adapter = [part.reshape(CHIPS * rows, part.shape[2]) for part in large]
    adapter = in_core_order(adapter, core_swap(adapter), core, 1)
    return small, expand, shrink, adapter, extra


def even_edges(width, count):
    tiles = width // LANES
    edges = [LANES * ((tiles * i + count - 1) // count) for i in range(count + 1)]
    return [(edges[i], edges[i + 1]) for i in range(count)]


def turn(left_ref, turned):
    for first in range(0, left_ref.shape[1], LANES):
        lanes = slice(first, first + LANES)
        turned[lanes, :] = left_ref[:, lanes].T


def slope_pack_kernel(
    orders, spans, place, left_a, right_a, left_b, right_b, extra_ref, *refs
):
    outs, (turned, tile, sems) = refs[:-3], refs[-3:]
    width = right_a.shape[1]
    step = pl.program_id(0)
    per_side = left_a.shape[1] // width
    total = 2 * per_side + 1
    blocks, rows = tile.shape[1], tile.shape[2]
    group = blocks // 4
    chip = place[0] >> 1
    slot = step % 2

    def sent(which, wide):
        box_ref = tile.at[which, :, :, pl.ds(0, wide)]
        return pltpu.make_async_copy(box_ref, box_ref, sems.at[which])

    @pl.when(step >= 2)
    def _():
        sent(slot, width).wait()

    @pl.when(step == 0)
    def _():
        turn(left_a, turned)

    @pl.when(step == per_side)
    def _():
        turn(left_b, turned)

    def fill(right):
        for part in range(4):
            lines = slice(part * group * rows, (part + 1) * group * rows)
            value = jnp.dot(turned[lines, :], right[...], preferred_element_type=jnp.float32)
            tile[slot, part * group : (part + 1) * group] = value.astype(tile.dtype).reshape(
                group, rows, width
            )

    @pl.when(step < per_side)
    def _():
        fill(right_a)

    @pl.when((step >= per_side) & (step < 2 * per_side))
    def _():
        fill(right_b)

    last = extra_ref.shape[2]

    @pl.when(step == 2 * per_side)
    def _():
        tile[slot, :, :, 0:last] = extra_ref[...]

    for index in range(total):
        begin = index * width
        wide = width if index < 2 * per_side else last
        goal = [i for i, span in enumerate(spans) if span[0] <= begin < span[1]][0]
        cols = pl.ds(begin - spans[goal][0], wide)

        @pl.when(step == index)
        def _(goal=goal, cols=cols, wide=wide):
            def send(place_in, carry):
                for side in range(2):
                    owner = chip ^ chip_offset(
                        place_in + side * (blocks // 2), orders[goal], True
                    )
                    pltpu.make_async_copy(
                        tile.at[slot, owner, :, pl.ds(0, wide)],
                        outs[2 * goal + side].at[place_in, :, cols],
                        sems.at[slot],
                    ).start()
                return carry

            lax.fori_loop(0, blocks // 2, send, 0)

    @pl.when(step == total - 1)
    def _():
        sent(1 - slot, width).wait()
        sent(slot, last).wait()


def packed_map_slopes(place, orders, spans, left_a, right_a, left_b, right_b, extra):
    depth, channels = left_a.shape
    hidden = right_a.shape[1]
    width = 384
    steps = hidden // width
    rows = channels // CHIPS
    extra = extra.reshape(CHIPS, rows, extra.shape[1])
    whole = pl.BlockSpec((depth, channels), lambda i: (0, 0), pipeline_mode=pl.Buffered(1))
    return pl.pallas_call(
        functools.partial(slope_pack_kernel, orders, spans),
        grid=(2 * steps + 1,),
        in_specs=[
            SCALARS,
            whole,
            pl.BlockSpec((depth, width), lambda i: (0, jnp.minimum(i, steps - 1))),
            whole,
            pl.BlockSpec((depth, width), lambda i: (0, jnp.clip(i - steps, 0, steps - 1))),
            pl.BlockSpec(extra.shape, lambda i: (0, 0, 0), pipeline_mode=pl.Buffered(1)),
        ],
        out_specs=[pl.BlockSpec(memory_space=pl.ANY)] * (2 * len(spans)),
        out_shape=[
            jax.ShapeDtypeStruct((CHIPS // 2, rows, high - low), jnp.bfloat16)
            for low, high in spans
            for _ in range(2)
        ],
        scratch_shapes=[
            pltpu.VMEM((channels, depth), jnp.bfloat16),
            pltpu.VMEM((2, CHIPS, rows, width), jnp.bfloat16),
            pltpu.SemaphoreType.DMA((2,)),
        ],
        compiler_params=pltpu.CompilerParams(vmem_limit_bytes=40 * 1024 * 1024),
        cost_estimate=pl.CostEstimate(flops=0, bytes_accessed=1 << 20, transcendentals=0),
    )(place, left_a, right_a, left_b, right_b, extra)


def unpacked_map_slopes(core, blocks, widths):
    block = jnp.concatenate(blocks, axis=1)
    own = own_half(block, core, 0)
    got = core_swap(own_half(block, core, 0, True).astype(jnp.bfloat16)).astype(jnp.float32)
    outs = []
    start = 0
    for width in widths:
        outs.append(
            in_core_order(own[:, start : start + width], got[:, start : start + width], core, 1)
        )
        start += width
    return outs


def row_sums(values):
    count = values.shape[0]
    pieces = lax.all_to_all(values, "dp", 0, 0, tiled=True)
    return jnp.sum(pieces.astype(jnp.float32), axis=0)


def row_copies(row):
    count = lax.axis_size("dp")
    return lax.all_to_all(jnp.broadcast_to(row[None], (count,) + row.shape), "dp", 0, 0, tiled=True)


def on_device(
    lowres_in,
    highres_in,
    image_sizes,
    attn_gain,
    query_weight,
    key_weight,
    value_weight,
    output_weight,
    mlp_gain,
    up_weight,
    down_weight,
    depth_kernel,
    conv_gain,
    expand_weight,
    shrink_weight,
    layer_scale,
    adapter_weight,
    adapter_kernel,
    gate_vector,
    out_cotangent,
    map_cotangent,
):
    device = lax.axis_index("dp")
    core = device & 1
    place = device.reshape(1).astype(jnp.int32)
    group_count = lax.axis_size("dp") // TILES
    position = (device + 2) % TILES
    group_id = (device + 2) // TILES % group_count
    model_half = lax.axis_index("mp")
    low_strip, _, grid_side, width = lowres_in.shape
    high_strip, _, high_side, channels = highres_in.shape
    own_width = adapter_kernel.shape[1]
    local_width = query_weight.shape[1]
    local_heads = local_width // HD
    scaling = HD ** (-0.5)
    token_count = low_strip * grid_side
    pixel_count = high_strip * high_side

    high_map = highres_in.reshape(high_strip, high_side, channels)
    table_ids = jnp.arange(image_sizes.shape[0])
    extent = jnp.sum(jnp.where(table_ids == group_id, image_sizes, 0))
    first_row = position * high_strip
    map_place = jnp.stack([first_row, extent]).astype(jnp.int32)
    token_rows = lowres_in.astype(jnp.float32).reshape(token_count, width)
    local_grad_low = out_cotangent.reshape(low_strip, grid_side, own_width)
    backs = []
    depth = query_weight.shape[0]
    pickers = [row_picker(device, rotated(i), depth) for i in range(2)]

    def convolve(map_low, map_high):
        backs.extend([map_low, map_high])
        return [map_conv(map_place, high_map, map_low, map_high, depth_kernel)]

    small, expand_full, shrink_full, adapter_full, extra = all_weights(
        place,
        core,
        (query_weight, key_weight, value_weight, output_weight.T, up_weight, down_weight.T),
        (expand_weight, shrink_weight.T, adapter_weight),
        list(halo_rows(high_map, RADIUS)),
        convolve,
    )
    map_low, map_high = backs
    convolved = extra[0].reshape(pixel_count, channels)
    normed_map, conv_norm_back = jax.vjp(normalize, convolved, conv_gain.astype(jnp.float32))
    normed_map_low = normed_map.astype(jnp.bfloat16)
    normed, attn_norm_back = jax.vjp(normalize, token_rows, attn_gain.astype(jnp.float32))
    normed_low = normed.astype(jnp.bfloat16)
    normed_first = matmul(normed_low, pickers[0]).astype(jnp.bfloat16)
    normed_map_pair = jnp.concatenate([normed_map_low, core_swap(normed_map_low)], axis=0)
    triple = 3 * local_width
    quad = 4 * local_width
    hidden_width = up_weight.shape[1]
    hidden_half = hidden_width // 2

    def pieces(index, low, high):
        return [part[:, low:high] for part in small[index]]

    qkv_parts = pieces(0, 0, triple)
    output_parts = pieces(0, triple, quad)
    up_parts = [pieces(0, quad, quad + hidden_half), pieces(1, 0, hidden_half)]
    down_parts = pieces(1, hidden_half, hidden_half + hidden_width)

    def picked(values, index):
        return matmul(values, pickers[index]).astype(jnp.bfloat16)

    def restored(values, index):
        return matmul_nt(values.astype(jnp.bfloat16), pickers[index])

    def into(values, parts):
        half = values.shape[1] // 2
        return matmul(values[:, :half], parts[0]) + matmul(values[:, half:], parts[1])

    def outof(values, parts):
        return jnp.concatenate([matmul_nt(values, part) for part in parts], axis=1)

    qkv_rows = into(normed_first, qkv_parts).astype(jnp.bfloat16)
    pair = qkv_rows[:, local_width:]
    pair = jnp.concatenate([pair, core_swap(pair)], axis=0)
    pair = jnp.concatenate([pair, pair_swap(pair)], axis=0)
    attended_low = attend(qkv_rows, pair)
    hidden_rows = token_rows + exchange(restored(outof(attended_low, output_parts), 0))
    normed_two, mlp_norm_back = jax.vjp(normalize, hidden_rows, mlp_gain.astype(jnp.float32))
    normed_two_low = normed_two.astype(jnp.bfloat16)
    normed_two_picked = [picked(normed_two_low, i) for i in range(2)]
    expanded = jnp.concatenate(
        [into(normed_two_picked[i], up_parts[i]) for i in range(2)], axis=1
    )
    activated_low, activated_slope = gelu_pair(expanded)
    result_own = restored(outof(activated_low, down_parts), 1).astype(jnp.bfloat16)
    result_rows = (
        hidden_rows + result_own.astype(jnp.float32) + model_swap(result_own).astype(jnp.float32)
    )

    result_grid = result_rows.reshape(low_strip, grid_side, width)
    gate_wide = gate_vector.astype(jnp.float32)
    gating = jax.nn.sigmoid(jnp.sum(result_grid * gate_wide, axis=-1, keepdims=True))
    out_grad = local_grad_low.astype(jnp.float32)
    lifted_grad_low = (out_grad * gating).reshape(token_count, own_width).astype(jnp.bfloat16)
    grid_shape = (low_strip, grid_side, channels)
    pooled_own = matmul_nt(lifted_grad_low, adapter_full).astype(jnp.bfloat16).reshape(grid_shape)
    pooled_other = model_swap(pooled_own)

    widened = matmul(normed_map_pair, expand_full)
    widened_low, widened_slope = gelu_pair(widened)
    widened_low = after(widened_low, pooled_own)
    narrowed_part, narrowed_given = dense(widened_low, shrink_full, True, halves=True)
    narrowed_part = narrowed_part + core_swap(narrowed_given).astype(jnp.float32)
    map_shape = (high_strip, high_side, channels)
    narrowed_own = narrowed_part.astype(jnp.bfloat16).reshape(map_shape)
    narrowed_own, pooled_other = together([narrowed_own, pooled_other])
    narrowed_other = model_swap(narrowed_own)

    map_grad, narrowed_grad_low = spread_map(
        map_place, pooled_own, pooled_other, map_cotangent.reshape(map_shape), layer_scale[None]
    )
    narrowed_grad_low = narrowed_grad_low.reshape(pixel_count, channels)
    narrowed_grad_pair = jnp.concatenate([narrowed_grad_low, core_swap(narrowed_grad_low)], axis=0)
    (widened_grad_low,) = dense(narrowed_grad_pair, shrink_full, False, widened_slope)
    normed_map_part, normed_map_given = dense(widened_grad_low, expand_full, True, halves=True)
    normed_map_given, narrowed_other = together([normed_map_given, narrowed_other])
    normed_map_part = normed_map_part + core_swap(normed_map_given).astype(jnp.float32)
    normed_map_own = normed_map_part.astype(jnp.bfloat16)

    mapped, pooled_low, layer_scale_slope = blend_map(
        map_place, narrowed_own, narrowed_other, high_map, layer_scale[None], map_grad
    )
    pooled_low = pooled_low.reshape(token_count, channels)
    lifted = matmul(pooled_low, adapter_full).reshape(low_strip, grid_side, own_width)

    own_result = lax.dynamic_slice_in_dim(result_grid, model_half * own_width, own_width, 2)
    own_result_low = own_result.astype(jnp.bfloat16)
    both_low = jnp.concatenate([own_result_low, local_grad_low], axis=2)
    both_edges = halo_rows(after(both_low, widened_grad_low), 1)
    mix_place = jnp.stack([position * low_strip, TILES * low_strip]).astype(jnp.int32)
    local_mix, local_back, adapter_kernel_slope = mix(
        mix_place, both_low, *both_edges, adapter_kernel
    )
    blended = own_result + local_mix + gating * lifted

    gate_part = jnp.sum(out_grad * lifted, axis=-1, keepdims=True)
    gate_grad = exchange(gate_part)
    adapter_slope = matmul_tn(pooled_low, lifted_grad_low)
    adapter_slope = own_half(adapter_slope, core, 1) + core_swap(
        own_half(adapter_slope, core, 1, True).astype(jnp.bfloat16)
    ).astype(jnp.float32)
    own_grad = out_grad + local_back
    own_grad_low = own_grad.astype(jnp.bfloat16)
    other_grad = model_swap(own_grad_low)
    result_grad = in_core_order(own_grad_low, other_grad, model_half, 2).astype(jnp.float32)
    gate_slope = gate_grad * gating * (1.0 - gating)
    gate_vector_slope = jnp.sum((gate_slope * result_grid).reshape(token_count, width), axis=0)
    result_grad = (result_grad + gate_slope * gate_wide).reshape(token_count, width)

    result_low = after(result_grad.astype(jnp.bfloat16), widened_grad_low)
    result_picked = picked(result_low, 1)
    activated_grad = into(result_picked, down_parts)
    expanded_grad_low = (activated_grad * activated_slope.astype(jnp.float32)).astype(jnp.bfloat16)
    expanded_grad_parts = [expanded_grad_low[:, :hidden_half], expanded_grad_low[:, hidden_half:]]
    second_slopes = split_rows(
        paired_slopes(
            (normed_two_picked[1], result_picked), (expanded_grad_parts[1], activated_low)
        )
    )
    second_far = core_swap(second_slopes[1])
    normed_two_own = sum(
        restored(outof(expanded_grad_parts[i], up_parts[i]), i) for i in range(2)
    ).astype(jnp.bfloat16)
    normed_two_other = model_swap(normed_two_own)
    normed_two_other, normed_map_own = together([normed_two_other, normed_map_own])
    normed_map_other = model_swap(normed_map_own)
    normed_two_grad = normed_two_own.astype(jnp.float32) + normed_two_other.astype(jnp.float32)
    hidden_part, mlp_gain_slope = mlp_norm_back(normed_two_grad)
    hidden_grad = result_grad + hidden_part
    hidden_low = hidden_grad.astype(jnp.bfloat16)
    hidden_picked = picked(hidden_low, 0)
    attended_grad_low = into(hidden_picked, output_parts).astype(jnp.bfloat16)
    query_grad_rows, key_grad_all, value_grad_all = attend_back(qkv_rows, pair, attended_grad_low)
    pair_back = jnp.concatenate(
        [key_grad_all, value_grad_all], axis=1
    )
    pair_other = pair_swap(pair_back[2 * token_count :].astype(jnp.bfloat16))
    map_widths = (widened_low.shape[1], widened_low.shape[1], adapter_slope.shape[1])
    map_slopes_packed = packed_map_slopes(
        after(place, attended_grad_low),
        [rotated(i) for i in range(2, 5)],
        even_edges(sum(map_widths), 3),
        normed_map_pair,
        widened_grad_low,
        narrowed_grad_pair,
        widened_low,
        adapter_slope.astype(jnp.bfloat16),
    )
    pair_other, normed_map_other, *map_slopes_packed = together(
        [pair_other, normed_map_other, *map_slopes_packed]
    )
    pair_back = pair_back[: 2 * token_count] + pair_other.astype(jnp.float32)
    pair_back = pair_back[:token_count] + core_swap(
        pair_back[token_count:].astype(jnp.bfloat16)
    ).astype(jnp.float32)
    qkv_grad = jnp.concatenate([query_grad_rows, pair_back.astype(jnp.bfloat16)], axis=1)
    normed_own = restored(outof(qkv_grad, qkv_parts), 0).astype(jnp.bfloat16)
    normed_other = model_swap(normed_own)
    first_slopes = split_rows(
        paired_slopes(
            (normed_first, hidden_picked, normed_two_picked[0]),
            (qkv_grad, attended_low, expanded_grad_parts[0]),
        )
    )
    first_far = core_swap(first_slopes[1])
    normed_map_grad = normed_map_own.astype(jnp.float32) + normed_map_other.astype(jnp.float32)
    convolved_grad, conv_gain_slope = conv_norm_back(normed_map_grad)
    convolved_grad_low = convolved_grad.reshape(map_shape).astype(jnp.bfloat16)
    grad_low, grad_high = halo_rows(convolved_grad_low, RADIUS)
    grad_low, grad_high, *map_slopes_packed = together(
        [grad_low, grad_high, *map_slopes_packed]
    )
    near = [
        split_sum(pair[0], part)
        for pair, part in ((first_slopes, first_far), (second_slopes, second_far))
    ]
    scatter = Scatter(
        [low for low, _ in near] + list(map_slopes_packed[0::2]),
        [high for _, high in near] + list(map_slopes_packed[1::2]),
        [rotated(i)[::-1] for i in range(5)],
    )

    depth_kernel_slope = map_slopes(map_place, high_map, map_low, map_high, convolved_grad_low)
    highres_grad = map_conv(
        map_place, convolved_grad_low, grad_low, grad_high, depth_kernel, map_grad
    )
    normed_grad = normed_own.astype(jnp.float32) + normed_other.astype(jnp.float32)
    input_part, attn_gain_slope = attn_norm_back(normed_grad)
    lowres_grad = (hidden_grad + input_part).reshape(low_strip, 1, grid_side, width)

    def as_rows(values):
        return jnp.pad(values, ((0, 0), (0, channels - values.shape[1])))

    minor_rows = jnp.concatenate(
        [
            depth_kernel_slope,
            conv_gain_slope[None],
            layer_scale_slope,
            as_rows(jnp.stack([attn_gain_slope, mlp_gain_slope, gate_vector_slope], 0)),
            as_rows(adapter_kernel_slope),
        ],
        axis=0,
    )
    lines = channels // LANES
    block_rows = -(-lines // 16) * 16
    minor = jnp.pad(
        minor_rows.astype(jnp.bfloat16).reshape(minor_rows.shape[0], lines, LANES),
        ((0, 2 * CHIPS - minor_rows.shape[0]), (0, block_rows - lines), (0, 0)),
    )
    depth_kernel_slope, highres_grad = scatter.advance(depth_kernel_slope, highres_grad)
    minor_own = row_sums(minor).astype(jnp.bfloat16)
    (minor_own,) = scatter.advance(minor_own)
    minor_copies = row_copies(minor_own)
    (minor_copies,) = scatter.advance(minor_copies)
    minor_all = (
        minor_copies[:, :lines].reshape(2 * CHIPS, channels).astype(jnp.float32)
    )
    while scatter.step < len(RINGS):
        scatter.advance()
    first_own, second_own, *map_blocks = scatter.result()
    up_own = jnp.concatenate([first_own[:, quad:], second_own[:, :hidden_half]], axis=1)
    down_own = second_own[:, hidden_half:]
    expand_own, shrink_own, adapter_own = unpacked_map_slopes(
        core,
        map_blocks,
        map_widths,
    )
    firsts = [first_own[:, i * local_width : (i + 1) * local_width] for i in range(4)]
    taps = depth_kernel.shape[0]
    side_taps = adapter_kernel.shape[0]
    return (
        blended.astype(jnp.bfloat16)[:, None],
        mapped[:, None],
        lowres_grad,
        highres_grad[:, None],
        minor_all[taps + 2, :width],
        firsts[0],
        firsts[1],
        firsts[2],
        firsts[3].T,
        minor_all[taps + 3, :width],
        up_own,
        down_own.T,
        minor_all[:taps],
        minor_all[taps],
        expand_own,
        shrink_own.T,
        minor_all[taps + 1],
        adapter_own,
        minor_all[taps + 5 : taps + 5 + side_taps, :own_width],
        minor_all[taps + 4, :width],
    )


def solution(mesh):
    in_specs = (
        P("dp", None, None, None),
        P("dp", None, None, None),
        P(),
        P(),
        P("dp", "mp"),
        P("dp", "mp"),
        P("dp", "mp"),
        P("mp", "dp"),
        P(),
        P("dp", "mp"),
        P("mp", "dp"),
        P(),
        P(),
        P("dp", "mp"),
        P("mp", "dp"),
        P(),
        P("dp", "mp"),
        P(None, "mp"),
        P(),
        P("dp", None, None, "mp"),
        P("dp", None, None, None),
    )
    out_specs = (
        P("dp", None, None, "mp"),
        P("dp", None, None, None),
        P("dp", None, None, None),
        P("dp", None, None, None),
        P(),
        P("dp", "mp"),
        P("dp", "mp"),
        P("dp", "mp"),
        P("mp", "dp"),
        P(),
        P("dp", "mp"),
        P("mp", "dp"),
        P(),
        P(),
        P("dp", "mp"),
        P("mp", "dp"),
        P(),
        P("dp", "mp"),
        P(None, "mp"),
        P(),
    )
    return jax.shard_map(
        on_device, mesh=mesh, in_specs=in_specs, out_specs=out_specs, check_vma=False
    )
```

```python
import functools

import jax
import jax.numpy as jnp
from jax import lax
from jax.experimental import pallas as pl
from jax.experimental.pallas import tpu as pltpu
from jax.sharding import PartitionSpec as P

HD = 64
TILES = 4
CHIPS = 32
CORE = 1
RINGS = (2, 6, 8, 24, 32)

norm_epsilon = 1e-06

LANES = 128
RADIUS = 3
WINDOW = 7
PAD = 8


def masked_rows(place, main_ref, low_ref, high_ref, wide, strip, side, bounded):
    first, extent = place[0], place[1]
    cols = lax.broadcasted_iota(jnp.int32, (side, LANES), 0)

    def put(slot, value):
        row = first + slot - RADIUS
        limit = extent if bounded else side
        keep = (cols < limit) & (row >= 0) & (row < limit)
        wide[slot] = jnp.where(keep, value.astype(jnp.float32), 0.0)

    for slot in range(RADIUS):
        put(slot, low_ref[slot])
        put(RADIUS + strip + slot, high_ref[slot])
    for slot in range(strip):
        put(RADIUS + slot, main_ref[slot])


def window_sum(wide, taps_ref, shifted, row, side, flipped):
    sums = [None] * WINDOW
    for a in range(WINDOW):
        line = wide[row + a]
        for b in range(WINDOW):
            tap = WINDOW * a + b
            if flipped:
                tap = WINDOW * WINDOW - 1 - tap
            term = line * taps_ref[tap : tap + 1]
            sums[b] = term if sums[b] is None else sums[b] + term
    total = sums[RADIUS]
    for b in range(WINDOW):
        if b != RADIUS:
            shifted[b, PAD : PAD + side] = sums[b]
    for b in range(WINDOW):
        if b != RADIUS:
            total = total + shifted[b, PAD + b - RADIUS : PAD + b - RADIUS + side]
    return total


def clear_edges(shifted, side):
    for b in range(WINDOW):
        shifted[b, 0:PAD] = jnp.zeros((PAD, LANES), jnp.float32)
        shifted[b, PAD + side : 2 * PAD + side] = jnp.zeros((PAD, LANES), jnp.float32)


def forward_kernel(place, main_ref, low_ref, high_ref, taps_in, out_ref, wide, taps, shifted):
    strip, side = main_ref.shape[0], main_ref.shape[1]
    masked_rows(place, main_ref, low_ref, high_ref, wide, strip, side, True)
    clear_edges(shifted, side)
    taps[...] = taps_in[...].astype(jnp.float32)

    def step(row, carry):
        out_ref[row] = window_sum(wide, taps, shifted, row, side, False)
        return carry

    lax.fori_loop(0, strip, step, 0)


def backward_kernel(place, main_ref, low_ref, high_ref, taps_in, add_ref, out_ref, wide, taps, shifted):
    strip, side = main_ref.shape[0], main_ref.shape[1]
    masked_rows(place, main_ref, low_ref, high_ref, wide, strip, side, False)
    clear_edges(shifted, side)
    taps[...] = taps_in[...].astype(jnp.float32)
    cols = lax.broadcasted_iota(jnp.int32, (side, LANES), 0)

    def step(row, carry):
        total = window_sum(wide, taps, shifted, row, side, True) + add_ref[row]
        keep = (cols < place[1]) & (place[0] + row < place[1])
        out_ref[row] = jnp.where(keep, total, 0.0)
        return carry

    lax.fori_loop(0, strip, step, 0)


def slope_kernel(place, main_ref, low_ref, high_ref, grad_ref, out_ref, wide, padded):
    strip, side = main_ref.shape[0], main_ref.shape[1]
    masked_rows(place, main_ref, low_ref, high_ref, wide, strip, side, True)
    edge = jnp.zeros((PAD, LANES), jnp.float32)
    for row in range(strip):
        padded[row, 0:PAD] = edge
        padded[row, PAD : PAD + side] = grad_ref[row].astype(jnp.float32)
        padded[row, PAD + side : 2 * PAD + side] = edge
    for group in ((0, 1, 2, 3), (4, 5, 6)):

        def step(row, sums):
            lines = [wide[row + a] for a in group]
            fresh = list(sums)
            for b in range(WINDOW):
                start = PAD + RADIUS - b
                part = padded[row, start : start + side]
                for i in range(len(group)):
                    term = (lines[i] * part).reshape(side // 8, 8, LANES)
                    fresh[i * WINDOW + b] = fresh[i * WINDOW + b] + jnp.sum(term, axis=0)
            return tuple(fresh)

        start = tuple(jnp.zeros((8, LANES), jnp.float32) for _ in range(len(group) * WINDOW))
        sums = lax.fori_loop(0, strip, step, start)
        for i, a in enumerate(group):
            for b in range(WINDOW):
                tap = a * WINDOW + b
                out_ref[tap : tap + 1] = jnp.sum(sums[i * WINDOW + b], axis=0, keepdims=True)


def block3(rows, side):
    return pl.BlockSpec((rows, side, LANES), lambda i: (0, 0, i))


SCALARS = pl.BlockSpec(memory_space=pltpu.SMEM)


def map_conv(place, main, low, high, taps, added=None):
    strip, side, channels = main.shape
    count = taps.shape[0]
    tap_spec = pl.BlockSpec((count, LANES), lambda i: (0, i))
    specs = [SCALARS, block3(strip, side), block3(RADIUS, side), block3(RADIUS, side), tap_spec]
    args = [place, main, low, high, taps]
    if added is not None:
        specs.append(block3(strip, side))
        args.append(added)
    work = strip * side * channels
    return pl.pallas_call(
        forward_kernel if added is None else backward_kernel,
        grid=(channels // LANES,),
        in_specs=specs,
        out_specs=block3(strip, side),
        out_shape=jax.ShapeDtypeStruct((strip, side, channels), jnp.float32),
        scratch_shapes=[
            pltpu.VMEM((strip + 2 * RADIUS, side, LANES), jnp.float32),
            pltpu.VMEM((count, LANES), jnp.float32),
            pltpu.VMEM((WINDOW, side + 2 * PAD, LANES), jnp.float32),
        ],
        compiler_params=pltpu.CompilerParams(vmem_limit_bytes=24 * 1024 * 1024),
        cost_estimate=pl.CostEstimate(flops=0, bytes_accessed=work // 8, transcendentals=0),
    )(*args)


def map_slopes(place, main, low, high, grad):
    strip, side, channels = main.shape
    count = WINDOW * WINDOW
    work = strip * side * channels
    return pl.pallas_call(
        slope_kernel,
        grid=(channels // LANES,),
        in_specs=[SCALARS, block3(strip, side), block3(RADIUS, side), block3(RADIUS, side), block3(strip, side)],
        out_specs=pl.BlockSpec((count, LANES), lambda i: (0, i)),
        out_shape=jax.ShapeDtypeStruct((count, channels), jnp.float32),
        scratch_shapes=[
            pltpu.VMEM((strip + 2 * RADIUS, side, LANES), jnp.float32),
            pltpu.VMEM((strip, side + 2 * PAD, LANES), jnp.float32),
        ],
        compiler_params=pltpu.CompilerParams(vmem_limit_bytes=24 * 1024 * 1024),
        cost_estimate=pl.CostEstimate(flops=0, bytes_accessed=work // 8, transcendentals=0),
    )(place, main, low, high, grad)


WIDE = 384


def inside(place, row, side):
    cols = lax.broadcasted_iota(jnp.int32, (side, LANES), 0)
    return (cols < place[1]) & (place[0] + row < place[1])


def blend_kernel(
    place, own_ref, other_ref, map_ref, scale_ref, grad_ref, out_ref, pool_ref, slope_ref, line
):
    strip, side = map_ref.shape[0], map_ref.shape[1]
    half = side // 2
    for part in range(map_ref.shape[2] // LANES):
        lanes = slice(part * LANES, (part + 1) * LANES)
        scale = scale_ref[:, lanes].astype(jnp.float32)

        def step(pair, slope):
            total = None
            for i in range(2):
                row = 2 * pair + i
                narrow = own_ref[row, :, lanes].astype(jnp.float32) + other_ref[
                    row, :, lanes
                ].astype(jnp.float32)
                value = map_ref[row, :, lanes].astype(jnp.float32) + scale * narrow
                value = jnp.where(inside(place, row, side), value, 0.0)
                out_ref[row, :, lanes] = value.astype(out_ref.dtype)
                total = value if total is None else total + value
                product = grad_ref[row, :, lanes] * narrow
                slope = slope + jnp.sum(product.reshape(side // 8, 8, LANES), axis=0)
            line[...] = total
            pooled = line[pl.ds(0, half, 2), :] + line[pl.ds(1, half, 2), :]
            pool_ref[pair, :, lanes] = (pooled * 0.25).astype(pool_ref.dtype)
            return slope

        slope = lax.fori_loop(0, strip // 2, step, jnp.zeros((8, LANES), jnp.float32))
        slope_ref[:, lanes] = jnp.sum(slope, axis=0, keepdims=True)


def spread_kernel(place, pool_ref, pool_other_ref, cot_ref, scale_ref, grad_ref, low_ref, line):
    strip, side = cot_ref.shape[0], cot_ref.shape[1]
    half = side // 2
    for part in range(cot_ref.shape[2] // LANES):
        lanes = slice(part * LANES, (part + 1) * LANES)
        scale = scale_ref[:, lanes].astype(jnp.float32)

        def step(pair, carry):
            pooled = pool_ref[pair, :, lanes].astype(jnp.float32) + pool_other_ref[
                pair, :, lanes
            ].astype(jnp.float32)
            pooled = pooled * 0.25
            line[pl.ds(0, half, 2), :] = pooled
            line[pl.ds(1, half, 2), :] = pooled
            spread = line[...]
            for i in range(2):
                row = 2 * pair + i
                value = cot_ref[row, :, lanes].astype(jnp.float32) + spread
                value = jnp.where(inside(place, row, side), value, 0.0)
                grad_ref[row, :, lanes] = value
                low_ref[row, :, lanes] = (value * scale).astype(low_ref.dtype)
            return carry

        lax.fori_loop(0, strip // 2, step, 0)


def wide_block(*lead):
    return pl.BlockSpec(lead + (WIDE,), lambda i: (0,) * len(lead) + (i,))


def blend_map(place, own, other, main, scale, grad):
    strip, side, channels = main.shape
    full = wide_block(strip, side)
    pool = (strip // 2, side // 2)
    return pl.pallas_call(
        blend_kernel,
        grid=(channels // WIDE,),
        in_specs=[SCALARS, full, full, full, wide_block(1), full],
        out_specs=[full, wide_block(*pool), wide_block(1)],
        out_shape=[
            jax.ShapeDtypeStruct(main.shape, jnp.bfloat16),
            jax.ShapeDtypeStruct(pool + (channels,), jnp.bfloat16),
            jax.ShapeDtypeStruct((1, channels), jnp.float32),
        ],
        scratch_shapes=[pltpu.VMEM((side, LANES), jnp.float32)],
        compiler_params=pltpu.CompilerParams(vmem_limit_bytes=24 * 1024 * 1024),
        cost_estimate=pl.CostEstimate(flops=0, bytes_accessed=1 << 20, transcendentals=0),
    )(place, own, other, main, scale, grad)


def spread_map(place, pool, pool_other, cot, scale):
    strip, side, channels = cot.shape
    full = wide_block(strip, side)
    pooled = wide_block(strip // 2, side // 2)
    return pl.pallas_call(
        spread_kernel,
        grid=(channels // WIDE,),
        in_specs=[SCALARS, pooled, pooled, full, wide_block(1)],
        out_specs=[full, full],
        out_shape=[
            jax.ShapeDtypeStruct(cot.shape, jnp.float32),
            jax.ShapeDtypeStruct(cot.shape, jnp.bfloat16),
        ],
        scratch_shapes=[pltpu.VMEM((side, LANES), jnp.float32)],
        compiler_params=pltpu.CompilerParams(vmem_limit_bytes=24 * 1024 * 1024),
        cost_estimate=pl.CostEstimate(flops=0, bytes_accessed=1 << 20, transcendentals=0),
    )(place, pool, pool_other, cot, scale)


def head_lanes(rows, head):
    lanes = lax.broadcasted_iota(jnp.int32, (rows, LANES), 1)
    return (lanes >= head * HD) & (lanes < (head + 1) * HD)


def nt(former, latter):
    return lax.dot_general(
        former, latter, (((1,), (1,)), ((), ())), preferred_element_type=jnp.float32
    )


def tn(former, latter):
    return lax.dot_general(
        former, latter, (((0,), (0,)), ((), ())), preferred_element_type=jnp.float32
    )


def softmax_rows(scores):
    top = jnp.max(scores, axis=-1, keepdims=True)
    raised = jnp.exp(scores - top)
    return raised * (1.0 / jnp.sum(raised, axis=-1, keepdims=True))


def attend_kernel(query_ref, key_ref, value_ref, out_ref):
    rows = query_ref.shape[0]
    query, key, value = query_ref[...], key_ref[...], value_ref[...]
    total = jnp.zeros((rows, LANES), jnp.float32)
    for head in range(LANES // HD):
        mine = head_lanes(rows, head)
        scores = nt(jnp.where(mine, query, jnp.zeros_like(query)), key) * HD ** (-0.5)
        weights = softmax_rows(scores).astype(jnp.bfloat16)
        part = jnp.dot(weights, value, preferred_element_type=jnp.float32)
        total = jnp.where(mine, part, total)
    out_ref[...] = total.astype(out_ref.dtype)


def attend_back_kernel(
    query_ref, key_ref, value_ref, grad_ref, query_out, key_out, value_out
):
    rows = query_ref.shape[0]
    query, key, value, grad = query_ref[...], key_ref[...], value_ref[...], grad_ref[...]
    none = jnp.zeros_like(query)
    query_grad = jnp.zeros((rows, LANES), jnp.float32)
    key_grad, value_grad = None, None
    for head in range(LANES // HD):
        mine = head_lanes(rows, head)
        query_own = jnp.where(mine, query, none)
        grad_own = jnp.where(mine, grad, none)
        weights = softmax_rows(nt(query_own, key) * HD ** (-0.5))
        weight_grad = nt(grad_own, value)
        row_dot = jnp.sum(weights * weight_grad, axis=-1, keepdims=True)
        score_grad = (weights * (weight_grad - row_dot)).astype(jnp.bfloat16)
        part = jnp.dot(score_grad, key, preferred_element_type=jnp.float32)
        query_grad = jnp.where(mine, part, query_grad)
        key_part = tn(score_grad, query_own)
        value_part = tn(weights.astype(jnp.bfloat16), grad_own)
        key_grad = key_part if key_grad is None else key_grad + key_part
        value_grad = value_part if value_grad is None else value_grad + value_part
    query_out[...] = (query_grad * HD ** (-0.5)).astype(query_out.dtype)
    key_out[...] = key_grad * HD ** (-0.5)
    value_out[...] = value_grad


def lane_block(rows, shift=0):
    return pl.BlockSpec((rows, LANES), lambda i: (0, i + shift))


def attend(rows, pair):
    count, keys = rows.shape[0], pair.shape[0]
    width = pair.shape[1] // 2
    steps = width // LANES
    work = 4 * count * keys * width
    return pl.pallas_call(
        attend_kernel,
        grid=(steps,),
        in_specs=[lane_block(count), lane_block(keys), lane_block(keys, steps)],
        out_specs=lane_block(count),
        out_shape=jax.ShapeDtypeStruct((count, width), jnp.bfloat16),
        compiler_params=pltpu.CompilerParams(vmem_limit_bytes=24 * 1024 * 1024),
        cost_estimate=pl.CostEstimate(flops=0, bytes_accessed=1 << 20, transcendentals=0),
    )(rows, pair, pair)


def attend_back(rows, pair, grad):
    count, keys = rows.shape[0], pair.shape[0]
    width = pair.shape[1] // 2
    steps = width // LANES
    work = 10 * count * keys * width
    return pl.pallas_call(
        attend_back_kernel,
        grid=(steps,),
        in_specs=[
            lane_block(count),
            lane_block(keys),
            lane_block(keys, steps),
            lane_block(count),
        ],
        out_specs=[lane_block(count), lane_block(keys), lane_block(keys)],
        out_shape=[
            jax.ShapeDtypeStruct((count, width), jnp.bfloat16),
            jax.ShapeDtypeStruct((keys, width), jnp.float32),
            jax.ShapeDtypeStruct((keys, width), jnp.float32),
        ],
        compiler_params=pltpu.CompilerParams(vmem_limit_bytes=24 * 1024 * 1024),
        cost_estimate=pl.CostEstimate(flops=0, bytes_accessed=1 << 20, transcendentals=0),
    )(rows, pair, pair, grad)


def slopes_kernel(ends, *refs):
    count = len(ends)
    lefts, rights = refs[:count], refs[count : 2 * count]
    near_ref, far_ref = refs[2 * count :]
    half = near_ref.shape[0]
    step = pl.program_id(0)
    first = 0
    for left, right, end in zip(lefts, rights, ends):

        @pl.when((step >= first) & (step < end))
        def _(left=left, right=right):
            near_ref[...] = tn(left[:, :half], right[...]).astype(near_ref.dtype)
            far_ref[...] = tn(left[:, half:], right[...]).astype(far_ref.dtype)

        first = end


def paired_slopes(lefts, rights):
    tile = 512
    rows, depth = lefts[0].shape
    half = depth // 2
    starts, ends = [], []
    total = 0
    for right in rights:
        starts.append(total)
        total += right.shape[1] // tile
        ends.append(total)

    def column(start, end):
        return lambda i: (0, jnp.clip(i - start, 0, end - start - 1))

    whole = pl.BlockSpec((rows, depth), lambda i: (0, 0))
    out = pl.BlockSpec((half, tile), lambda i: (0, i))
    shape = jax.ShapeDtypeStruct((half, total * tile), jnp.bfloat16)
    near, far = pl.pallas_call(
        functools.partial(slopes_kernel, tuple(ends)),
        grid=(total,),
        in_specs=[whole] * len(lefts)
        + [pl.BlockSpec((rows, tile), column(a, b)) for a, b in zip(starts, ends)],
        out_specs=[out, out],
        out_shape=[shape, shape],
        compiler_params=pltpu.CompilerParams(vmem_limit_bytes=24 * 1024 * 1024),
        cost_estimate=pl.CostEstimate(
            flops=0,
            bytes_accessed=1 << 20,
            transcendentals=0,
        ),
    )(*lefts, *rights)
    return near, far


def split_rows(pair):
    return [part.reshape(CHIPS, part.shape[0] // CHIPS, part.shape[1]) for part in pair]


def dense_kernel(flipped, scaled, halves, lefts, *refs):
    left_refs, right_ref, refs = refs[:lefts], refs[lefts], refs[lefts + 1 :]
    scale_ref, outs = (refs[0], refs[1:]) if scaled else (None, refs)
    rows = sum(ref.shape[0] for ref in left_refs)
    chunk = rows // 6
    for part in range(6):
        lines = slice(part * chunk, (part + 1) * chunk)
        product = nt if flipped else functools.partial(jnp.dot, preferred_element_type=jnp.float32)
        left = left_refs[part * lefts // 6]
        start = part * chunk % left.shape[0]
        value = product(left[start : start + chunk, :], right_ref[...])
        if scaled:
            value = value * scale_ref[lines, :].astype(jnp.float32)
        if halves:
            out, first = (outs[0], 0) if part < 3 else (outs[1], rows // 2)
            out[part * chunk - first : (part + 1) * chunk - first, :] = value.astype(out.dtype)
        else:
            outs[0][lines, :] = value.astype(outs[0].dtype)


def dense(lefts, right, flipped, scale=None, halves=False):
    rows, depth = sum(left.shape[0] for left in lefts), lefts[0].shape[1]
    count = right.shape[0] if flipped else right.shape[1]
    tile = 512
    specs = [
        *(
            pl.BlockSpec(left.shape, lambda i: (0, 0), pipeline_mode=pl.Buffered(1))
            for left in lefts
        ),
        pl.BlockSpec((tile, depth), lambda i: (i, 0))
        if flipped
        else pl.BlockSpec((depth, tile), lambda i: (0, i)),
    ]
    args = [*lefts, right]
    if scale is not None:
        specs.append(pl.BlockSpec((rows, tile), lambda i: (0, i)))
        args.append(scale)
    if halves:
        kinds = [(rows // 2, jnp.float32), (rows // 2, jnp.bfloat16)]
    else:
        kinds = [(rows, jnp.bfloat16)]
    return pl.pallas_call(
        functools.partial(dense_kernel, flipped, scale is not None, halves, len(lefts)),
        grid=(count // tile,),
        in_specs=specs,
        out_specs=[pl.BlockSpec((size, tile), lambda i: (0, i)) for size, _ in kinds],
        out_shape=[jax.ShapeDtypeStruct((size, count), kind) for size, kind in kinds],
        compiler_params=pltpu.CompilerParams(vmem_limit_bytes=24 * 1024 * 1024),
        cost_estimate=pl.CostEstimate(flops=0, bytes_accessed=1 << 20, transcendentals=0),
    )(*[pltpu.with_memory_space_constraint(a, pltpu.MemorySpace.HBM) for a in args])


def mix_kernel(place, main_ref, low_ref, high_ref, taps_ref, mix_ref, back_ref, slope_ref, wide):
    strip, side, width = mix_ref.shape
    top, bottom = place[0] > 0, place[0] + strip < place[1]
    blank = jnp.zeros((PAD, LANES), jnp.float32)
    for first in range(0, width, LANES):
        for kind in range(2):
            lanes = slice(kind * width + first, kind * width + first + LANES)
            for slot in range(strip + 2):
                if slot == 0:
                    value = jnp.where(top, low_ref[0, :, lanes].astype(jnp.float32), 0.0)
                elif slot == strip + 1:
                    value = jnp.where(bottom, high_ref[0, :, lanes].astype(jnp.float32), 0.0)
                else:
                    value = main_ref[slot - 1, :, lanes].astype(jnp.float32)
                wide[kind, slot, 0:PAD] = blank
                wide[kind, slot, PAD : PAD + side] = value
                wide[kind, slot, PAD + side : 2 * PAD + side] = blank
        own = slice(first, first + LANES)
        taps = taps_ref[:, own].astype(jnp.float32)
        sums = [jnp.zeros((side, LANES), jnp.float32) for _ in range(9)]
        for row in range(strip):
            grad = wide[1, row + 1, PAD : PAD + side]
            mixed = jnp.zeros((side, LANES), jnp.float32)
            back = jnp.zeros((side, LANES), jnp.float32)
            for a in range(3):
                for b in range(3):
                    tap = 3 * a + b
                    span = slice(PAD + b - 1, PAD + b - 1 + side)
                    value = wide[0, row + a, span]
                    mixed = mixed + value * taps[tap : tap + 1]
                    back = back + wide[1, row + a, span] * taps[8 - tap : 9 - tap]
                    sums[tap] = sums[tap] + value * grad
            mix_ref[row, :, own] = mixed
            back_ref[row, :, own] = back
        for tap in range(9):
            slope_ref[tap : tap + 1, own] = jnp.sum(sums[tap], axis=0, keepdims=True)


def mix(place, both, low, high, taps):
    strip, side, double = both.shape
    width = double // 2
    grid = jax.ShapeDtypeStruct((strip, side, width), jnp.float32)
    return pl.pallas_call(
        mix_kernel,
        in_specs=[SCALARS] + [pl.BlockSpec(memory_space=pltpu.VMEM)] * 4,
        out_specs=[pl.BlockSpec(memory_space=pltpu.VMEM)] * 3,
        out_shape=[grid, grid, jax.ShapeDtypeStruct(taps.shape, jnp.float32)],
        scratch_shapes=[pltpu.VMEM((2, strip + 2, side + 2 * PAD, LANES), jnp.float32)],
        compiler_params=pltpu.CompilerParams(vmem_limit_bytes=16 * 1024 * 1024),
        cost_estimate=pl.CostEstimate(flops=0, bytes_accessed=1 << 20, transcendentals=0),
    )(place, both, low, high, taps)


def row_moments(value):
    average = jnp.mean(value, axis=-1, keepdims=True)
    centred = value - average
    spread = jnp.mean(centred * centred, axis=-1, keepdims=True)
    rate = lax.rsqrt(spread + norm_epsilon)
    return centred * rate, rate


def wide_sum(refs):
    total = refs[0][...].astype(jnp.float32)
    for ref in refs[1:]:
        total = total + ref[...].astype(jnp.float32)
    return total


def norm_kernel(count, *refs):
    gain = refs[count][...].astype(jnp.float32)
    total = wide_sum(refs[:count])
    outs = refs[count + 1 :]
    shape, _ = row_moments(total)
    outs[-1][...] = (shape * gain).astype(outs[-1].dtype)
    if count > 1:
        outs[0][...] = total


def norm_back_kernel(kinds, value_ref, own_ref, other_ref, gain_ref, *refs):
    extra, (slope_ref, *outs) = (refs[0], refs[1:]) if kinds[0] else (None, refs)
    gain = gain_ref[...].astype(jnp.float32)
    shape, rate = row_moments(value_ref[...].astype(jnp.float32))
    grad = own_ref[...].astype(jnp.float32) + other_ref[...].astype(jnp.float32)
    scaled = grad * gain
    first = jnp.mean(scaled, axis=-1, keepdims=True)
    second = jnp.mean(scaled * shape, axis=-1, keepdims=True)
    result = rate * (scaled - first - shape * second)
    if extra is not None:
        result = result + extra[...]
    for out in outs:
        out[...] = result.astype(out.dtype)
    slope = jnp.sum(grad * shape, axis=0, keepdims=True)

    @pl.when(pl.program_id(0) == 0)
    def _():
        slope_ref[...] = slope

    @pl.when(pl.program_id(0) > 0)
    def _():
        slope_ref[...] += slope


ROWS = 144
CHEAP = pl.CostEstimate(flops=0, bytes_accessed=1 << 20, transcendentals=0)


def row_block(width):
    return pl.BlockSpec((ROWS, width), lambda i: (i, 0))


def norm(values, gain):
    rows, width = values[0].shape
    whole = pl.BlockSpec((1, width), lambda i: (0, 0))
    kinds = [jnp.float32, jnp.bfloat16] if len(values) > 1 else [jnp.bfloat16]
    return pl.pallas_call(
        functools.partial(norm_kernel, len(values)),
        grid=(rows // ROWS,),
        in_specs=[row_block(width)] * len(values) + [whole],
        out_specs=[row_block(width)] * len(kinds),
        out_shape=[jax.ShapeDtypeStruct((rows, width), kind) for kind in kinds],
        compiler_params=pltpu.CompilerParams(vmem_limit_bytes=24 * 1024 * 1024),
        cost_estimate=CHEAP,
    )(*values, gain[None])


def norm_back(value, own, other, gain, kinds, extra=None):
    rows, width = value.shape
    whole = pl.BlockSpec((1, width), lambda i: (0, 0))
    more = [] if extra is None else [extra]
    return pl.pallas_call(
        functools.partial(norm_back_kernel, (extra is not None,)),
        grid=(rows // ROWS,),
        in_specs=[row_block(width)] * 3 + [whole] + [row_block(width)] * len(more),
        out_specs=[whole] + [row_block(width)] * len(kinds),
        out_shape=[jax.ShapeDtypeStruct((1, width), jnp.float32)]
        + [jax.ShapeDtypeStruct((rows, width), kind) for kind in kinds],
        compiler_params=pltpu.CompilerParams(vmem_limit_bytes=24 * 1024 * 1024),
        cost_estimate=CHEAP,
    )(value, own, other, gain[None], *more)


def gate_kernel(hidden_ref, own_ref, other_ref, gate_ref, cot_ref, result_ref, gating_ref, low_ref):
    result = wide_sum((hidden_ref, own_ref, other_ref))
    result_ref[...] = result
    total = jnp.sum(result * gate_ref[...].astype(jnp.float32), axis=-1, keepdims=True)
    gating = jax.nn.sigmoid(total)
    gating_ref[...] = jnp.broadcast_to(gating, gating_ref.shape)
    low_ref[...] = (cot_ref[...].astype(jnp.float32) * gating).astype(low_ref.dtype)


def gate(hidden, own, other, vector, cot):
    rows, width = hidden.shape
    return pl.pallas_call(
        gate_kernel,
        out_shape=[
            jax.ShapeDtypeStruct((rows, width), jnp.float32),
            jax.ShapeDtypeStruct((rows, LANES), jnp.float32),
            jax.ShapeDtypeStruct(cot.shape, jnp.bfloat16),
        ],
        compiler_params=pltpu.CompilerParams(vmem_limit_bytes=24 * 1024 * 1024),
        cost_estimate=CHEAP,
    )(hidden, own, other, vector[None], cot)


def rotated(start):
    return tuple(RINGS[(start + i) % len(RINGS)] for i in range(len(RINGS)))


def xor_swap(values, mask):
    count = lax.axis_size("dp")
    return lax.ppermute(values, "dp", [(i, i ^ mask) for i in range(count)])


def chip_offset(place, order, low_first):
    offset = 0
    for k, mask in enumerate(order):
        bit = k if low_first else len(order) - 1 - k
        offset = offset ^ (((place >> bit) & 1) * (mask >> 1))
    return offset


def together(values):
    return list(lax.optimization_barrier(tuple(values)))


def after(value, *others):
    return lax.optimization_barrier((value,) + others)[0]


def gathered_parts(blocks, orders, early, work):
    held = [block[None] for block in blocks]
    count, last = len(blocks), len(RINGS) - 1
    for step in range(last):
        other = [xor_swap(part, order[step]) for part, order in zip(held, orders)]
        held = [jnp.concatenate([a, b], axis=0) for a, b in zip(held, other)]
        done = together(held + (early if step == last - 1 else []))
        held = done[:count]
    other = [xor_swap(part, order[last]) for part, order in zip(held, orders)]
    done = together(other + work(*done[count:]))
    return held, done[:count], done[count:]


def split_sum(kept, other):
    half = kept.shape[0] // 2
    if half == 0:
        return kept.astype(jnp.float32) + other.astype(jnp.float32), None
    return kept[:half] + other[:half], kept[half:] + other[half:]


class Scatter:
    def __init__(self, kept, given, orders):
        self.kept, self.given, self.orders = list(kept), list(given), orders
        self.step = 0

    def advance(self, *tied):
        other = [
            xor_swap(part, order[self.step]) for part, order in zip(self.given, self.orders)
        ]
        done = together(other + list(tied))
        sums = [split_sum(own, got) for own, got in zip(self.kept, done)]
        self.kept, self.given = [low for low, _ in sums], [high for _, high in sums]
        self.step += 1
        return done[len(other) :]

    def result(self):
        return [part[0] for part in self.kept]


def route_kernel(moves, steps, n_in, n_out, place, *refs):
    ins, outs = refs[:n_in], refs[n_in : n_in + n_out]
    held = refs[n_in + n_out : n_in + 2 * n_out]
    sems = refs[n_in + 2 * n_out]
    device = place[0]
    chip, core = device >> 1, device & 1

    for target in range(n_out):

        def step(index, carry):
            for source, take, goal, put, source_box, target_box in moves:
                if goal == target:
                    pltpu.make_async_copy(
                        ins[source].at[(take(chip, core, index),) + source_box],
                        held[goal].at[(put(chip, core, index),) + target_box],
                        sems.at[goal],
                    ).start()
            return carry

        lax.fori_loop(0, steps, step, 0)
    for target in range(n_out):
        pltpu.make_async_copy(held[target], held[target], sems.at[target]).wait()
        pltpu.make_async_copy(held[target], outs[target], sems.at[target]).start()
    for target in range(n_out):
        pltpu.make_async_copy(held[target], outs[target], sems.at[target]).wait()


def route(moves, steps, place, arrays, shapes):
    anywhere = pl.BlockSpec(memory_space=pl.ANY)
    volume = sum(2 * a.size for a in arrays)
    return pl.pallas_call(
        functools.partial(route_kernel, moves, steps, len(arrays), len(shapes)),
        in_specs=[SCALARS] + [anywhere] * len(arrays),
        out_specs=[anywhere] * len(shapes),
        out_shape=[jax.ShapeDtypeStruct(s, jnp.bfloat16) for s in shapes],
        scratch_shapes=[pltpu.VMEM(s, jnp.bfloat16) for s in shapes]
        + [pltpu.SemaphoreType.DMA((len(shapes),))],
        compiler_params=pltpu.CompilerParams(vmem_limit_bytes=volume + volume // 4 + (4 << 20)),
        cost_estimate=CHEAP,
    )(place, *arrays)


def box(rows, cols):
    return (pl.ds(rows[0], rows[1] - rows[0]), pl.ds(cols[0], cols[1] - cols[0]))


def overlap(first, second):
    low, high = max(first[0], second[0]), min(first[1], second[1])
    return (low, high) if low < high else None


def shifted_span(span, base):
    return (span[0] - base, span[1] - base)


def core_swap(values):
    return xor_swap(values, CORE)


def model_swap(values):
    return lax.ppermute(values, "mp", [(0, 1), (1, 0)])


def exchange(values):
    low = values.astype(jnp.bfloat16)
    other = model_swap(low)
    return low.astype(jnp.float32) + other.astype(jnp.float32)


def halo_rows(block, width):
    count = lax.axis_size("dp")
    forward = [(i, (i + 1) % count) for i in range(count)]
    backward = [((i + 1) % count, i) for i in range(count)]
    low = lax.ppermute(block[block.shape[0] - width :], "dp", forward)
    high = lax.ppermute(block[:width], "dp", backward)
    return low, high


def gelu_pair(values):
    below = 0.5 * (1.0 + lax.erf(values * 0.5**0.5))
    slope = below + values * (jnp.exp(-0.5 * values * values) * (2.0 * jnp.pi) ** -0.5)
    return (values * below).astype(jnp.bfloat16), slope.astype(jnp.bfloat16)


def matmul(former, latter):
    return jnp.dot(former, latter, preferred_element_type=jnp.float32)


def matmul_nt(former, latter):
    return lax.dot_general(
        former, latter, (((1,), (1,)), ((), ())), preferred_element_type=jnp.float32
    )


def matmul_tn(former, latter):
    return lax.dot_general(
        former, latter, (((0,), (0,)), ((), ())), preferred_element_type=jnp.float32
    )


def pair_swap(values):
    chips = lax.axis_size("dp") // 2
    pairs = []
    for chip in range(chips):
        other = (chip + 1) % chips if chip % 2 else (chip - 1) % chips
        pairs += [(2 * chip + core, 2 * other + core) for core in range(2)]
    return lax.ppermute(values, "dp", pairs)


def own_half(first, core, axis, other=False):
    size = first.shape[axis] // 2
    low = lax.slice_in_dim(first, 0, size, axis=axis)
    high = lax.slice_in_dim(first, size, 2 * size, axis=axis)
    return jnp.where((core == 0) != other, low, high)


def in_core_order(own, other, core, axis):
    return jnp.where(
        core == 0,
        jnp.concatenate([own, other], axis=axis),
        jnp.concatenate([other, own], axis=axis),
    )


def row_places(device, order, depth):
    chip, core = device >> 1, device & 1
    place = jnp.arange(2 * CHIPS * depth)
    block, line = place // depth, place % depth
    owner = 2 * (chip ^ chip_offset(block % CHIPS, order, True)) + (core ^ (block // CHIPS))
    return owner * depth + line


def row_picker(device, order, depth):
    places = row_places(device, order, depth)
    rows = lax.broadcasted_iota(jnp.int32, (places.shape[0], places.shape[0]), 0)
    return (rows == places[None, :]).astype(jnp.bfloat16)


def all_weights(place, core, small_rows, common_rows, *ties):
    middle = small_rows[4].shape[1] // 2
    first = jnp.concatenate(small_rows[:4] + (small_rows[4][:, :middle],), axis=1)
    second = jnp.concatenate([small_rows[4][:, middle:], small_rows[5]], axis=1)
    kept = jnp.concatenate([own_half(rows, core, 1) for rows in common_rows], axis=1)
    given = jnp.concatenate([own_half(rows, core, 1, True) for rows in common_rows], axis=1)
    common = in_core_order(kept, core_swap(given), core, 0)
    rows = common.shape[0]
    widths = [block.shape[1] // 2 for block in common_rows]
    spans = even_edges(common.shape[1], 3)
    orders = [rotated(i) for i in range(5)]
    held, other, extra = gathered_parts(
        [first, second] + [common[:, low:high] for low, high in spans], orders, *ties
    )
    near = [jnp.concatenate([a, b], axis=0) for a, b in zip(held[:2], other[:2])]
    far = [core_swap(part) for part in near]
    small = [
        tuple(part.reshape(-1, part.shape[2]) for part in pair) for pair in zip(near, far)
    ]
    starts = [0]
    for width in widths:
        starts.append(starts[-1] + width)
    moves = []
    half = CHIPS // 2
    for i, span in enumerate(spans):
        order = orders[i + 2]
        for target in range(len(widths)):
            cols_span = (starts[target], starts[target + 1])
            shared = overlap(cols_span, span)
            if shared is None:
                continue
            for side in range(2):

                def put(chip, core, index, side=side, order=order):
                    return chip ^ chip_offset(index + side * half, order, True)

                moves.append(
                    (
                        2 * i + side,
                        lambda chip, core, index: index,
                        target,
                        put,
                        box((0, rows), shifted_span(shared, span[0])),
                        box((0, rows), shifted_span(shared, cols_span[0])),
                    )
                )
    arrays = [part for pair in zip(held[2:], other[2:]) for part in pair]
    large = route(moves, half, place, arrays, [(CHIPS, rows, width) for width in widths])
    expand, shrink, adapter = [part.reshape(CHIPS * rows, part.shape[2]) for part in large]
    adapter = in_core_order(adapter, core_swap(adapter), core, 1)
    return small, expand, shrink, adapter, extra


def even_edges(width, count):
    tiles = width // LANES
    edges = [LANES * ((tiles * i + count - 1) // count) for i in range(count + 1)]
    return [(edges[i], edges[i + 1]) for i in range(count)]


def turn(left_refs, turned):
    first = 0
    for left_ref in left_refs:
        rows = left_ref.shape[0]
        for start in range(0, left_ref.shape[1], LANES):
            lanes = slice(start, start + LANES)
            turned[lanes, first : first + rows] = left_ref[:, lanes].T
        first += rows


def slope_pack_kernel(order, lefts, place, *refs):
    left_refs, right_ref = refs[:lefts], refs[lefts]
    extra_ref = refs[lefts + 1] if len(refs) > lefts + 6 else None
    near_ref, far_ref, turned, tile, sems = refs[-5:]
    width = right_ref.shape[1]
    step = pl.program_id(0)
    full = turned.shape[0] // width
    total = full + (extra_ref is not None)
    blocks, rows = tile.shape[1], tile.shape[2]
    group = blocks // 4
    chip = place[0] >> 1
    slot = step % 2

    def sent(which, wide):
        box_ref = tile.at[which, :, :, pl.ds(0, wide)]
        return pltpu.make_async_copy(box_ref, box_ref, sems.at[which])

    @pl.when(step >= 2)
    def _():
        sent(slot, width).wait()

    @pl.when(step == 0)
    def _():
        turn(left_refs, turned)

    @pl.when(step < full)
    def _():
        for part in range(4):
            lines = slice(part * group * rows, (part + 1) * group * rows)
            value = jnp.dot(turned[lines, :], right_ref[...], preferred_element_type=jnp.float32)
            tile[slot, part * group : (part + 1) * group] = value.astype(tile.dtype).reshape(
                group, rows, width
            )

    last = width
    if extra_ref is not None:
        last = extra_ref.shape[2]

        @pl.when(step == full)
        def _():
            tile[slot, :, :, 0:last] = extra_ref[...]

    for index in range(total):
        wide = width if index < full else last
        cols = pl.ds(index * width, wide)

        @pl.when(step == index)
        def _(cols=cols, wide=wide):
            def send(spot, carry):
                for side, out in enumerate((near_ref, far_ref)):
                    owner = chip ^ chip_offset(spot + side * (blocks // 2), order, True)
                    pltpu.make_async_copy(
                        tile.at[slot, owner, :, pl.ds(0, wide)],
                        out.at[spot, :, cols],
                        sems.at[slot],
                    ).start()
                return carry

            lax.fori_loop(0, blocks // 2, send, 0)

    @pl.when(step == total - 1)
    def _():
        sent(1 - slot, width).wait()
        sent(slot, last).wait()


def packed_slopes(place, order, lefts, right, extra=None):
    channels = lefts[0].shape[1]
    depth, hidden = right.shape
    width = 384
    steps = hidden // width
    rows = channels // CHIPS
    total, more, specs = hidden, [], []
    if extra is not None:
        total += extra.shape[1]
        more = [extra.reshape(CHIPS, rows, extra.shape[1])]
        specs = [
            pl.BlockSpec(more[0].shape, lambda i: (0, 0, 0), pipeline_mode=pl.Buffered(1))
        ]
    shape = jax.ShapeDtypeStruct((CHIPS // 2, rows, total), jnp.bfloat16)
    return pl.pallas_call(
        functools.partial(slope_pack_kernel, order, len(lefts)),
        grid=(steps + len(more),),
        in_specs=[SCALARS]
        + [
            pl.BlockSpec(left.shape, lambda i: (0, 0), pipeline_mode=pl.Buffered(1))
            for left in lefts
        ]
        + [pl.BlockSpec((depth, width), lambda i: (0, jnp.minimum(i, steps - 1)))]
        + specs,
        out_specs=[pl.BlockSpec(memory_space=pl.ANY)] * 2,
        out_shape=[shape, shape],
        scratch_shapes=[
            pltpu.VMEM((channels, depth), jnp.bfloat16),
            pltpu.VMEM((2, CHIPS, rows, width), jnp.bfloat16),
            pltpu.SemaphoreType.DMA((2,)),
        ],
        compiler_params=pltpu.CompilerParams(vmem_limit_bytes=32 * 1024 * 1024),
        cost_estimate=pl.CostEstimate(flops=0, bytes_accessed=1 << 20, transcendentals=0),
    )(place, *lefts, right, *more)


def unpacked_map_slopes(core, blocks, widths):
    block = jnp.concatenate(blocks, axis=1)
    own = own_half(block, core, 0)
    got = core_swap(own_half(block, core, 0, True).astype(jnp.bfloat16)).astype(jnp.float32)
    outs = []
    start = 0
    for width in widths:
        outs.append(
            in_core_order(own[:, start : start + width], got[:, start : start + width], core, 1)
        )
        start += width
    return outs


def row_sums(values):
    count = values.shape[0]
    pieces = lax.all_to_all(values, "dp", 0, 0, tiled=True)
    return jnp.sum(pieces.astype(jnp.float32), axis=0)


def row_copies(row):
    count = lax.axis_size("dp")
    return lax.all_to_all(jnp.broadcast_to(row[None], (count,) + row.shape), "dp", 0, 0, tiled=True)


def on_device(
    lowres_in,
    highres_in,
    image_sizes,
    attn_gain,
    query_weight,
    key_weight,
    value_weight,
    output_weight,
    mlp_gain,
    up_weight,
    down_weight,
    depth_kernel,
    conv_gain,
    expand_weight,
    shrink_weight,
    layer_scale,
    adapter_weight,
    adapter_kernel,
    gate_vector,
    out_cotangent,
    map_cotangent,
):
    device = lax.axis_index("dp")
    core = device & 1
    place = device.reshape(1).astype(jnp.int32)
    group_count = lax.axis_size("dp") // TILES
    position = (device + 2) % TILES
    group_id = (device + 2) // TILES % group_count
    model_half = lax.axis_index("mp")
    low_strip, _, grid_side, width = lowres_in.shape
    high_strip, _, high_side, channels = highres_in.shape
    own_width = adapter_kernel.shape[1]
    local_width = query_weight.shape[1]
    local_heads = local_width // HD
    scaling = HD ** (-0.5)
    token_count = low_strip * grid_side
    pixel_count = high_strip * high_side

    high_map = highres_in.reshape(high_strip, high_side, channels)
    table_ids = jnp.arange(image_sizes.shape[0])
    extent = jnp.sum(jnp.where(table_ids == group_id, image_sizes, 0))
    first_row = position * high_strip
    map_place = jnp.stack([first_row, extent]).astype(jnp.int32)
    token_low = lowres_in.reshape(token_count, width)
    local_grad_low = out_cotangent.reshape(low_strip, grid_side, own_width)
    backs = []
    depth = query_weight.shape[0]
    pickers = [row_picker(device, rotated(i), depth) for i in range(2)]

    def convolve(map_low, map_high):
        convolved = map_conv(map_place, high_map, map_low, map_high, depth_kernel)
        convolved = convolved.reshape(pixel_count, channels)
        (normed_low,) = norm([token_low], attn_gain)
        normed_first = matmul(normed_low, pickers[0]).astype(jnp.bfloat16)
        backs.extend([map_low, map_high, convolved])
        return [*norm([convolved], conv_gain), normed_low, normed_first]

    small, expand_full, shrink_full, adapter_full, extra = all_weights(
        place,
        core,
        (query_weight, key_weight, value_weight, output_weight.T, up_weight, down_weight.T),
        (expand_weight, shrink_weight.T, adapter_weight),
        list(halo_rows(high_map, RADIUS)),
        convolve,
    )
    map_low, map_high, convolved = backs
    normed_map_low, normed_low, normed_first = extra
    normed_map_given_low = core_swap(normed_map_low)
    normed_map_pair = jnp.concatenate([normed_map_low, normed_map_given_low], axis=0)
    triple = 3 * local_width
    quad = 4 * local_width
    hidden_width = up_weight.shape[1]
    hidden_half = hidden_width // 2

    def pieces(index, low, high):
        return [part[:, low:high] for part in small[index]]

    qkv_parts = pieces(0, 0, triple)
    output_parts = pieces(0, triple, quad)
    up_parts = [pieces(0, quad, quad + hidden_half), pieces(1, 0, hidden_half)]
    down_parts = pieces(1, hidden_half, hidden_half + hidden_width)

    def picked(values, index):
        return matmul(values, pickers[index]).astype(jnp.bfloat16)

    def restored(values, index):
        return matmul_nt(values.astype(jnp.bfloat16), pickers[index])

    def into(values, parts):
        half = values.shape[1] // 2
        return matmul(values[:, :half], parts[0]) + matmul(values[:, half:], parts[1])

    def outof(values, parts):
        return jnp.concatenate([matmul_nt(values, part) for part in parts], axis=1)

    qkv_rows = into(normed_first, qkv_parts).astype(jnp.bfloat16)
    pair = qkv_rows[:, local_width:]
    pair_other, expand_full, shrink_full = together([pair_swap(pair), expand_full, shrink_full])
    pair = jnp.concatenate([pair, pair_other], axis=0)
    pair = jnp.concatenate([pair, core_swap(pair)], axis=0)
    attended_low = attend(qkv_rows, pair)
    hidden_own = restored(outof(attended_low, output_parts), 0).astype(jnp.bfloat16)
    hidden_rows, normed_two_low = norm([token_low, hidden_own, model_swap(hidden_own)], mlp_gain)
    normed_two_picked = [picked(normed_two_low, i) for i in range(2)]
    expanded = jnp.concatenate(
        [into(normed_two_picked[i], up_parts[i]) for i in range(2)], axis=1
    )
    activated_low, activated_slope = gelu_pair(expanded)
    result_own = restored(outof(activated_low, down_parts), 1).astype(jnp.bfloat16)
    result_rows, gating, lifted_grad_low = gate(
        hidden_rows,
        result_own,
        model_swap(result_own),
        gate_vector,
        local_grad_low.reshape(token_count, own_width),
    )

    result_grid = result_rows.reshape(low_strip, grid_side, width)
    gate_wide = gate_vector.astype(jnp.float32)
    gating = gating[:, :1].reshape(low_strip, grid_side, 1)
    out_grad = local_grad_low.astype(jnp.float32)
    grid_shape = (low_strip, grid_side, channels)
    pooled_own = matmul_nt(lifted_grad_low, adapter_full).astype(jnp.bfloat16).reshape(grid_shape)
    pooled_other = model_swap(pooled_own)

    widened = matmul(normed_map_pair, expand_full)
    widened_low, widened_slope = gelu_pair(widened)
    widened_low = after(widened_low, pooled_own)
    narrowed_part, narrowed_given = dense([widened_low], shrink_full, True, halves=True)
    narrowed_part = narrowed_part + core_swap(narrowed_given).astype(jnp.float32)
    map_shape = (high_strip, high_side, channels)
    narrowed_own = narrowed_part.astype(jnp.bfloat16).reshape(map_shape)
    narrowed_own, pooled_other = together([narrowed_own, pooled_other])
    narrowed_other = model_swap(narrowed_own)

    map_grad, narrowed_grad_low = spread_map(
        map_place, pooled_own, pooled_other, map_cotangent.reshape(map_shape), layer_scale[None]
    )
    narrowed_grad_low = narrowed_grad_low.reshape(pixel_count, channels)
    narrowed_grad_pair = [narrowed_grad_low, core_swap(narrowed_grad_low)]
    (widened_grad_low,) = dense(narrowed_grad_pair, shrink_full, False, widened_slope)
    normed_map_part, normed_map_given = dense([widened_grad_low], expand_full, True, halves=True)
    normed_map_given, narrowed_other = together([normed_map_given, narrowed_other])
    normed_map_part = normed_map_part + core_swap(normed_map_given).astype(jnp.float32)
    normed_map_own = normed_map_part.astype(jnp.bfloat16)

    mapped, pooled_low, layer_scale_slope = blend_map(
        map_place, narrowed_own, narrowed_other, high_map, layer_scale[None], map_grad
    )
    pooled_low = pooled_low.reshape(token_count, channels)
    lifted = matmul(pooled_low, adapter_full).reshape(low_strip, grid_side, own_width)

    own_result = lax.dynamic_slice_in_dim(result_grid, model_half * own_width, own_width, 2)
    own_result_low = own_result.astype(jnp.bfloat16)
    both_low = jnp.concatenate([own_result_low, local_grad_low], axis=2)
    both_edges = halo_rows(after(both_low, widened_grad_low), 1)
    mix_place = jnp.stack([position * low_strip, TILES * low_strip]).astype(jnp.int32)
    local_mix, local_back, adapter_kernel_slope = mix(
        mix_place, both_low, *both_edges, adapter_kernel
    )
    blended = own_result + local_mix + gating * lifted

    gate_part = jnp.sum(out_grad * lifted, axis=-1, keepdims=True)
    gate_grad = exchange(gate_part)
    adapter_slope = matmul_tn(pooled_low, lifted_grad_low)
    adapter_slope = own_half(adapter_slope, core, 1) + core_swap(
        own_half(adapter_slope, core, 1, True).astype(jnp.bfloat16)
    ).astype(jnp.float32)
    own_grad = out_grad + local_back
    own_grad_low = own_grad.astype(jnp.bfloat16)
    other_grad = model_swap(own_grad_low)
    result_grad = in_core_order(own_grad_low, other_grad, model_half, 2).astype(jnp.float32)
    gate_slope = gate_grad * gating * (1.0 - gating)
    gate_vector_slope = jnp.sum((gate_slope * result_grid).reshape(token_count, width), axis=0)
    result_grad = (result_grad + gate_slope * gate_wide).reshape(token_count, width)

    result_low = after(result_grad.astype(jnp.bfloat16), widened_grad_low)
    result_picked = picked(result_low, 1)
    activated_grad = into(result_picked, down_parts)
    expanded_grad_low = (activated_grad * activated_slope.astype(jnp.float32)).astype(jnp.bfloat16)
    expanded_grad_parts = [expanded_grad_low[:, :hidden_half], expanded_grad_low[:, hidden_half:]]
    second_slopes = split_rows(
        paired_slopes(
            (normed_two_picked[1], result_picked), (expanded_grad_parts[1], activated_low)
        )
    )
    normed_two_own = sum(
        restored(outof(expanded_grad_parts[i], up_parts[i]), i) for i in range(2)
    ).astype(jnp.bfloat16)
    normed_two_other = model_swap(normed_two_own)
    normed_two_other, normed_map_own, *second_slopes = together(
        [normed_two_other, normed_map_own, *second_slopes]
    )
    second_far = core_swap(second_slopes[1])
    normed_map_other = model_swap(normed_map_own)
    mlp_gain_slope, hidden_grad, hidden_low = norm_back(
        hidden_rows,
        normed_two_own,
        normed_two_other,
        mlp_gain,
        (jnp.float32, jnp.bfloat16),
        result_grad,
    )
    hidden_picked = picked(hidden_low, 0)
    attended_grad_low = into(hidden_picked, output_parts).astype(jnp.bfloat16)
    query_grad_rows, key_grad_all, value_grad_all = attend_back(qkv_rows, pair, attended_grad_low)
    pair_back = jnp.concatenate(
        [key_grad_all, value_grad_all], axis=1
    )
    pair_back = pair_back[: 2 * token_count] + core_swap(
        pair_back[2 * token_count :].astype(jnp.bfloat16)
    ).astype(jnp.float32)
    pair_given, late_place = together([pair_back[token_count:].astype(jnp.bfloat16), place])
    pair_other = pair_swap(pair_given)
    shrink_packed = packed_slopes(late_place, rotated(3), narrowed_grad_pair, widened_low)
    expand_packed = packed_slopes(
        late_place,
        rotated(2),
        [normed_map_low, normed_map_given_low],
        widened_grad_low,
        adapter_slope.astype(jnp.bfloat16),
    )
    map_slopes_packed = [*expand_packed, *shrink_packed]
    second_near = split_sum(second_slopes[0], second_far)
    pair_other, normed_map_other, *rest = together(
        [pair_other, normed_map_other, *second_near, *map_slopes_packed]
    )
    second_near, map_slopes_packed = rest[:2], rest[2:]
    pair_back = pair_back[:token_count] + pair_other.astype(jnp.float32)
    qkv_grad = jnp.concatenate([query_grad_rows, pair_back.astype(jnp.bfloat16)], axis=1)
    normed_own = restored(outof(qkv_grad, qkv_parts), 0).astype(jnp.bfloat16)
    normed_other = model_swap(normed_own)
    first_slopes = split_rows(
        paired_slopes(
            (normed_first, hidden_picked, normed_two_picked[0]),
            (qkv_grad, attended_low, expanded_grad_parts[0]),
        )
    )
    first_far = core_swap(first_slopes[1])
    conv_gain_slope, convolved_grad_low = norm_back(
        convolved, normed_map_own, normed_map_other, conv_gain, (jnp.bfloat16,)
    )
    convolved_grad_low = convolved_grad_low.reshape(map_shape)
    grad_low, grad_high = halo_rows(convolved_grad_low, RADIUS)
    grad_low, grad_high, *map_slopes_packed = together(
        [grad_low, grad_high, *map_slopes_packed]
    )
    near = [split_sum(first_slopes[0], first_far), second_near]
    scatter = Scatter(
        [low for low, _ in near] + list(map_slopes_packed[0::2]),
        [high for _, high in near] + list(map_slopes_packed[1::2]),
        [rotated(i)[::-1] for i in range(4)],
    )

    depth_kernel_slope = map_slopes(map_place, high_map, map_low, map_high, convolved_grad_low)
    highres_grad = map_conv(
        map_place, convolved_grad_low, grad_low, grad_high, depth_kernel, map_grad
    )
    attn_gain_slope, lowres_grad = norm_back(
        token_low, normed_own, normed_other, attn_gain, (jnp.float32,), hidden_grad
    )
    lowres_grad = lowres_grad.reshape(low_strip, 1, grid_side, width)

    def as_rows(values):
        return jnp.pad(values, ((0, 0), (0, channels - values.shape[1])))

    minor_rows = jnp.concatenate(
        [
            depth_kernel_slope,
            conv_gain_slope,
            layer_scale_slope,
            as_rows(
                jnp.concatenate([attn_gain_slope, mlp_gain_slope, gate_vector_slope[None]], axis=0)
            ),
            as_rows(adapter_kernel_slope),
        ],
        axis=0,
    )
    lines = channels // LANES
    block_rows = -(-lines // 16) * 16
    minor = jnp.pad(
        minor_rows.astype(jnp.bfloat16).reshape(minor_rows.shape[0], lines, LANES),
        ((0, 2 * CHIPS - minor_rows.shape[0]), (0, block_rows - lines), (0, 0)),
    )
    depth_kernel_slope, highres_grad = scatter.advance(depth_kernel_slope, highres_grad)
    minor_own = row_sums(minor).astype(jnp.bfloat16)
    (minor_own,) = scatter.advance(minor_own)
    minor_copies = row_copies(minor_own)
    (minor_copies,) = scatter.advance(minor_copies)
    minor_all = (
        minor_copies[:, :lines].reshape(2 * CHIPS, channels).astype(jnp.float32)
    )
    while scatter.step < len(RINGS):
        scatter.advance()
    first_own, second_own, *map_blocks = scatter.result()
    up_own = jnp.concatenate([first_own[:, quad:], second_own[:, :hidden_half]], axis=1)
    down_own = second_own[:, hidden_half:]
    expand_own, adapter_own, shrink_own = unpacked_map_slopes(
        core,
        map_blocks,
        (widened_low.shape[1], adapter_slope.shape[1], widened_low.shape[1]),
    )
    firsts = [first_own[:, i * local_width : (i + 1) * local_width] for i in range(4)]
    taps = depth_kernel.shape[0]
    side_taps = adapter_kernel.shape[0]
    return (
        blended.astype(jnp.bfloat16)[:, None],
        mapped[:, None],
        lowres_grad,
        highres_grad[:, None],
        minor_all[taps + 2, :width],
        firsts[0],
        firsts[1],
        firsts[2],
        firsts[3].T,
        minor_all[taps + 3, :width],
        up_own,
        down_own.T,
        minor_all[:taps],
        minor_all[taps],
        expand_own,
        shrink_own.T,
        minor_all[taps + 1],
        adapter_own,
        minor_all[taps + 5 : taps + 5 + side_taps, :own_width],
        minor_all[taps + 4, :width],
    )


def solution(mesh):
    in_specs = (
        P("dp", None, None, None),
        P("dp", None, None, None),
        P(),
        P(),
        P("dp", "mp"),
        P("dp", "mp"),
        P("dp", "mp"),
        P("mp", "dp"),
        P(),
        P("dp", "mp"),
        P("mp", "dp"),
        P(),
        P(),
        P("dp", "mp"),
        P("mp", "dp"),
        P(),
        P("dp", "mp"),
        P(None, "mp"),
        P(),
        P("dp", None, None, "mp"),
        P("dp", None, None, None),
    )
    out_specs = (
        P("dp", None, None, "mp"),
        P("dp", None, None, None),
        P("dp", None, None, None),
        P("dp", None, None, None),
        P(),
        P("dp", "mp"),
        P("dp", "mp"),
        P("dp", "mp"),
        P("mp", "dp"),
        P(),
        P("dp", "mp"),
        P("mp", "dp"),
        P(),
        P(),
        P("dp", "mp"),
        P("mp", "dp"),
        P(),
        P("dp", "mp"),
        P(None, "mp"),
        P(),
    )
    return jax.shard_map(
        on_device, mesh=mesh, in_specs=in_specs, out_specs=out_specs, check_vma=False
    )
```

```python
import functools

import jax
import jax.numpy as jnp
from jax import lax
from jax.experimental import pallas as pl
from jax.experimental.pallas import tpu as pltpu
from jax.sharding import PartitionSpec as P

HD = 64
TILES = 4
CHIPS = 32
CORE = 1
RINGS = (2, 6, 8, 24, 32)

norm_epsilon = 1e-06

LANES = 128
RADIUS = 3
WINDOW = 7
PAD = 8


def masked_rows(place, main_ref, low_ref, high_ref, wide, strip, side, bounded):
    first, extent = place[0], place[1]
    cols = lax.broadcasted_iota(jnp.int32, (side, LANES), 0)

    def put(slot, value):
        row = first + slot - RADIUS
        limit = extent if bounded else side
        keep = (cols < limit) & (row >= 0) & (row < limit)
        wide[slot] = jnp.where(keep, value.astype(jnp.float32), 0.0)

    for slot in range(RADIUS):
        put(slot, low_ref[slot])
        put(RADIUS + strip + slot, high_ref[slot])
    for slot in range(strip):
        put(RADIUS + slot, main_ref[slot])


def window_sum(wide, taps_ref, shifted, row, side, flipped):
    sums = [None] * WINDOW
    for a in range(WINDOW):
        line = wide[row + a]
        for b in range(WINDOW):
            tap = WINDOW * a + b
            if flipped:
                tap = WINDOW * WINDOW - 1 - tap
            term = line * taps_ref[tap : tap + 1]
            sums[b] = term if sums[b] is None else sums[b] + term
    total = sums[RADIUS]
    for b in range(WINDOW):
        if b != RADIUS:
            shifted[b, PAD : PAD + side] = sums[b]
    for b in range(WINDOW):
        if b != RADIUS:
            total = total + shifted[b, PAD + b - RADIUS : PAD + b - RADIUS + side]
    return total


def clear_edges(shifted, side):
    for b in range(WINDOW):
        shifted[b, 0:PAD] = jnp.zeros((PAD, LANES), jnp.float32)
        shifted[b, PAD + side : 2 * PAD + side] = jnp.zeros((PAD, LANES), jnp.float32)


def forward_kernel(place, main_ref, low_ref, high_ref, taps_in, out_ref, wide, taps, shifted):
    strip, side = main_ref.shape[0], main_ref.shape[1]
    masked_rows(place, main_ref, low_ref, high_ref, wide, strip, side, True)
    clear_edges(shifted, side)
    taps[...] = taps_in[...].astype(jnp.float32)

    def step(row, carry):
        out_ref[row] = window_sum(wide, taps, shifted, row, side, False)
        return carry

    lax.fori_loop(0, strip, step, 0)


def backward_kernel(place, main_ref, low_ref, high_ref, taps_in, add_ref, out_ref, wide, taps, shifted):
    strip, side = main_ref.shape[0], main_ref.shape[1]
    masked_rows(place, main_ref, low_ref, high_ref, wide, strip, side, False)
    clear_edges(shifted, side)
    taps[...] = taps_in[...].astype(jnp.float32)
    cols = lax.broadcasted_iota(jnp.int32, (side, LANES), 0)

    def step(row, carry):
        total = window_sum(wide, taps, shifted, row, side, True) + add_ref[row]
        keep = (cols < place[1]) & (place[0] + row < place[1])
        out_ref[row] = jnp.where(keep, total, 0.0)
        return carry

    lax.fori_loop(0, strip, step, 0)


def slope_kernel(place, main_ref, low_ref, high_ref, grad_ref, out_ref, wide, padded):
    strip, side = main_ref.shape[0], main_ref.shape[1]
    masked_rows(place, main_ref, low_ref, high_ref, wide, strip, side, True)
    edge = jnp.zeros((PAD, LANES), jnp.float32)
    for row in range(strip):
        padded[row, 0:PAD] = edge
        padded[row, PAD : PAD + side] = grad_ref[row].astype(jnp.float32)
        padded[row, PAD + side : 2 * PAD + side] = edge
    for group in ((0, 1, 2, 3), (4, 5, 6)):

        def step(row, sums):
            lines = [wide[row + a] for a in group]
            fresh = list(sums)
            for b in range(WINDOW):
                start = PAD + RADIUS - b
                part = padded[row, start : start + side]
                for i in range(len(group)):
                    term = (lines[i] * part).reshape(side // 8, 8, LANES)
                    fresh[i * WINDOW + b] = fresh[i * WINDOW + b] + jnp.sum(term, axis=0)
            return tuple(fresh)

        start = tuple(jnp.zeros((8, LANES), jnp.float32) for _ in range(len(group) * WINDOW))
        sums = lax.fori_loop(0, strip, step, start)
        for i, a in enumerate(group):
            for b in range(WINDOW):
                tap = a * WINDOW + b
                out_ref[tap : tap + 1] = jnp.sum(sums[i * WINDOW + b], axis=0, keepdims=True)


def block3(rows, side):
    return pl.BlockSpec((rows, side, LANES), lambda i: (0, 0, i))


SCALARS = pl.BlockSpec(memory_space=pltpu.SMEM)


def in_hbm(values):
    return [pltpu.with_memory_space_constraint(v, pltpu.MemorySpace.HBM) for v in values]


def map_conv(place, main, low, high, taps, added=None):
    strip, side, channels = main.shape
    count = taps.shape[0]
    tap_spec = pl.BlockSpec((count, LANES), lambda i: (0, i))
    specs = [SCALARS, block3(strip, side), block3(RADIUS, side), block3(RADIUS, side), tap_spec]
    args = [place, main, low, high, taps]
    if added is not None:
        specs.append(block3(strip, side))
        args.append(added)
        args[1:] = in_hbm(args[1:])
    work = strip * side * channels
    return pl.pallas_call(
        forward_kernel if added is None else backward_kernel,
        grid=(channels // LANES,),
        in_specs=specs,
        out_specs=block3(strip, side),
        out_shape=jax.ShapeDtypeStruct((strip, side, channels), jnp.float32),
        scratch_shapes=[
            pltpu.VMEM((strip + 2 * RADIUS, side, LANES), jnp.float32),
            pltpu.VMEM((count, LANES), jnp.float32),
            pltpu.VMEM((WINDOW, side + 2 * PAD, LANES), jnp.float32),
        ],
        compiler_params=pltpu.CompilerParams(vmem_limit_bytes=24 * 1024 * 1024),
        cost_estimate=pl.CostEstimate(flops=0, bytes_accessed=work // 8, transcendentals=0),
    )(*args)


def map_slopes(place, main, low, high, grad):
    strip, side, channels = main.shape
    count = WINDOW * WINDOW
    work = strip * side * channels
    return pl.pallas_call(
        slope_kernel,
        grid=(channels // LANES,),
        in_specs=[SCALARS, block3(strip, side), block3(RADIUS, side), block3(RADIUS, side), block3(strip, side)],
        out_specs=pl.BlockSpec((count, LANES), lambda i: (0, i)),
        out_shape=jax.ShapeDtypeStruct((count, channels), jnp.float32),
        scratch_shapes=[
            pltpu.VMEM((strip + 2 * RADIUS, side, LANES), jnp.float32),
            pltpu.VMEM((strip, side + 2 * PAD, LANES), jnp.float32),
        ],
        compiler_params=pltpu.CompilerParams(vmem_limit_bytes=24 * 1024 * 1024),
        cost_estimate=pl.CostEstimate(flops=0, bytes_accessed=work // 8, transcendentals=0),
    )(place, *in_hbm([main, low, high, grad]))


WIDE = 384


def inside(place, row, side):
    cols = lax.broadcasted_iota(jnp.int32, (side, LANES), 0)
    return (cols < place[1]) & (place[0] + row < place[1])


def blend_kernel(
    place, own_ref, other_ref, map_ref, scale_ref, grad_ref, out_ref, pool_ref, slope_ref, line
):
    strip, side = map_ref.shape[0], map_ref.shape[1]
    half = side // 2
    for part in range(map_ref.shape[2] // LANES):
        lanes = slice(part * LANES, (part + 1) * LANES)
        scale = scale_ref[:, lanes].astype(jnp.float32)

        def step(pair, slope):
            total = None
            for i in range(2):
                row = 2 * pair + i
                narrow = own_ref[row, :, lanes].astype(jnp.float32) + other_ref[
                    row, :, lanes
                ].astype(jnp.float32)
                value = map_ref[row, :, lanes].astype(jnp.float32) + scale * narrow
                value = jnp.where(inside(place, row, side), value, 0.0)
                out_ref[row, :, lanes] = value.astype(out_ref.dtype)
                total = value if total is None else total + value
                product = grad_ref[row, :, lanes] * narrow
                slope = slope + jnp.sum(product.reshape(side // 8, 8, LANES), axis=0)
            line[...] = total
            pooled = line[pl.ds(0, half, 2), :] + line[pl.ds(1, half, 2), :]
            pool_ref[pair, :, lanes] = (pooled * 0.25).astype(pool_ref.dtype)
            return slope

        slope = lax.fori_loop(0, strip // 2, step, jnp.zeros((8, LANES), jnp.float32))
        slope_ref[:, lanes] = jnp.sum(slope, axis=0, keepdims=True)


def spread_kernel(place, pool_ref, pool_other_ref, cot_ref, scale_ref, grad_ref, low_ref, line):
    strip, side = cot_ref.shape[0], cot_ref.shape[1]
    half = side // 2
    for part in range(cot_ref.shape[2] // LANES):
        lanes = slice(part * LANES, (part + 1) * LANES)
        scale = scale_ref[:, lanes].astype(jnp.float32)

        def step(pair, carry):
            pooled = pool_ref[pair, :, lanes].astype(jnp.float32) + pool_other_ref[
                pair, :, lanes
            ].astype(jnp.float32)
            pooled = pooled * 0.25
            line[pl.ds(0, half, 2), :] = pooled
            line[pl.ds(1, half, 2), :] = pooled
            spread = line[...]
            for i in range(2):
                row = 2 * pair + i
                value = cot_ref[row, :, lanes].astype(jnp.float32) + spread
                value = jnp.where(inside(place, row, side), value, 0.0)
                grad_ref[row, :, lanes] = value
                low_ref[row, :, lanes] = (value * scale).astype(low_ref.dtype)
            return carry

        lax.fori_loop(0, strip // 2, step, 0)


def wide_block(*lead):
    return pl.BlockSpec(lead + (WIDE,), lambda i: (0,) * len(lead) + (i,))


def blend_map(place, own, other, main, scale, grad):
    strip, side, channels = main.shape
    full = wide_block(strip, side)
    pool = (strip // 2, side // 2)
    return pl.pallas_call(
        blend_kernel,
        grid=(channels // WIDE,),
        in_specs=[SCALARS, full, full, full, wide_block(1), full],
        out_specs=[full, wide_block(*pool), wide_block(1)],
        out_shape=[
            jax.ShapeDtypeStruct(main.shape, jnp.bfloat16),
            jax.ShapeDtypeStruct(pool + (channels,), jnp.bfloat16),
            jax.ShapeDtypeStruct((1, channels), jnp.float32),
        ],
        scratch_shapes=[pltpu.VMEM((side, LANES), jnp.float32)],
        compiler_params=pltpu.CompilerParams(vmem_limit_bytes=24 * 1024 * 1024),
        cost_estimate=pl.CostEstimate(flops=0, bytes_accessed=1 << 20, transcendentals=0),
    )(place, own, other, main, scale, grad)


def spread_map(place, pool, pool_other, cot, scale):
    strip, side, channels = cot.shape
    full = wide_block(strip, side)
    pooled = wide_block(strip // 2, side // 2)
    return pl.pallas_call(
        spread_kernel,
        grid=(channels // WIDE,),
        in_specs=[SCALARS, pooled, pooled, full, wide_block(1)],
        out_specs=[full, full],
        out_shape=[
            jax.ShapeDtypeStruct(cot.shape, jnp.float32),
            jax.ShapeDtypeStruct(cot.shape, jnp.bfloat16),
        ],
        scratch_shapes=[pltpu.VMEM((side, LANES), jnp.float32)],
        compiler_params=pltpu.CompilerParams(vmem_limit_bytes=24 * 1024 * 1024),
        cost_estimate=pl.CostEstimate(flops=0, bytes_accessed=1 << 20, transcendentals=0),
    )(place, pool, pool_other, cot, scale)


def head_lanes(rows, head):
    lanes = lax.broadcasted_iota(jnp.int32, (rows, LANES), 1)
    return (lanes >= head * HD) & (lanes < (head + 1) * HD)


def nt(former, latter):
    return lax.dot_general(
        former, latter, (((1,), (1,)), ((), ())), preferred_element_type=jnp.float32
    )


def tn(former, latter):
    return lax.dot_general(
        former, latter, (((0,), (0,)), ((), ())), preferred_element_type=jnp.float32
    )


def softmax_rows(scores):
    top = jnp.max(scores, axis=-1, keepdims=True)
    raised = jnp.exp(scores - top)
    return raised * (1.0 / jnp.sum(raised, axis=-1, keepdims=True))


def attend_kernel(query_ref, key_ref, value_ref, out_ref):
    rows = query_ref.shape[0]
    query, key, value = query_ref[...], key_ref[...], value_ref[...]
    total = jnp.zeros((rows, LANES), jnp.float32)
    for head in range(LANES // HD):
        mine = head_lanes(rows, head)
        scores = nt(jnp.where(mine, query, jnp.zeros_like(query)), key) * HD ** (-0.5)
        weights = softmax_rows(scores).astype(jnp.bfloat16)
        part = jnp.dot(weights, value, preferred_element_type=jnp.float32)
        total = jnp.where(mine, part, total)
    out_ref[...] = total.astype(out_ref.dtype)


def attend_back_kernel(
    query_ref, key_ref, value_ref, grad_ref, query_out, key_out, value_out
):
    rows = query_ref.shape[0]
    query, key, value, grad = query_ref[...], key_ref[...], value_ref[...], grad_ref[...]
    none = jnp.zeros_like(query)
    query_grad = jnp.zeros((rows, LANES), jnp.float32)
    key_grad, value_grad = None, None
    for head in range(LANES // HD):
        mine = head_lanes(rows, head)
        query_own = jnp.where(mine, query, none)
        grad_own = jnp.where(mine, grad, none)
        weights = softmax_rows(nt(query_own, key) * HD ** (-0.5))
        weight_grad = nt(grad_own, value)
        row_dot = jnp.sum(weights * weight_grad, axis=-1, keepdims=True)
        score_grad = (weights * (weight_grad - row_dot)).astype(jnp.bfloat16)
        part = jnp.dot(score_grad, key, preferred_element_type=jnp.float32)
        query_grad = jnp.where(mine, part, query_grad)
        key_part = tn(score_grad, query_own)
        value_part = tn(weights.astype(jnp.bfloat16), grad_own)
        key_grad = key_part if key_grad is None else key_grad + key_part
        value_grad = value_part if value_grad is None else value_grad + value_part
    query_out[...] = (query_grad * HD ** (-0.5)).astype(query_out.dtype)
    key_out[...] = key_grad * HD ** (-0.5)
    value_out[...] = value_grad


def lane_block(rows, shift=0):
    return pl.BlockSpec((rows, LANES), lambda i: (0, i + shift))


def attend(rows, pair):
    count, keys = rows.shape[0], pair.shape[0]
    width = pair.shape[1] // 2
    steps = width // LANES
    work = 4 * count * keys * width
    return pl.pallas_call(
        attend_kernel,
        grid=(steps,),
        in_specs=[lane_block(count), lane_block(keys), lane_block(keys, steps)],
        out_specs=lane_block(count),
        out_shape=jax.ShapeDtypeStruct((count, width), jnp.bfloat16),
        compiler_params=pltpu.CompilerParams(vmem_limit_bytes=24 * 1024 * 1024),
        cost_estimate=pl.CostEstimate(flops=0, bytes_accessed=1 << 20, transcendentals=0),
    )(rows, pair, pair)


def attend_back(rows, pair, grad):
    count, keys = rows.shape[0], pair.shape[0]
    width = pair.shape[1] // 2
    steps = width // LANES
    work = 10 * count * keys * width
    return pl.pallas_call(
        attend_back_kernel,
        grid=(steps,),
        in_specs=[
            lane_block(count),
            lane_block(keys),
            lane_block(keys, steps),
            lane_block(count),
        ],
        out_specs=[lane_block(count), lane_block(keys), lane_block(keys)],
        out_shape=[
            jax.ShapeDtypeStruct((count, width), jnp.bfloat16),
            jax.ShapeDtypeStruct((keys, width), jnp.float32),
            jax.ShapeDtypeStruct((keys, width), jnp.float32),
        ],
        compiler_params=pltpu.CompilerParams(vmem_limit_bytes=24 * 1024 * 1024),
        cost_estimate=pl.CostEstimate(flops=0, bytes_accessed=1 << 20, transcendentals=0),
    )(rows, pair, pair, grad)


def slopes_kernel(ends, *refs):
    count = len(ends)
    lefts, rights = refs[:count], refs[count : 2 * count]
    near_ref, far_ref = refs[2 * count :]
    half = near_ref.shape[0]
    step = pl.program_id(0)
    first = 0
    for left, right, end in zip(lefts, rights, ends):

        @pl.when((step >= first) & (step < end))
        def _(left=left, right=right):
            near_ref[...] = tn(left[:, :half], right[...]).astype(near_ref.dtype)
            far_ref[...] = tn(left[:, half:], right[...]).astype(far_ref.dtype)

        first = end


def paired_slopes(lefts, rights):
    tile = 512
    rows, depth = lefts[0].shape
    half = depth // 2
    starts, ends = [], []
    total = 0
    for right in rights:
        starts.append(total)
        total += right.shape[1] // tile
        ends.append(total)

    def column(start, end):
        return lambda i: (0, jnp.clip(i - start, 0, end - start - 1))

    whole = pl.BlockSpec((rows, depth), lambda i: (0, 0))
    out = pl.BlockSpec((half, tile), lambda i: (0, i))
    shape = jax.ShapeDtypeStruct((half, total * tile), jnp.bfloat16)
    near, far = pl.pallas_call(
        functools.partial(slopes_kernel, tuple(ends)),
        grid=(total,),
        in_specs=[whole] * len(lefts)
        + [pl.BlockSpec((rows, tile), column(a, b)) for a, b in zip(starts, ends)],
        out_specs=[out, out],
        out_shape=[shape, shape],
        compiler_params=pltpu.CompilerParams(vmem_limit_bytes=24 * 1024 * 1024),
        cost_estimate=pl.CostEstimate(
            flops=0,
            bytes_accessed=1 << 20,
            transcendentals=0,
        ),
    )(*lefts, *rights)
    return near, far


def split_rows(pair):
    return [part.reshape(CHIPS, part.shape[0] // CHIPS, part.shape[1]) for part in pair]


def dense_kernel(flipped, scaled, halves, lefts, *refs):
    left_refs, right_ref, refs = refs[:lefts], refs[lefts], refs[lefts + 1 :]
    scale_ref, outs = (refs[0], refs[1:]) if scaled else (None, refs)
    rows = sum(ref.shape[0] for ref in left_refs)
    chunk = rows // 6
    for part in range(6):
        lines = slice(part * chunk, (part + 1) * chunk)
        product = nt if flipped else functools.partial(jnp.dot, preferred_element_type=jnp.float32)
        left = left_refs[part * lefts // 6]
        start = part * chunk % left.shape[0]
        value = product(left[start : start + chunk, :], right_ref[...])
        if scaled:
            value = value * scale_ref[lines, :].astype(jnp.float32)
        if halves:
            out, first = (outs[0], 0) if part < 3 else (outs[1], rows // 2)
            out[part * chunk - first : (part + 1) * chunk - first, :] = value.astype(out.dtype)
        else:
            outs[0][lines, :] = value.astype(outs[0].dtype)


def dense(lefts, right, flipped, scale=None, halves=False):
    rows, depth = sum(left.shape[0] for left in lefts), lefts[0].shape[1]
    count = right.shape[0] if flipped else right.shape[1]
    tile = 512
    specs = [
        *(
            pl.BlockSpec(left.shape, lambda i: (0, 0), pipeline_mode=pl.Buffered(1))
            for left in lefts
        ),
        pl.BlockSpec((tile, depth), lambda i: (i, 0))
        if flipped
        else pl.BlockSpec((depth, tile), lambda i: (0, i)),
    ]
    args = [*lefts, right]
    if scale is not None:
        specs.append(pl.BlockSpec((rows, tile), lambda i: (0, i)))
        args.append(scale)
    if halves:
        kinds = [(rows // 2, jnp.float32), (rows // 2, jnp.bfloat16)]
    else:
        kinds = [(rows, jnp.bfloat16)]
    return pl.pallas_call(
        functools.partial(dense_kernel, flipped, scale is not None, halves, len(lefts)),
        grid=(count // tile,),
        in_specs=specs,
        out_specs=[pl.BlockSpec((size, tile), lambda i: (0, i)) for size, _ in kinds],
        out_shape=[jax.ShapeDtypeStruct((size, count), kind) for size, kind in kinds],
        compiler_params=pltpu.CompilerParams(vmem_limit_bytes=24 * 1024 * 1024),
        cost_estimate=pl.CostEstimate(flops=0, bytes_accessed=1 << 20, transcendentals=0),
    )(*[pltpu.with_memory_space_constraint(a, pltpu.MemorySpace.HBM) for a in args])


def mix_kernel(place, main_ref, low_ref, high_ref, taps_ref, mix_ref, back_ref, slope_ref, wide):
    strip, side, width = mix_ref.shape
    top, bottom = place[0] > 0, place[0] + strip < place[1]
    blank = jnp.zeros((PAD, LANES), jnp.float32)
    for first in range(0, width, LANES):
        for kind in range(2):
            lanes = slice(kind * width + first, kind * width + first + LANES)
            for slot in range(strip + 2):
                if slot == 0:
                    value = jnp.where(top, low_ref[0, :, lanes].astype(jnp.float32), 0.0)
                elif slot == strip + 1:
                    value = jnp.where(bottom, high_ref[0, :, lanes].astype(jnp.float32), 0.0)
                else:
                    value = main_ref[slot - 1, :, lanes].astype(jnp.float32)
                wide[kind, slot, 0:PAD] = blank
                wide[kind, slot, PAD : PAD + side] = value
                wide[kind, slot, PAD + side : 2 * PAD + side] = blank
        own = slice(first, first + LANES)
        taps = taps_ref[:, own].astype(jnp.float32)
        sums = [jnp.zeros((side, LANES), jnp.float32) for _ in range(9)]
        for row in range(strip):
            grad = wide[1, row + 1, PAD : PAD + side]
            mixed = jnp.zeros((side, LANES), jnp.float32)
            back = jnp.zeros((side, LANES), jnp.float32)
            for a in range(3):
                for b in range(3):
                    tap = 3 * a + b
                    span = slice(PAD + b - 1, PAD + b - 1 + side)
                    value = wide[0, row + a, span]
                    mixed = mixed + value * taps[tap : tap + 1]
                    back = back + wide[1, row + a, span] * taps[8 - tap : 9 - tap]
                    sums[tap] = sums[tap] + value * grad
            mix_ref[row, :, own] = mixed
            back_ref[row, :, own] = back
        for tap in range(9):
            slope_ref[tap : tap + 1, own] = jnp.sum(sums[tap], axis=0, keepdims=True)


def mix(place, both, low, high, taps):
    strip, side, double = both.shape
    width = double // 2
    grid = jax.ShapeDtypeStruct((strip, side, width), jnp.float32)
    return pl.pallas_call(
        mix_kernel,
        in_specs=[SCALARS] + [pl.BlockSpec(memory_space=pltpu.VMEM)] * 4,
        out_specs=[pl.BlockSpec(memory_space=pltpu.VMEM)] * 3,
        out_shape=[grid, grid, jax.ShapeDtypeStruct(taps.shape, jnp.float32)],
        scratch_shapes=[pltpu.VMEM((2, strip + 2, side + 2 * PAD, LANES), jnp.float32)],
        compiler_params=pltpu.CompilerParams(vmem_limit_bytes=16 * 1024 * 1024),
        cost_estimate=pl.CostEstimate(flops=0, bytes_accessed=1 << 20, transcendentals=0),
    )(place, both, low, high, taps)


def row_moments(value):
    average = jnp.mean(value, axis=-1, keepdims=True)
    centred = value - average
    spread = jnp.mean(centred * centred, axis=-1, keepdims=True)
    rate = lax.rsqrt(spread + norm_epsilon)
    return centred * rate, rate


def wide_sum(refs):
    total = refs[0][...].astype(jnp.float32)
    for ref in refs[1:]:
        total = total + ref[...].astype(jnp.float32)
    return total


def norm_kernel(count, *refs):
    gain = refs[count][...].astype(jnp.float32)
    total = wide_sum(refs[:count])
    outs = refs[count + 1 :]
    shape, _ = row_moments(total)
    outs[-1][...] = (shape * gain).astype(outs[-1].dtype)
    if count > 1:
        outs[0][...] = total


def norm_back_kernel(kinds, value_ref, own_ref, other_ref, gain_ref, *refs):
    extra, (slope_ref, *outs) = (refs[0], refs[1:]) if kinds[0] else (None, refs)
    gain = gain_ref[...].astype(jnp.float32)
    shape, rate = row_moments(value_ref[...].astype(jnp.float32))
    grad = own_ref[...].astype(jnp.float32) + other_ref[...].astype(jnp.float32)
    scaled = grad * gain
    first = jnp.mean(scaled, axis=-1, keepdims=True)
    second = jnp.mean(scaled * shape, axis=-1, keepdims=True)
    result = rate * (scaled - first - shape * second)
    if extra is not None:
        result = result + extra[...]
    for out in outs:
        out[...] = result.astype(out.dtype)
    slope = jnp.sum(grad * shape, axis=0, keepdims=True)

    @pl.when(pl.program_id(0) == 0)
    def _():
        slope_ref[...] = slope

    @pl.when(pl.program_id(0) > 0)
    def _():
        slope_ref[...] += slope


ROWS = 144
CHEAP = pl.CostEstimate(flops=0, bytes_accessed=1 << 20, transcendentals=0)


def row_block(width):
    return pl.BlockSpec((ROWS, width), lambda i: (i, 0))


def norm(values, gain):
    rows, width = values[0].shape
    whole = pl.BlockSpec((1, width), lambda i: (0, 0))
    kinds = [jnp.float32, jnp.bfloat16] if len(values) > 1 else [jnp.bfloat16]
    return pl.pallas_call(
        functools.partial(norm_kernel, len(values)),
        grid=(rows // ROWS,),
        in_specs=[row_block(width)] * len(values) + [whole],
        out_specs=[row_block(width)] * len(kinds),
        out_shape=[jax.ShapeDtypeStruct((rows, width), kind) for kind in kinds],
        compiler_params=pltpu.CompilerParams(vmem_limit_bytes=24 * 1024 * 1024),
        cost_estimate=CHEAP,
    )(*values, gain[None])


def norm_back(value, own, other, gain, kinds, extra=None):
    rows, width = value.shape
    whole = pl.BlockSpec((1, width), lambda i: (0, 0))
    more = [] if extra is None else [extra]
    return pl.pallas_call(
        functools.partial(norm_back_kernel, (extra is not None,)),
        grid=(rows // ROWS,),
        in_specs=[row_block(width)] * 3 + [whole] + [row_block(width)] * len(more),
        out_specs=[whole] + [row_block(width)] * len(kinds),
        out_shape=[jax.ShapeDtypeStruct((1, width), jnp.float32)]
        + [jax.ShapeDtypeStruct((rows, width), kind) for kind in kinds],
        compiler_params=pltpu.CompilerParams(vmem_limit_bytes=24 * 1024 * 1024),
        cost_estimate=CHEAP,
    )(value, own, other, gain[None], *more)


def gate_kernel(hidden_ref, own_ref, other_ref, gate_ref, cot_ref, result_ref, gating_ref, low_ref):
    result = wide_sum((hidden_ref, own_ref, other_ref))
    result_ref[...] = result
    total = jnp.sum(result * gate_ref[...].astype(jnp.float32), axis=-1, keepdims=True)
    gating = jax.nn.sigmoid(total)
    gating_ref[...] = jnp.broadcast_to(gating, gating_ref.shape)
    low_ref[...] = (cot_ref[...].astype(jnp.float32) * gating).astype(low_ref.dtype)


def gate(hidden, own, other, vector, cot):
    rows, width = hidden.shape
    return pl.pallas_call(
        gate_kernel,
        out_shape=[
            jax.ShapeDtypeStruct((rows, width), jnp.float32),
            jax.ShapeDtypeStruct((rows, LANES), jnp.float32),
            jax.ShapeDtypeStruct(cot.shape, jnp.bfloat16),
        ],
        compiler_params=pltpu.CompilerParams(vmem_limit_bytes=24 * 1024 * 1024),
        cost_estimate=CHEAP,
    )(hidden, own, other, vector[None], cot)


def rotated(start):
    return tuple(RINGS[(start + i) % len(RINGS)] for i in range(len(RINGS)))


def xor_swap(values, mask):
    count = lax.axis_size("dp")
    return lax.ppermute(values, "dp", [(i, i ^ mask) for i in range(count)])


def chip_offset(place, order, low_first):
    offset = 0
    for k, mask in enumerate(order):
        bit = k if low_first else len(order) - 1 - k
        offset = offset ^ (((place >> bit) & 1) * (mask >> 1))
    return offset


def together(values):
    return list(lax.optimization_barrier(tuple(values)))


def after(value, *others):
    return lax.optimization_barrier((value,) + others)[0]


def gathered_parts(blocks, orders, early, work):
    held = [block[None] for block in blocks]
    count, last = len(blocks), len(RINGS) - 1
    for step in range(last):
        other = [xor_swap(part, order[step]) for part, order in zip(held, orders)]
        held = [jnp.concatenate([a, b], axis=0) for a, b in zip(held, other)]
        done = together(held + (early if step == last - 1 else []))
        held = done[:count]
    other = [xor_swap(part, order[last]) for part, order in zip(held, orders)]
    done = together(other + work(*done[count:]))
    return held, done[:count], done[count:]


def split_sum(kept, other):
    half = kept.shape[0] // 2
    if half == 0:
        return kept.astype(jnp.float32) + other.astype(jnp.float32), None
    return kept[:half] + other[:half], kept[half:] + other[half:]


class Scatter:
    def __init__(self, kept, given, orders):
        self.kept, self.given, self.orders = list(kept), list(given), orders
        self.step = 0

    def advance(self, *tied):
        other = [
            xor_swap(part, order[self.step]) for part, order in zip(self.given, self.orders)
        ]
        done = together(other + list(tied))
        sums = [split_sum(own, got) for own, got in zip(self.kept, done)]
        self.kept, self.given = [low for low, _ in sums], [high for _, high in sums]
        self.step += 1
        return done[len(other) :]

    def result(self):
        return [part[0] for part in self.kept]


def route_kernel(moves, steps, n_in, n_out, place, *refs):
    ins, outs = refs[:n_in], refs[n_in : n_in + n_out]
    held = refs[n_in + n_out : n_in + 2 * n_out]
    sems = refs[n_in + 2 * n_out]
    device = place[0]
    chip, core = device >> 1, device & 1

    for target in range(n_out):

        def step(index, carry):
            for source, take, goal, put, source_box, target_box in moves:
                if goal == target:
                    pltpu.make_async_copy(
                        ins[source].at[(take(chip, core, index),) + source_box],
                        held[goal].at[(put(chip, core, index),) + target_box],
                        sems.at[goal],
                    ).start()
            return carry

        lax.fori_loop(0, steps, step, 0)
    for target in range(n_out):
        pltpu.make_async_copy(held[target], held[target], sems.at[target]).wait()
        pltpu.make_async_copy(held[target], outs[target], sems.at[target]).start()
    for target in range(n_out):
        pltpu.make_async_copy(held[target], outs[target], sems.at[target]).wait()


def route(moves, steps, place, arrays, shapes):
    anywhere = pl.BlockSpec(memory_space=pl.ANY)
    volume = sum(2 * a.size for a in arrays)
    return pl.pallas_call(
        functools.partial(route_kernel, moves, steps, len(arrays), len(shapes)),
        in_specs=[SCALARS] + [anywhere] * len(arrays),
        out_specs=[anywhere] * len(shapes),
        out_shape=[jax.ShapeDtypeStruct(s, jnp.bfloat16) for s in shapes],
        scratch_shapes=[pltpu.VMEM(s, jnp.bfloat16) for s in shapes]
        + [pltpu.SemaphoreType.DMA((len(shapes),))],
        compiler_params=pltpu.CompilerParams(vmem_limit_bytes=volume + volume // 4 + (4 << 20)),
        cost_estimate=CHEAP,
    )(place, *arrays)


def box(rows, cols):
    return (pl.ds(rows[0], rows[1] - rows[0]), pl.ds(cols[0], cols[1] - cols[0]))


def overlap(first, second):
    low, high = max(first[0], second[0]), min(first[1], second[1])
    return (low, high) if low < high else None


def shifted_span(span, base):
    return (span[0] - base, span[1] - base)


def core_swap(values):
    return xor_swap(values, CORE)


def model_swap(values):
    return lax.ppermute(values, "mp", [(0, 1), (1, 0)])


def exchange(values):
    low = values.astype(jnp.bfloat16)
    other = model_swap(low)
    return low.astype(jnp.float32) + other.astype(jnp.float32)


def halo_rows(block, width):
    count = lax.axis_size("dp")
    forward = [(i, (i + 1) % count) for i in range(count)]
    backward = [((i + 1) % count, i) for i in range(count)]
    low = lax.ppermute(block[block.shape[0] - width :], "dp", forward)
    high = lax.ppermute(block[:width], "dp", backward)
    return low, high


def gelu_pair(values):
    below = 0.5 * (1.0 + lax.erf(values * 0.5**0.5))
    slope = below + values * (jnp.exp(-0.5 * values * values) * (2.0 * jnp.pi) ** -0.5)
    return (values * below).astype(jnp.bfloat16), slope.astype(jnp.bfloat16)


def matmul(former, latter):
    return jnp.dot(former, latter, preferred_element_type=jnp.float32)


def matmul_nt(former, latter):
    return lax.dot_general(
        former, latter, (((1,), (1,)), ((), ())), preferred_element_type=jnp.float32
    )


def matmul_tn(former, latter):
    return lax.dot_general(
        former, latter, (((0,), (0,)), ((), ())), preferred_element_type=jnp.float32
    )


def pair_swap(values):
    chips = lax.axis_size("dp") // 2
    pairs = []
    for chip in range(chips):
        other = (chip + 1) % chips if chip % 2 else (chip - 1) % chips
        pairs += [(2 * chip + core, 2 * other + core) for core in range(2)]
    return lax.ppermute(values, "dp", pairs)


def own_half(first, core, axis, other=False):
    size = first.shape[axis] // 2
    low = lax.slice_in_dim(first, 0, size, axis=axis)
    high = lax.slice_in_dim(first, size, 2 * size, axis=axis)
    return jnp.where((core == 0) != other, low, high)


def in_core_order(own, other, core, axis):
    return jnp.where(
        core == 0,
        jnp.concatenate([own, other], axis=axis),
        jnp.concatenate([other, own], axis=axis),
    )


def row_places(device, order, depth):
    chip, core = device >> 1, device & 1
    place = jnp.arange(2 * CHIPS * depth)
    block, line = place // depth, place % depth
    owner = 2 * (chip ^ chip_offset(block % CHIPS, order, True)) + (core ^ (block // CHIPS))
    return owner * depth + line


def row_picker(device, order, depth):
    places = row_places(device, order, depth)
    rows = lax.broadcasted_iota(jnp.int32, (places.shape[0], places.shape[0]), 0)
    return (rows == places[None, :]).astype(jnp.bfloat16)


def all_weights(place, core, small_rows, common_rows, *ties):
    middle = small_rows[4].shape[1] // 2
    first = jnp.concatenate(small_rows[:4] + (small_rows[4][:, :middle],), axis=1)
    second = jnp.concatenate([small_rows[4][:, middle:], small_rows[5]], axis=1)
    kept = jnp.concatenate([own_half(rows, core, 1) for rows in common_rows], axis=1)
    given = jnp.concatenate([own_half(rows, core, 1, True) for rows in common_rows], axis=1)
    common = in_core_order(kept, core_swap(given), core, 0)
    rows = common.shape[0]
    widths = [block.shape[1] // 2 for block in common_rows]
    spans = even_edges(common.shape[1], 3)
    orders = [rotated(i) for i in range(5)]
    held, other, extra = gathered_parts(
        [first, second] + [common[:, low:high] for low, high in spans], orders, *ties
    )
    near = [jnp.concatenate([a, b], axis=0) for a, b in zip(held[:2], other[:2])]
    far = [core_swap(part) for part in near]
    small = [
        tuple(part.reshape(-1, part.shape[2]) for part in pair) for pair in zip(near, far)
    ]
    starts = [0]
    for width in widths:
        starts.append(starts[-1] + width)
    moves = []
    half = CHIPS // 2
    for i, span in enumerate(spans):
        order = orders[i + 2]
        for target in range(len(widths)):
            cols_span = (starts[target], starts[target + 1])
            shared = overlap(cols_span, span)
            if shared is None:
                continue
            for side in range(2):

                def put(chip, core, index, side=side, order=order):
                    return chip ^ chip_offset(index + side * half, order, True)

                moves.append(
                    (
                        2 * i + side,
                        lambda chip, core, index: index,
                        target,
                        put,
                        box((0, rows), shifted_span(shared, span[0])),
                        box((0, rows), shifted_span(shared, cols_span[0])),
                    )
                )
    arrays = [part for pair in zip(held[2:], other[2:]) for part in pair]
    large = route(moves, half, place, arrays, [(CHIPS, rows, width) for width in widths])
    expand, shrink, adapter = [part.reshape(CHIPS * rows, part.shape[2]) for part in large]
    adapter = in_core_order(adapter, core_swap(adapter), core, 1)
    return small, expand, shrink, adapter, extra


def even_edges(width, count):
    tiles = width // LANES
    edges = [LANES * ((tiles * i + count - 1) // count) for i in range(count + 1)]
    return [(edges[i], edges[i + 1]) for i in range(count)]


def turn(left_refs, turned):
    first = 0
    for left_ref in left_refs:
        rows = left_ref.shape[0]
        for start in range(0, left_ref.shape[1], LANES):
            lanes = slice(start, start + LANES)
            turned[lanes, first : first + rows] = left_ref[:, lanes].T
        first += rows


def slope_pack_kernel(orders, spans, place, *refs):
    first_lefts, second_lefts, (right_a, right_b, extra_ref) = refs[:2], refs[2:4], refs[4:7]
    outs, (turned, tile, sems) = refs[7:-3], refs[-3:]
    width = right_a.shape[1]
    step = pl.program_id(0)
    per_side = turned.shape[0] // width
    total = 2 * per_side + 1
    blocks, rows = tile.shape[1], tile.shape[2]
    group = blocks // 4
    chip = place[0] >> 1
    slot = step % 2

    def sent(which, wide):
        box_ref = tile.at[which, :, :, pl.ds(0, wide)]
        return pltpu.make_async_copy(box_ref, box_ref, sems.at[which])

    @pl.when(step >= 2)
    def _():
        sent(slot, width).wait()

    @pl.when(step == 0)
    def _():
        turn(first_lefts, turned)

    @pl.when(step == per_side)
    def _():
        turn(second_lefts, turned)

    def fill(right):
        for part in range(4):
            lines = slice(part * group * rows, (part + 1) * group * rows)
            value = jnp.dot(turned[lines, :], right[...], preferred_element_type=jnp.float32)
            tile[slot, part * group : (part + 1) * group] = value.astype(tile.dtype).reshape(
                group, rows, width
            )

    @pl.when(step < per_side)
    def _():
        fill(right_a)

    @pl.when((step >= per_side) & (step < 2 * per_side))
    def _():
        fill(right_b)

    last = extra_ref.shape[2]

    @pl.when(step == 2 * per_side)
    def _():
        tile[slot, :, :, 0:last] = extra_ref[...]

    for index in range(total):
        begin = index * width
        wide = width if index < 2 * per_side else last
        goal = [i for i, span in enumerate(spans) if span[0] <= begin < span[1]][0]
        cols = pl.ds(begin - spans[goal][0], wide)

        @pl.when(step == index)
        def _(goal=goal, cols=cols, wide=wide):
            def send(spot, carry):
                for side in range(2):
                    owner = chip ^ chip_offset(spot + side * (blocks // 2), orders[goal], True)
                    pltpu.make_async_copy(
                        tile.at[slot, owner, :, pl.ds(0, wide)],
                        outs[2 * goal + side].at[spot, :, cols],
                        sems.at[slot],
                    ).start()
                return carry

            lax.fori_loop(0, blocks // 2, send, 0)

    @pl.when(step == total - 1)
    def _():
        sent(1 - slot, width).wait()
        sent(slot, last).wait()


def packed_slopes(place, orders, spans, first_lefts, right_a, second_lefts, right_b, extra):
    channels = first_lefts[0].shape[1]
    depth, hidden = right_a.shape
    width = 384
    steps = hidden // width
    rows = channels // CHIPS
    extra = extra.reshape(CHIPS, rows, extra.shape[1])
    once = pl.Buffered(1)
    return pl.pallas_call(
        functools.partial(slope_pack_kernel, orders, spans),
        grid=(2 * steps + 1,),
        in_specs=[SCALARS]
        + [
            pl.BlockSpec(left.shape, lambda i: (0, 0), pipeline_mode=once)
            for left in (*first_lefts, *second_lefts)
        ]
        + [
            pl.BlockSpec((depth, width), lambda i: (0, jnp.minimum(i, steps - 1))),
            pl.BlockSpec((depth, width), lambda i: (0, jnp.clip(i - steps, 0, steps - 1))),
            pl.BlockSpec(extra.shape, lambda i: (0, 0, 0), pipeline_mode=once),
        ],
        out_specs=[pl.BlockSpec(memory_space=pl.ANY)] * (2 * len(spans)),
        out_shape=[
            jax.ShapeDtypeStruct((CHIPS // 2, rows, high - low), jnp.bfloat16)
            for low, high in spans
            for _ in range(2)
        ],
        scratch_shapes=[
            pltpu.VMEM((channels, depth), jnp.bfloat16),
            pltpu.VMEM((2, CHIPS, rows, width), jnp.bfloat16),
            pltpu.SemaphoreType.DMA((2,)),
        ],
        compiler_params=pltpu.CompilerParams(vmem_limit_bytes=40 * 1024 * 1024),
        cost_estimate=CHEAP,
    )(place, *first_lefts, *second_lefts, right_a, right_b, extra)


def unpacked_map_slopes(core, blocks, widths):
    block = jnp.concatenate(blocks, axis=1)
    own = own_half(block, core, 0)
    got = core_swap(own_half(block, core, 0, True).astype(jnp.bfloat16)).astype(jnp.float32)
    outs = []
    start = 0
    for width in widths:
        outs.append(
            in_core_order(own[:, start : start + width], got[:, start : start + width], core, 1)
        )
        start += width
    return outs


def row_sums(values):
    count = values.shape[0]
    pieces = lax.all_to_all(values, "dp", 0, 0, tiled=True)
    return jnp.sum(pieces.astype(jnp.float32), axis=0)


def row_copies(row):
    count = lax.axis_size("dp")
    return lax.all_to_all(jnp.broadcast_to(row[None], (count,) + row.shape), "dp", 0, 0, tiled=True)


def on_device(
    lowres_in,
    highres_in,
    image_sizes,
    attn_gain,
    query_weight,
    key_weight,
    value_weight,
    output_weight,
    mlp_gain,
    up_weight,
    down_weight,
    depth_kernel,
    conv_gain,
    expand_weight,
    shrink_weight,
    layer_scale,
    adapter_weight,
    adapter_kernel,
    gate_vector,
    out_cotangent,
    map_cotangent,
):
    device = lax.axis_index("dp")
    core = device & 1
    place = device.reshape(1).astype(jnp.int32)
    group_count = lax.axis_size("dp") // TILES
    position = (device + 2) % TILES
    group_id = (device + 2) // TILES % group_count
    model_half = lax.axis_index("mp")
    low_strip, _, grid_side, width = lowres_in.shape
    high_strip, _, high_side, channels = highres_in.shape
    own_width = adapter_kernel.shape[1]
    local_width = query_weight.shape[1]
    local_heads = local_width // HD
    scaling = HD ** (-0.5)
    token_count = low_strip * grid_side
    pixel_count = high_strip * high_side

    high_map = highres_in.reshape(high_strip, high_side, channels)
    table_ids = jnp.arange(image_sizes.shape[0])
    extent = jnp.sum(jnp.where(table_ids == group_id, image_sizes, 0))
    first_row = position * high_strip
    map_place = jnp.stack([first_row, extent]).astype(jnp.int32)
    token_low = lowres_in.reshape(token_count, width)
    local_grad_low = out_cotangent.reshape(low_strip, grid_side, own_width)
    backs = []
    depth = query_weight.shape[0]
    pickers = [row_picker(device, rotated(i), depth) for i in range(2)]

    def convolve(map_low, map_high):
        convolved = map_conv(map_place, high_map, map_low, map_high, depth_kernel)
        convolved = convolved.reshape(pixel_count, channels)
        (normed_low,) = norm([token_low], attn_gain)
        normed_first = matmul(normed_low, pickers[0]).astype(jnp.bfloat16)
        backs.extend([map_low, map_high, convolved])
        return [*norm([convolved], conv_gain), normed_low, normed_first]

    small, expand_full, shrink_full, adapter_full, extra = all_weights(
        place,
        core,
        (query_weight, key_weight, value_weight, output_weight.T, up_weight, down_weight.T),
        (expand_weight, shrink_weight.T, adapter_weight),
        list(halo_rows(high_map, RADIUS)),
        convolve,
    )
    map_low, map_high, convolved = backs
    normed_map_low, normed_low, normed_first = extra
    normed_map_given_low = core_swap(normed_map_low)
    normed_map_pair = jnp.concatenate([normed_map_low, normed_map_given_low], axis=0)
    triple = 3 * local_width
    quad = 4 * local_width
    hidden_width = up_weight.shape[1]
    hidden_half = hidden_width // 2

    def pieces(index, low, high):
        return [part[:, low:high] for part in small[index]]

    qkv_parts = pieces(0, 0, triple)
    output_parts = pieces(0, triple, quad)
    up_parts = [pieces(0, quad, quad + hidden_half), pieces(1, 0, hidden_half)]
    down_parts = pieces(1, hidden_half, hidden_half + hidden_width)

    def picked(values, index):
        return matmul(values, pickers[index]).astype(jnp.bfloat16)

    def restored(values, index):
        return matmul_nt(values.astype(jnp.bfloat16), pickers[index])

    def into(values, parts):
        half = values.shape[1] // 2
        return matmul(values[:, :half], parts[0]) + matmul(values[:, half:], parts[1])

    def outof(values, parts):
        return jnp.concatenate([matmul_nt(values, part) for part in parts], axis=1)

    qkv_rows = into(normed_first, qkv_parts).astype(jnp.bfloat16)
    pair = qkv_rows[:, local_width:]
    pair_other, expand_full, shrink_full = together([pair_swap(pair), expand_full, shrink_full])
    pair = jnp.concatenate([pair, pair_other], axis=0)
    pair = jnp.concatenate([pair, core_swap(pair)], axis=0)
    attended_low = attend(qkv_rows, pair)
    hidden_own = restored(outof(attended_low, output_parts), 0).astype(jnp.bfloat16)
    hidden_rows, normed_two_low = norm([token_low, hidden_own, model_swap(hidden_own)], mlp_gain)
    normed_two_picked = [picked(normed_two_low, i) for i in range(2)]
    expanded = jnp.concatenate(
        [into(normed_two_picked[i], up_parts[i]) for i in range(2)], axis=1
    )
    activated_low, activated_slope = gelu_pair(expanded)
    result_own = restored(outof(activated_low, down_parts), 1).astype(jnp.bfloat16)
    result_rows, gating, lifted_grad_low = gate(
        hidden_rows,
        result_own,
        model_swap(result_own),
        gate_vector,
        local_grad_low.reshape(token_count, own_width),
    )

    result_grid = result_rows.reshape(low_strip, grid_side, width)
    gate_wide = gate_vector.astype(jnp.float32)
    gating = gating[:, :1].reshape(low_strip, grid_side, 1)
    out_grad = local_grad_low.astype(jnp.float32)
    grid_shape = (low_strip, grid_side, channels)
    pooled_own = matmul_nt(lifted_grad_low, adapter_full).astype(jnp.bfloat16).reshape(grid_shape)
    pooled_other = model_swap(pooled_own)

    widened = matmul(normed_map_pair, expand_full)
    widened_low, widened_slope = gelu_pair(widened)
    widened_low = after(widened_low, pooled_own)
    narrowed_part, narrowed_given = dense([widened_low], shrink_full, True, halves=True)
    narrowed_part = narrowed_part + core_swap(narrowed_given).astype(jnp.float32)
    map_shape = (high_strip, high_side, channels)
    narrowed_own = narrowed_part.astype(jnp.bfloat16).reshape(map_shape)
    narrowed_own, pooled_other = together([narrowed_own, pooled_other])
    narrowed_other = model_swap(narrowed_own)

    map_grad, narrowed_grad_low = spread_map(
        map_place, pooled_own, pooled_other, map_cotangent.reshape(map_shape), layer_scale[None]
    )
    narrowed_grad_low = narrowed_grad_low.reshape(pixel_count, channels)
    narrowed_grad_pair = [narrowed_grad_low, core_swap(narrowed_grad_low)]
    (widened_grad_low,) = dense(narrowed_grad_pair, shrink_full, False, widened_slope)
    normed_map_part, normed_map_given = dense([widened_grad_low], expand_full, True, halves=True)
    normed_map_given, narrowed_other = together([normed_map_given, narrowed_other])
    normed_map_part = normed_map_part + core_swap(normed_map_given).astype(jnp.float32)
    normed_map_own = normed_map_part.astype(jnp.bfloat16)

    mapped, pooled_low, layer_scale_slope = blend_map(
        map_place, narrowed_own, narrowed_other, high_map, layer_scale[None], map_grad
    )
    pooled_low = pooled_low.reshape(token_count, channels)
    lifted = matmul(pooled_low, adapter_full).reshape(low_strip, grid_side, own_width)

    own_result = lax.dynamic_slice_in_dim(result_grid, model_half * own_width, own_width, 2)
    own_result_low = own_result.astype(jnp.bfloat16)
    both_low = jnp.concatenate([own_result_low, local_grad_low], axis=2)
    both_edges = halo_rows(after(both_low, widened_grad_low), 1)
    mix_place = jnp.stack([position * low_strip, TILES * low_strip]).astype(jnp.int32)
    local_mix, local_back, adapter_kernel_slope = mix(
        mix_place, both_low, *both_edges, adapter_kernel
    )
    blended = own_result + local_mix + gating * lifted

    gate_part = jnp.sum(out_grad * lifted, axis=-1, keepdims=True)
    gate_grad = exchange(gate_part)
    adapter_slope = matmul_tn(pooled_low, lifted_grad_low)
    adapter_slope = own_half(adapter_slope, core, 1) + core_swap(
        own_half(adapter_slope, core, 1, True).astype(jnp.bfloat16)
    ).astype(jnp.float32)
    own_grad = out_grad + local_back
    own_grad_low = own_grad.astype(jnp.bfloat16)
    other_grad = model_swap(own_grad_low)
    result_grad = in_core_order(own_grad_low, other_grad, model_half, 2).astype(jnp.float32)
    gate_slope = gate_grad * gating * (1.0 - gating)
    gate_vector_slope = jnp.sum((gate_slope * result_grid).reshape(token_count, width), axis=0)
    result_grad = (result_grad + gate_slope * gate_wide).reshape(token_count, width)

    result_low = after(result_grad.astype(jnp.bfloat16), widened_grad_low)
    result_picked = picked(result_low, 1)
    activated_grad = into(result_picked, down_parts)
    expanded_grad_low = (activated_grad * activated_slope.astype(jnp.float32)).astype(jnp.bfloat16)
    expanded_grad_parts = [expanded_grad_low[:, :hidden_half], expanded_grad_low[:, hidden_half:]]
    second_slopes = split_rows(
        paired_slopes(
            (normed_two_picked[1], result_picked), (expanded_grad_parts[1], activated_low)
        )
    )
    normed_two_own = sum(
        restored(outof(expanded_grad_parts[i], up_parts[i]), i) for i in range(2)
    ).astype(jnp.bfloat16)
    normed_two_other = model_swap(normed_two_own)
    normed_two_other, normed_map_own, *second_slopes = together(
        [normed_two_other, normed_map_own, *second_slopes]
    )
    second_far = core_swap(second_slopes[1])
    normed_map_other = model_swap(normed_map_own)
    mlp_gain_slope, hidden_grad, hidden_low = norm_back(
        hidden_rows,
        normed_two_own,
        normed_two_other,
        mlp_gain,
        (jnp.float32, jnp.bfloat16),
        result_grad,
    )
    hidden_picked = picked(hidden_low, 0)
    attended_grad_low = into(hidden_picked, output_parts).astype(jnp.bfloat16)
    query_grad_rows, key_grad_all, value_grad_all = attend_back(qkv_rows, pair, attended_grad_low)
    pair_back = jnp.concatenate(
        [key_grad_all, value_grad_all], axis=1
    )
    pair_back = pair_back[: 2 * token_count] + core_swap(
        pair_back[2 * token_count :].astype(jnp.bfloat16)
    ).astype(jnp.float32)
    pair_given, late_place = together([pair_back[token_count:].astype(jnp.bfloat16), place])
    pair_other = pair_swap(pair_given)
    map_widths = (widened_low.shape[1], widened_low.shape[1], adapter_slope.shape[1])
    map_slopes_packed = packed_slopes(
        late_place,
        [rotated(i) for i in range(2, 5)],
        even_edges(sum(map_widths), 3),
        [normed_map_low, normed_map_given_low],
        widened_grad_low,
        narrowed_grad_pair,
        widened_low,
        adapter_slope.astype(jnp.bfloat16),
    )
    second_near = split_sum(second_slopes[0], second_far)
    pair_other, normed_map_other, *rest = together(
        [pair_other, normed_map_other, *second_near, *map_slopes_packed]
    )
    second_near, map_slopes_packed = rest[:2], rest[2:]
    pair_back = pair_back[:token_count] + pair_other.astype(jnp.float32)
    qkv_grad = jnp.concatenate([query_grad_rows, pair_back.astype(jnp.bfloat16)], axis=1)
    normed_own = restored(outof(qkv_grad, qkv_parts), 0).astype(jnp.bfloat16)
    normed_other = model_swap(normed_own)
    conv_gain_slope, convolved_grad_low = norm_back(
        convolved, normed_map_own, normed_map_other, conv_gain, (jnp.bfloat16,)
    )
    convolved_grad_low = convolved_grad_low.reshape(map_shape)
    convolved_grad_low, qkv_grad = together([convolved_grad_low, qkv_grad])
    grad_low, grad_high = halo_rows(convolved_grad_low, RADIUS)
    first_slopes = split_rows(
        paired_slopes(
            (normed_first, hidden_picked, normed_two_picked[0]),
            (qkv_grad, attended_low, expanded_grad_parts[0]),
        )
    )
    first_far = core_swap(first_slopes[1])
    grad_low, grad_high, *map_slopes_packed = together(
        [grad_low, grad_high, *map_slopes_packed]
    )
    near = [split_sum(first_slopes[0], first_far), second_near]
    scatter = Scatter(
        [low for low, _ in near] + list(map_slopes_packed[0::2]),
        [high for _, high in near] + list(map_slopes_packed[1::2]),
        [rotated(i)[::-1] for i in range(5)],
    )

    depth_kernel_slope = map_slopes(map_place, high_map, map_low, map_high, convolved_grad_low)
    highres_grad = map_conv(
        map_place, convolved_grad_low, grad_low, grad_high, depth_kernel, map_grad
    )
    attn_gain_slope, lowres_grad = norm_back(
        token_low, normed_own, normed_other, attn_gain, (jnp.float32,), hidden_grad
    )
    lowres_grad = lowres_grad.reshape(low_strip, 1, grid_side, width)

    def as_rows(values):
        return jnp.pad(values, ((0, 0), (0, channels - values.shape[1])))

    minor_rows = jnp.concatenate(
        [
            depth_kernel_slope,
            conv_gain_slope,
            layer_scale_slope,
            as_rows(
                jnp.concatenate([attn_gain_slope, mlp_gain_slope, gate_vector_slope[None]], axis=0)
            ),
            as_rows(adapter_kernel_slope),
        ],
        axis=0,
    )
    lines = channels // LANES
    block_rows = -(-lines // 16) * 16
    minor = jnp.pad(
        minor_rows.astype(jnp.bfloat16).reshape(minor_rows.shape[0], lines, LANES),
        ((0, 2 * CHIPS - minor_rows.shape[0]), (0, block_rows - lines), (0, 0)),
    )
    minor_own = row_sums(minor).astype(jnp.bfloat16)
    highres_grad, minor_own = scatter.advance(highres_grad, minor_own)
    minor_copies = row_copies(minor_own)
    (minor_copies,) = scatter.advance(minor_copies)
    minor_all = (
        minor_copies[:, :lines].reshape(2 * CHIPS, channels).astype(jnp.float32)
    )
    while scatter.step < len(RINGS):
        scatter.advance()
    first_own, second_own, *map_blocks = scatter.result()
    up_own = jnp.concatenate([first_own[:, quad:], second_own[:, :hidden_half]], axis=1)
    down_own = second_own[:, hidden_half:]
    expand_own, shrink_own, adapter_own = unpacked_map_slopes(
        core,
        map_blocks,
        map_widths,
    )
    firsts = [first_own[:, i * local_width : (i + 1) * local_width] for i in range(4)]
    taps = depth_kernel.shape[0]
    side_taps = adapter_kernel.shape[0]
    return (
        blended.astype(jnp.bfloat16)[:, None],
        mapped[:, None],
        lowres_grad,
        highres_grad[:, None],
        minor_all[taps + 2, :width],
        firsts[0],
        firsts[1],
        firsts[2],
        firsts[3].T,
        minor_all[taps + 3, :width],
        up_own,
        down_own.T,
        minor_all[:taps],
        minor_all[taps],
        expand_own,
        shrink_own.T,
        minor_all[taps + 1],
        adapter_own,
        minor_all[taps + 5 : taps + 5 + side_taps, :own_width],
        minor_all[taps + 4, :width],
    )


def solution(mesh):
    in_specs = (
        P("dp", None, None, None),
        P("dp", None, None, None),
        P(),
        P(),
        P("dp", "mp"),
        P("dp", "mp"),
        P("dp", "mp"),
        P("mp", "dp"),
        P(),
        P("dp", "mp"),
        P("mp", "dp"),
        P(),
        P(),
        P("dp", "mp"),
        P("mp", "dp"),
        P(),
        P("dp", "mp"),
        P(None, "mp"),
        P(),
        P("dp", None, None, "mp"),
        P("dp", None, None, None),
    )
    out_specs = (
        P("dp", None, None, "mp"),
        P("dp", None, None, None),
        P("dp", None, None, None),
        P("dp", None, None, None),
        P(),
        P("dp", "mp"),
        P("dp", "mp"),
        P("dp", "mp"),
        P("mp", "dp"),
        P(),
        P("dp", "mp"),
        P("mp", "dp"),
        P(),
        P(),
        P("dp", "mp"),
        P("mp", "dp"),
        P(),
        P("dp", "mp"),
        P(None, "mp"),
        P(),
    )
    return jax.shard_map(
        on_device, mesh=mesh, in_specs=in_specs, out_specs=out_specs, check_vma=False
    )
```

```python
import functools

import jax
import jax.numpy as jnp
from jax import lax
from jax.experimental import pallas as pl
from jax.experimental.pallas import tpu as pltpu
from jax.sharding import PartitionSpec as P

HD = 64
TILES = 4
CHIPS = 32
CORE = 1
RINGS = (2, 6, 8, 24, 32)

norm_epsilon = 1e-06

LANES = 128
RADIUS = 3
WINDOW = 7
PAD = 8


def masked_rows(place, main_ref, low_ref, high_ref, wide, strip, side, bounded):
    first, extent = place[0], place[1]
    cols = lax.broadcasted_iota(jnp.int32, (side, LANES), 0)

    def put(slot, value):
        row = first + slot - RADIUS
        limit = extent if bounded else side
        keep = (cols < limit) & (row >= 0) & (row < limit)
        wide[slot] = jnp.where(keep, value.astype(jnp.float32), 0.0)

    for slot in range(RADIUS):
        put(slot, low_ref[slot])
        put(RADIUS + strip + slot, high_ref[slot])
    for slot in range(strip):
        put(RADIUS + slot, main_ref[slot])


def window_sum(wide, taps_ref, shifted, row, side, flipped):
    sums = [None] * WINDOW
    for a in range(WINDOW):
        line = wide[row + a]
        for b in range(WINDOW):
            tap = WINDOW * a + b
            if flipped:
                tap = WINDOW * WINDOW - 1 - tap
            term = line * taps_ref[tap : tap + 1]
            sums[b] = term if sums[b] is None else sums[b] + term
    total = sums[RADIUS]
    for b in range(WINDOW):
        if b != RADIUS:
            shifted[b, PAD : PAD + side] = sums[b]
    for b in range(WINDOW):
        if b != RADIUS:
            total = total + shifted[b, PAD + b - RADIUS : PAD + b - RADIUS + side]
    return total


def clear_edges(shifted, side):
    for b in range(WINDOW):
        shifted[b, 0:PAD] = jnp.zeros((PAD, LANES), jnp.float32)
        shifted[b, PAD + side : 2 * PAD + side] = jnp.zeros((PAD, LANES), jnp.float32)


def forward_kernel(place, main_ref, low_ref, high_ref, taps_in, out_ref, wide, taps, shifted):
    strip, side = main_ref.shape[0], main_ref.shape[1]
    masked_rows(place, main_ref, low_ref, high_ref, wide, strip, side, True)
    clear_edges(shifted, side)
    taps[...] = taps_in[...].astype(jnp.float32)

    def step(row, carry):
        out_ref[row] = window_sum(wide, taps, shifted, row, side, False)
        return carry

    lax.fori_loop(0, strip, step, 0, unroll=2)


def backward_kernel(place, main_ref, low_ref, high_ref, taps_in, add_ref, out_ref, wide, taps, shifted):
    strip, side = main_ref.shape[0], main_ref.shape[1]
    masked_rows(place, main_ref, low_ref, high_ref, wide, strip, side, False)
    clear_edges(shifted, side)
    taps[...] = taps_in[...].astype(jnp.float32)
    cols = lax.broadcasted_iota(jnp.int32, (side, LANES), 0)

    def step(row, carry):
        total = window_sum(wide, taps, shifted, row, side, True) + add_ref[row]
        keep = (cols < place[1]) & (place[0] + row < place[1])
        out_ref[row] = jnp.where(keep, total, 0.0)
        return carry

    lax.fori_loop(0, strip, step, 0, unroll=2)


def slope_kernel(place, main_ref, low_ref, high_ref, grad_ref, out_ref, wide, padded):
    strip, side = main_ref.shape[0], main_ref.shape[1]
    masked_rows(place, main_ref, low_ref, high_ref, wide, strip, side, True)
    edge = jnp.zeros((PAD, LANES), jnp.float32)
    for row in range(strip):
        padded[row, 0:PAD] = edge
        padded[row, PAD : PAD + side] = grad_ref[row].astype(jnp.float32)
        padded[row, PAD + side : 2 * PAD + side] = edge
    for group in ((0, 1, 2, 3), (4, 5, 6)):

        def step(row, sums):
            lines = [wide[row + a] for a in group]
            fresh = list(sums)
            for b in range(WINDOW):
                start = PAD + RADIUS - b
                part = padded[row, start : start + side]
                for i in range(len(group)):
                    term = (lines[i] * part).reshape(side // 8, 8, LANES)
                    fresh[i * WINDOW + b] = fresh[i * WINDOW + b] + jnp.sum(term, axis=0)
            return tuple(fresh)

        start = tuple(jnp.zeros((8, LANES), jnp.float32) for _ in range(len(group) * WINDOW))
        sums = lax.fori_loop(0, strip, step, start, unroll=4)
        for i, a in enumerate(group):
            for b in range(WINDOW):
                tap = a * WINDOW + b
                out_ref[tap : tap + 1] = jnp.sum(sums[i * WINDOW + b], axis=0, keepdims=True)


def block3(rows, side):
    return pl.BlockSpec((rows, side, LANES), lambda i: (0, 0, i))


SCALARS = pl.BlockSpec(memory_space=pltpu.SMEM)


def in_hbm(values):
    return [pltpu.with_memory_space_constraint(v, pltpu.MemorySpace.HBM) for v in values]


def map_conv(place, main, low, high, taps, added=None):
    strip, side, channels = main.shape
    count = taps.shape[0]
    tap_spec = pl.BlockSpec((count, LANES), lambda i: (0, i))
    specs = [SCALARS, block3(strip, side), block3(RADIUS, side), block3(RADIUS, side), tap_spec]
    args = [place, main, low, high, taps]
    if added is not None:
        specs.append(block3(strip, side))
        args.append(added)
        args[1:] = in_hbm(args[1:])
    work = strip * side * channels
    return pl.pallas_call(
        forward_kernel if added is None else backward_kernel,
        grid=(channels // LANES,),
        in_specs=specs,
        out_specs=block3(strip, side),
        out_shape=jax.ShapeDtypeStruct((strip, side, channels), jnp.float32),
        scratch_shapes=[
            pltpu.VMEM((strip + 2 * RADIUS, side, LANES), jnp.float32),
            pltpu.VMEM((count, LANES), jnp.float32),
            pltpu.VMEM((WINDOW, side + 2 * PAD, LANES), jnp.float32),
        ],
        compiler_params=pltpu.CompilerParams(vmem_limit_bytes=24 * 1024 * 1024),
        cost_estimate=pl.CostEstimate(flops=0, bytes_accessed=work // 8, transcendentals=0),
    )(*args)


def map_slopes(place, main, low, high, grad):
    strip, side, channels = main.shape
    count = WINDOW * WINDOW
    work = strip * side * channels
    return pl.pallas_call(
        slope_kernel,
        grid=(channels // LANES,),
        in_specs=[SCALARS, block3(strip, side), block3(RADIUS, side), block3(RADIUS, side), block3(strip, side)],
        out_specs=pl.BlockSpec((count, LANES), lambda i: (0, i)),
        out_shape=jax.ShapeDtypeStruct((count, channels), jnp.float32),
        scratch_shapes=[
            pltpu.VMEM((strip + 2 * RADIUS, side, LANES), jnp.float32),
            pltpu.VMEM((strip, side + 2 * PAD, LANES), jnp.float32),
        ],
        compiler_params=pltpu.CompilerParams(vmem_limit_bytes=24 * 1024 * 1024),
        cost_estimate=pl.CostEstimate(flops=0, bytes_accessed=work // 8, transcendentals=0),
    )(place, *in_hbm([main, low, high, grad]))


WIDE = 384


def inside(place, row, side):
    cols = lax.broadcasted_iota(jnp.int32, (side, LANES), 0)
    return (cols < place[1]) & (place[0] + row < place[1])


def blend_kernel(
    place, own_ref, other_ref, map_ref, scale_ref, grad_ref, out_ref, pool_ref, slope_ref, line
):
    strip, side = map_ref.shape[0], map_ref.shape[1]
    half = side // 2
    for part in range(map_ref.shape[2] // LANES):
        lanes = slice(part * LANES, (part + 1) * LANES)
        scale = scale_ref[:, lanes].astype(jnp.float32)

        def step(pair, slope):
            total = None
            for i in range(2):
                row = 2 * pair + i
                narrow = own_ref[row, :, lanes].astype(jnp.float32) + other_ref[
                    row, :, lanes
                ].astype(jnp.float32)
                value = map_ref[row, :, lanes].astype(jnp.float32) + scale * narrow
                value = jnp.where(inside(place, row, side), value, 0.0)
                out_ref[row, :, lanes] = value.astype(out_ref.dtype)
                total = value if total is None else total + value
                product = grad_ref[row, :, lanes] * narrow
                slope = slope + jnp.sum(product.reshape(side // 8, 8, LANES), axis=0)
            line[...] = total
            pooled = line[pl.ds(0, half, 2), :] + line[pl.ds(1, half, 2), :]
            pool_ref[pair, :, lanes] = (pooled * 0.25).astype(pool_ref.dtype)
            return slope

        slope = lax.fori_loop(0, strip // 2, step, jnp.zeros((8, LANES), jnp.float32))
        slope_ref[:, lanes] = jnp.sum(slope, axis=0, keepdims=True)


def spread_kernel(place, pool_ref, pool_other_ref, cot_ref, scale_ref, grad_ref, low_ref, line):
    strip, side = cot_ref.shape[0], cot_ref.shape[1]
    half = side // 2
    for part in range(cot_ref.shape[2] // LANES):
        lanes = slice(part * LANES, (part + 1) * LANES)
        scale = scale_ref[:, lanes].astype(jnp.float32)

        def step(pair, carry):
            pooled = pool_ref[pair, :, lanes].astype(jnp.float32) + pool_other_ref[
                pair, :, lanes
            ].astype(jnp.float32)
            pooled = pooled * 0.25
            line[pl.ds(0, half, 2), :] = pooled
            line[pl.ds(1, half, 2), :] = pooled
            spread = line[...]
            for i in range(2):
                row = 2 * pair + i
                value = cot_ref[row, :, lanes].astype(jnp.float32) + spread
                value = jnp.where(inside(place, row, side), value, 0.0)
                grad_ref[row, :, lanes] = value
                low_ref[row, :, lanes] = (value * scale).astype(low_ref.dtype)
            return carry

        lax.fori_loop(0, strip // 2, step, 0)


def wide_block(*lead):
    return pl.BlockSpec(lead + (WIDE,), lambda i: (0,) * len(lead) + (i,))


def blend_map(place, own, other, main, scale, grad):
    strip, side, channels = main.shape
    full = wide_block(strip, side)
    pool = (strip // 2, side // 2)
    return pl.pallas_call(
        blend_kernel,
        grid=(channels // WIDE,),
        in_specs=[SCALARS, full, full, full, wide_block(1), full],
        out_specs=[full, wide_block(*pool), wide_block(1)],
        out_shape=[
            jax.ShapeDtypeStruct(main.shape, jnp.bfloat16),
            jax.ShapeDtypeStruct(pool + (channels,), jnp.bfloat16),
            jax.ShapeDtypeStruct((1, channels), jnp.float32),
        ],
        scratch_shapes=[pltpu.VMEM((side, LANES), jnp.float32)],
        compiler_params=pltpu.CompilerParams(vmem_limit_bytes=24 * 1024 * 1024),
        cost_estimate=pl.CostEstimate(flops=0, bytes_accessed=1 << 20, transcendentals=0),
    )(place, own, other, main, scale, grad)


def spread_map(place, pool, pool_other, cot, scale):
    strip, side, channels = cot.shape
    full = wide_block(strip, side)
    pooled = wide_block(strip // 2, side // 2)
    return pl.pallas_call(
        spread_kernel,
        grid=(channels // WIDE,),
        in_specs=[SCALARS, pooled, pooled, full, wide_block(1)],
        out_specs=[full, full],
        out_shape=[
            jax.ShapeDtypeStruct(cot.shape, jnp.float32),
            jax.ShapeDtypeStruct(cot.shape, jnp.bfloat16),
        ],
        scratch_shapes=[pltpu.VMEM((side, LANES), jnp.float32)],
        compiler_params=pltpu.CompilerParams(vmem_limit_bytes=24 * 1024 * 1024),
        cost_estimate=pl.CostEstimate(flops=0, bytes_accessed=1 << 20, transcendentals=0),
    )(place, pool, pool_other, cot, scale)


def head_lanes(rows, head):
    lanes = lax.broadcasted_iota(jnp.int32, (rows, LANES), 1)
    return (lanes >= head * HD) & (lanes < (head + 1) * HD)


def nt(former, latter):
    return lax.dot_general(
        former, latter, (((1,), (1,)), ((), ())), preferred_element_type=jnp.float32
    )


def tn(former, latter):
    return lax.dot_general(
        former, latter, (((0,), (0,)), ((), ())), preferred_element_type=jnp.float32
    )


def softmax_rows(scores):
    top = jnp.max(scores, axis=-1, keepdims=True)
    raised = jnp.exp(scores - top)
    return raised * (1.0 / jnp.sum(raised, axis=-1, keepdims=True))


def attend_kernel(query_ref, key_ref, value_ref, out_ref):
    rows = query_ref.shape[0]
    query, key, value = query_ref[...], key_ref[...], value_ref[...]
    total = jnp.zeros((rows, LANES), jnp.float32)
    for head in range(LANES // HD):
        mine = head_lanes(rows, head)
        scores = nt(jnp.where(mine, query, jnp.zeros_like(query)), key) * HD ** (-0.5)
        weights = softmax_rows(scores).astype(jnp.bfloat16)
        part = jnp.dot(weights, value, preferred_element_type=jnp.float32)
        total = jnp.where(mine, part, total)
    out_ref[...] = total.astype(out_ref.dtype)


def attend_back_kernel(
    query_ref, key_ref, value_ref, grad_ref, query_out, key_out, value_out
):
    rows = query_ref.shape[0]
    query, key, value, grad = query_ref[...], key_ref[...], value_ref[...], grad_ref[...]
    none = jnp.zeros_like(query)
    query_grad = jnp.zeros((rows, LANES), jnp.float32)
    key_grad, value_grad = None, None
    for head in range(LANES // HD):
        mine = head_lanes(rows, head)
        query_own = jnp.where(mine, query, none)
        grad_own = jnp.where(mine, grad, none)
        weights = softmax_rows(nt(query_own, key) * HD ** (-0.5))
        weight_grad = nt(grad_own, value)
        row_dot = jnp.sum(weights * weight_grad, axis=-1, keepdims=True)
        score_grad = (weights * (weight_grad - row_dot)).astype(jnp.bfloat16)
        part = jnp.dot(score_grad, key, preferred_element_type=jnp.float32)
        query_grad = jnp.where(mine, part, query_grad)
        key_part = tn(score_grad, query_own)
        value_part = tn(weights.astype(jnp.bfloat16), grad_own)
        key_grad = key_part if key_grad is None else key_grad + key_part
        value_grad = value_part if value_grad is None else value_grad + value_part
    query_out[...] = (query_grad * HD ** (-0.5)).astype(query_out.dtype)
    key_out[...] = key_grad * HD ** (-0.5)
    value_out[...] = value_grad


def lane_block(rows, shift=0):
    return pl.BlockSpec((rows, LANES), lambda i: (0, i + shift))


def attend(rows, pair):
    count, keys = rows.shape[0], pair.shape[0]
    width = pair.shape[1] // 2
    steps = width // LANES
    work = 4 * count * keys * width
    return pl.pallas_call(
        attend_kernel,
        grid=(steps,),
        in_specs=[lane_block(count), lane_block(keys), lane_block(keys, steps)],
        out_specs=lane_block(count),
        out_shape=jax.ShapeDtypeStruct((count, width), jnp.bfloat16),
        compiler_params=pltpu.CompilerParams(vmem_limit_bytes=24 * 1024 * 1024),
        cost_estimate=pl.CostEstimate(flops=0, bytes_accessed=1 << 20, transcendentals=0),
    )(rows, pair, pair)


def attend_back(rows, pair, grad):
    count, keys = rows.shape[0], pair.shape[0]
    width = pair.shape[1] // 2
    steps = width // LANES
    work = 10 * count * keys * width
    return pl.pallas_call(
        attend_back_kernel,
        grid=(steps,),
        in_specs=[
            lane_block(count),
            lane_block(keys),
            lane_block(keys, steps),
            lane_block(count),
        ],
        out_specs=[lane_block(count), lane_block(keys), lane_block(keys)],
        out_shape=[
            jax.ShapeDtypeStruct((count, width), jnp.bfloat16),
            jax.ShapeDtypeStruct((keys, width), jnp.float32),
            jax.ShapeDtypeStruct((keys, width), jnp.float32),
        ],
        compiler_params=pltpu.CompilerParams(vmem_limit_bytes=24 * 1024 * 1024),
        cost_estimate=pl.CostEstimate(flops=0, bytes_accessed=1 << 20, transcendentals=0),
    )(rows, pair, pair, grad)


def slopes_kernel(ends, *refs):
    count = len(ends)
    lefts, rights = refs[:count], refs[count : 2 * count]
    near_ref, far_ref = refs[2 * count :]
    half = near_ref.shape[0]
    step = pl.program_id(0)
    first = 0
    for left, right, end in zip(lefts, rights, ends):

        @pl.when((step >= first) & (step < end))
        def _(left=left, right=right):
            near_ref[...] = tn(left[:, :half], right[...]).astype(near_ref.dtype)
            far_ref[...] = tn(left[:, half:], right[...]).astype(far_ref.dtype)

        first = end


def paired_slopes(lefts, rights):
    tile = 512
    rows, depth = lefts[0].shape
    half = depth // 2
    starts, ends = [], []
    total = 0
    for right in rights:
        starts.append(total)
        total += right.shape[1] // tile
        ends.append(total)

    def column(start, end):
        return lambda i: (0, jnp.clip(i - start, 0, end - start - 1))

    whole = pl.BlockSpec((rows, depth), lambda i: (0, 0))
    out = pl.BlockSpec((half, tile), lambda i: (0, i))
    shape = jax.ShapeDtypeStruct((half, total * tile), jnp.bfloat16)
    near, far = pl.pallas_call(
        functools.partial(slopes_kernel, tuple(ends)),
        grid=(total,),
        in_specs=[whole] * len(lefts)
        + [pl.BlockSpec((rows, tile), column(a, b)) for a, b in zip(starts, ends)],
        out_specs=[out, out],
        out_shape=[shape, shape],
        compiler_params=pltpu.CompilerParams(vmem_limit_bytes=24 * 1024 * 1024),
        cost_estimate=pl.CostEstimate(
            flops=0,
            bytes_accessed=1 << 20,
            transcendentals=0,
        ),
    )(*lefts, *rights)
    return near, far


def split_rows(pair):
    return [part.reshape(CHIPS, part.shape[0] // CHIPS, part.shape[1]) for part in pair]


def dense_kernel(flipped, scaled, halves, lefts, *refs):
    left_refs, right_ref, refs = refs[:lefts], refs[lefts], refs[lefts + 1 :]
    scale_ref, outs = (refs[0], refs[1:]) if scaled else (None, refs)
    rows = sum(ref.shape[0] for ref in left_refs)
    chunk = rows // 6
    for part in range(6):
        lines = slice(part * chunk, (part + 1) * chunk)
        product = nt if flipped else functools.partial(jnp.dot, preferred_element_type=jnp.float32)
        left = left_refs[part * lefts // 6]
        start = part * chunk % left.shape[0]
        value = product(left[start : start + chunk, :], right_ref[...])
        if scaled:
            value = value * scale_ref[lines, :].astype(jnp.float32)
        if halves:
            out, first = (outs[0], 0) if part < 3 else (outs[1], rows // 2)
            out[part * chunk - first : (part + 1) * chunk - first, :] = value.astype(out.dtype)
        else:
            outs[0][lines, :] = value.astype(outs[0].dtype)


def dense(lefts, right, flipped, scale=None, halves=False):
    rows, depth = sum(left.shape[0] for left in lefts), lefts[0].shape[1]
    count = right.shape[0] if flipped else right.shape[1]
    tile = 512
    specs = [
        *(
            pl.BlockSpec(left.shape, lambda i: (0, 0), pipeline_mode=pl.Buffered(1))
            for left in lefts
        ),
        pl.BlockSpec((tile, depth), lambda i: (i, 0))
        if flipped
        else pl.BlockSpec((depth, tile), lambda i: (0, i)),
    ]
    args = [*lefts, right]
    if scale is not None:
        specs.append(pl.BlockSpec((rows, tile), lambda i: (0, i)))
        args.append(scale)
    if halves:
        kinds = [(rows // 2, jnp.float32), (rows // 2, jnp.bfloat16)]
    else:
        kinds = [(rows, jnp.bfloat16)]
    return pl.pallas_call(
        functools.partial(dense_kernel, flipped, scale is not None, halves, len(lefts)),
        grid=(count // tile,),
        in_specs=specs,
        out_specs=[pl.BlockSpec((size, tile), lambda i: (0, i)) for size, _ in kinds],
        out_shape=[jax.ShapeDtypeStruct((size, count), kind) for size, kind in kinds],
        compiler_params=pltpu.CompilerParams(vmem_limit_bytes=24 * 1024 * 1024),
        cost_estimate=pl.CostEstimate(flops=0, bytes_accessed=1 << 20, transcendentals=0),
    )(*[pltpu.with_memory_space_constraint(a, pltpu.MemorySpace.HBM) for a in args])


def mix_kernel(place, main_ref, low_ref, high_ref, taps_ref, mix_ref, back_ref, slope_ref, wide):
    strip, side, width = mix_ref.shape
    top, bottom = place[0] > 0, place[0] + strip < place[1]
    blank = jnp.zeros((PAD, LANES), jnp.float32)
    for first in range(0, width, LANES):
        for kind in range(2):
            lanes = slice(kind * width + first, kind * width + first + LANES)
            for slot in range(strip + 2):
                if slot == 0:
                    value = jnp.where(top, low_ref[0, :, lanes].astype(jnp.float32), 0.0)
                elif slot == strip + 1:
                    value = jnp.where(bottom, high_ref[0, :, lanes].astype(jnp.float32), 0.0)
                else:
                    value = main_ref[slot - 1, :, lanes].astype(jnp.float32)
                wide[kind, slot, 0:PAD] = blank
                wide[kind, slot, PAD : PAD + side] = value
                wide[kind, slot, PAD + side : 2 * PAD + side] = blank
        own = slice(first, first + LANES)
        taps = taps_ref[:, own].astype(jnp.float32)
        sums = [jnp.zeros((side, LANES), jnp.float32) for _ in range(9)]
        for row in range(strip):
            grad = wide[1, row + 1, PAD : PAD + side]
            mixed = jnp.zeros((side, LANES), jnp.float32)
            back = jnp.zeros((side, LANES), jnp.float32)
            for a in range(3):
                for b in range(3):
                    tap = 3 * a + b
                    span = slice(PAD + b - 1, PAD + b - 1 + side)
                    value = wide[0, row + a, span]
                    mixed = mixed + value * taps[tap : tap + 1]
                    back = back + wide[1, row + a, span] * taps[8 - tap : 9 - tap]
                    sums[tap] = sums[tap] + value * grad
            mix_ref[row, :, own] = mixed
            back_ref[row, :, own] = back
        for tap in range(9):
            slope_ref[tap : tap + 1, own] = jnp.sum(sums[tap], axis=0, keepdims=True)


def mix(place, both, low, high, taps):
    strip, side, double = both.shape
    width = double // 2
    grid = jax.ShapeDtypeStruct((strip, side, width), jnp.float32)
    return pl.pallas_call(
        mix_kernel,
        in_specs=[SCALARS] + [pl.BlockSpec(memory_space=pltpu.VMEM)] * 4,
        out_specs=[pl.BlockSpec(memory_space=pltpu.VMEM)] * 3,
        out_shape=[grid, grid, jax.ShapeDtypeStruct(taps.shape, jnp.float32)],
        scratch_shapes=[pltpu.VMEM((2, strip + 2, side + 2 * PAD, LANES), jnp.float32)],
        compiler_params=pltpu.CompilerParams(vmem_limit_bytes=16 * 1024 * 1024),
        cost_estimate=pl.CostEstimate(flops=0, bytes_accessed=1 << 20, transcendentals=0),
    )(place, both, low, high, taps)


def row_moments(value):
    average = jnp.mean(value, axis=-1, keepdims=True)
    centred = value - average
    spread = jnp.mean(centred * centred, axis=-1, keepdims=True)
    rate = lax.rsqrt(spread + norm_epsilon)
    return centred * rate, rate


def wide_sum(refs):
    total = refs[0][...].astype(jnp.float32)
    for ref in refs[1:]:
        total = total + ref[...].astype(jnp.float32)
    return total


def norm_kernel(count, *refs):
    gain = refs[count][...].astype(jnp.float32)
    total = wide_sum(refs[:count])
    outs = refs[count + 1 :]
    shape, _ = row_moments(total)
    outs[-1][...] = (shape * gain).astype(outs[-1].dtype)
    if count > 1:
        outs[0][...] = total


def norm_back_kernel(kinds, value_ref, own_ref, other_ref, gain_ref, *refs):
    extra, (slope_ref, *outs) = (refs[0], refs[1:]) if kinds[0] else (None, refs)
    gain = gain_ref[...].astype(jnp.float32)
    shape, rate = row_moments(value_ref[...].astype(jnp.float32))
    grad = own_ref[...].astype(jnp.float32) + other_ref[...].astype(jnp.float32)
    scaled = grad * gain
    first = jnp.mean(scaled, axis=-1, keepdims=True)
    second = jnp.mean(scaled * shape, axis=-1, keepdims=True)
    result = rate * (scaled - first - shape * second)
    if extra is not None:
        result = result + extra[...]
    for out in outs:
        out[...] = result.astype(out.dtype)
    slope = jnp.sum(grad * shape, axis=0, keepdims=True)

    @pl.when(pl.program_id(0) == 0)
    def _():
        slope_ref[...] = slope

    @pl.when(pl.program_id(0) > 0)
    def _():
        slope_ref[...] += slope


ROWS = 144
CHEAP = pl.CostEstimate(flops=0, bytes_accessed=1 << 20, transcendentals=0)


def row_block(width):
    return pl.BlockSpec((ROWS, width), lambda i: (i, 0))


def norm(values, gain):
    rows, width = values[0].shape
    whole = pl.BlockSpec((1, width), lambda i: (0, 0))
    kinds = [jnp.float32, jnp.bfloat16] if len(values) > 1 else [jnp.bfloat16]
    return pl.pallas_call(
        functools.partial(norm_kernel, len(values)),
        grid=(rows // ROWS,),
        in_specs=[row_block(width)] * len(values) + [whole],
        out_specs=[row_block(width)] * len(kinds),
        out_shape=[jax.ShapeDtypeStruct((rows, width), kind) for kind in kinds],
        compiler_params=pltpu.CompilerParams(vmem_limit_bytes=24 * 1024 * 1024),
        cost_estimate=CHEAP,
    )(*values, gain[None])


def norm_back(value, own, other, gain, kinds, extra=None):
    rows, width = value.shape
    whole = pl.BlockSpec((1, width), lambda i: (0, 0))
    more = [] if extra is None else [extra]
    return pl.pallas_call(
        functools.partial(norm_back_kernel, (extra is not None,)),
        grid=(rows // ROWS,),
        in_specs=[row_block(width)] * 3 + [whole] + [row_block(width)] * len(more),
        out_specs=[whole] + [row_block(width)] * len(kinds),
        out_shape=[jax.ShapeDtypeStruct((1, width), jnp.float32)]
        + [jax.ShapeDtypeStruct((rows, width), kind) for kind in kinds],
        compiler_params=pltpu.CompilerParams(vmem_limit_bytes=24 * 1024 * 1024),
        cost_estimate=CHEAP,
    )(value, own, other, gain[None], *more)


def gate_kernel(hidden_ref, own_ref, other_ref, gate_ref, cot_ref, result_ref, gating_ref, low_ref):
    result = wide_sum((hidden_ref, own_ref, other_ref))
    result_ref[...] = result
    total = jnp.sum(result * gate_ref[...].astype(jnp.float32), axis=-1, keepdims=True)
    gating = jax.nn.sigmoid(total)
    gating_ref[...] = jnp.broadcast_to(gating, gating_ref.shape)
    low_ref[...] = (cot_ref[...].astype(jnp.float32) * gating).astype(low_ref.dtype)


def gate(hidden, own, other, vector, cot):
    rows, width = hidden.shape
    return pl.pallas_call(
        gate_kernel,
        out_shape=[
            jax.ShapeDtypeStruct((rows, width), jnp.float32),
            jax.ShapeDtypeStruct((rows, LANES), jnp.float32),
            jax.ShapeDtypeStruct(cot.shape, jnp.bfloat16),
        ],
        compiler_params=pltpu.CompilerParams(vmem_limit_bytes=24 * 1024 * 1024),
        cost_estimate=CHEAP,
    )(hidden, own, other, vector[None], cot)


def rotated(start):
    return tuple(RINGS[(start + i) % len(RINGS)] for i in range(len(RINGS)))


def xor_swap(values, mask):
    count = lax.axis_size("dp")
    return lax.ppermute(values, "dp", [(i, i ^ mask) for i in range(count)])


def chip_offset(place, order, low_first):
    offset = 0
    for k, mask in enumerate(order):
        bit = k if low_first else len(order) - 1 - k
        offset = offset ^ (((place >> bit) & 1) * (mask >> 1))
    return offset


def together(values):
    return list(lax.optimization_barrier(tuple(values)))


def after(value, *others):
    return lax.optimization_barrier((value,) + others)[0]


def gathered_parts(blocks, orders, early, work):
    held = [block[None] for block in blocks]
    count, last = len(blocks), len(RINGS) - 1
    tied = early
    for step in range(last):
        other = [xor_swap(part, order[step]) for part, order in zip(held, orders)]
        held = [jnp.concatenate([a, b], axis=0) for a, b in zip(held, other)]
        done = together(held + (tied if step == last - 2 else []))
        held = done[:count]
        if step == last - 2:
            tied = done[count:]
    other = [xor_swap(part, order[last]) for part, order in zip(held, orders)]
    done = together(other + work(*tied))
    return held, done[:count], done[count:]


def split_sum(kept, other):
    half = kept.shape[0] // 2
    if half == 0:
        return kept.astype(jnp.float32) + other.astype(jnp.float32), None
    return kept[:half] + other[:half], kept[half:] + other[half:]


class Scatter:
    def __init__(self, kept, given, orders):
        self.kept, self.given, self.orders = list(kept), list(given), orders
        self.step = 0

    def advance(self, *tied):
        other = [
            xor_swap(part, order[self.step]) for part, order in zip(self.given, self.orders)
        ]
        done = together(other + list(tied))
        sums = [split_sum(own, got) for own, got in zip(self.kept, done)]
        self.kept, self.given = [low for low, _ in sums], [high for _, high in sums]
        self.step += 1
        return done[len(other) :]

    def result(self):
        return [part[0] for part in self.kept]


def route_kernel(moves, steps, n_in, n_out, place, *refs):
    ins, outs = refs[:n_in], refs[n_in : n_in + n_out]
    held = refs[n_in + n_out : n_in + 2 * n_out]
    sems = refs[n_in + 2 * n_out]
    device = place[0]
    chip, core = device >> 1, device & 1

    for target in range(n_out):

        def step(index, carry):
            for source, take, goal, put, source_box, target_box in moves:
                if goal == target:
                    pltpu.make_async_copy(
                        ins[source].at[(take(chip, core, index),) + source_box],
                        held[goal].at[(put(chip, core, index),) + target_box],
                        sems.at[goal],
                    ).start()
            return carry

        lax.fori_loop(0, steps, step, 0)
    for target in range(n_out):
        pltpu.make_async_copy(held[target], held[target], sems.at[target]).wait()
        pltpu.make_async_copy(held[target], outs[target], sems.at[target]).start()
    for target in range(n_out):
        pltpu.make_async_copy(held[target], outs[target], sems.at[target]).wait()


def route(moves, steps, place, arrays, shapes):
    anywhere = pl.BlockSpec(memory_space=pl.ANY)
    volume = sum(2 * a.size for a in arrays)
    return pl.pallas_call(
        functools.partial(route_kernel, moves, steps, len(arrays), len(shapes)),
        in_specs=[SCALARS] + [anywhere] * len(arrays),
        out_specs=[anywhere] * len(shapes),
        out_shape=[jax.ShapeDtypeStruct(s, jnp.bfloat16) for s in shapes],
        scratch_shapes=[pltpu.VMEM(s, jnp.bfloat16) for s in shapes]
        + [pltpu.SemaphoreType.DMA((len(shapes),))],
        compiler_params=pltpu.CompilerParams(vmem_limit_bytes=volume + volume // 4 + (4 << 20)),
        cost_estimate=CHEAP,
    )(place, *arrays)


def box(rows, cols):
    return (pl.ds(rows[0], rows[1] - rows[0]), pl.ds(cols[0], cols[1] - cols[0]))


def overlap(first, second):
    low, high = max(first[0], second[0]), min(first[1], second[1])
    return (low, high) if low < high else None


def shifted_span(span, base):
    return (span[0] - base, span[1] - base)


def core_swap(values):
    return xor_swap(values, CORE)


def model_swap(values):
    return lax.ppermute(values, "mp", [(0, 1), (1, 0)])


def exchange(values):
    low = values.astype(jnp.bfloat16)
    other = model_swap(low)
    return low.astype(jnp.float32) + other.astype(jnp.float32)


def halo_rows(block, width):
    count = lax.axis_size("dp")
    forward = [(i, (i + 1) % count) for i in range(count)]
    backward = [((i + 1) % count, i) for i in range(count)]
    low = lax.ppermute(block[block.shape[0] - width :], "dp", forward)
    high = lax.ppermute(block[:width], "dp", backward)
    return low, high


def gelu_pair(values):
    below = 0.5 * (1.0 + lax.erf(values * 0.5**0.5))
    slope = below + values * (jnp.exp(-0.5 * values * values) * (2.0 * jnp.pi) ** -0.5)
    return (values * below).astype(jnp.bfloat16), slope.astype(jnp.bfloat16)


def matmul(former, latter):
    return jnp.dot(former, latter, preferred_element_type=jnp.float32)


def matmul_nt(former, latter):
    return lax.dot_general(
        former, latter, (((1,), (1,)), ((), ())), preferred_element_type=jnp.float32
    )


def matmul_tn(former, latter):
    return lax.dot_general(
        former, latter, (((0,), (0,)), ((), ())), preferred_element_type=jnp.float32
    )


def pair_swap(values):
    chips = lax.axis_size("dp") // 2
    pairs = []
    for chip in range(chips):
        other = (chip + 1) % chips if chip % 2 else (chip - 1) % chips
        pairs += [(2 * chip + core, 2 * other + core) for core in range(2)]
    return lax.ppermute(values, "dp", pairs)


def own_half(first, core, axis, other=False):
    size = first.shape[axis] // 2
    low = lax.slice_in_dim(first, 0, size, axis=axis)
    high = lax.slice_in_dim(first, size, 2 * size, axis=axis)
    return jnp.where((core == 0) != other, low, high)


def in_core_order(own, other, core, axis):
    return jnp.where(
        core == 0,
        jnp.concatenate([own, other], axis=axis),
        jnp.concatenate([other, own], axis=axis),
    )


def row_places(device, order, depth):
    chip, core = device >> 1, device & 1
    place = jnp.arange(2 * CHIPS * depth)
    block, line = place // depth, place % depth
    owner = 2 * (chip ^ chip_offset(block % CHIPS, order, True)) + (core ^ (block // CHIPS))
    return owner * depth + line


def row_picker(device, order, depth):
    places = row_places(device, order, depth)
    rows = lax.broadcasted_iota(jnp.int32, (places.shape[0], places.shape[0]), 0)
    return (rows == places[None, :]).astype(jnp.bfloat16)


def all_weights(place, core, small_rows, common_rows, *ties):
    middle = small_rows[4].shape[1] // 2
    first = jnp.concatenate(small_rows[:4] + (small_rows[4][:, :middle],), axis=1)
    second = jnp.concatenate([small_rows[4][:, middle:], small_rows[5]], axis=1)
    kept = jnp.concatenate([own_half(rows, core, 1) for rows in common_rows], axis=1)
    given = jnp.concatenate([own_half(rows, core, 1, True) for rows in common_rows], axis=1)
    common = in_core_order(kept, core_swap(given), core, 0)
    rows = common.shape[0]
    widths = [block.shape[1] // 2 for block in common_rows]
    spans = even_edges(common.shape[1], 3)
    orders = [rotated(i) for i in range(5)]
    held, other, extra = gathered_parts(
        [first, second] + [common[:, low:high] for low, high in spans], orders, *ties
    )
    near = [jnp.concatenate([a, b], axis=0) for a, b in zip(held[:2], other[:2])]
    far = [core_swap(part) for part in near]
    small = [
        tuple(part.reshape(-1, part.shape[2]) for part in pair) for pair in zip(near, far)
    ]
    starts = [0]
    for width in widths:
        starts.append(starts[-1] + width)
    moves = []
    half = CHIPS // 2
    for i, span in enumerate(spans):
        order = orders[i + 2]
        for target in range(len(widths)):
            cols_span = (starts[target], starts[target + 1])
            shared = overlap(cols_span, span)
            if shared is None:
                continue
            for side in range(2):

                def put(chip, core, index, side=side, order=order):
                    return chip ^ chip_offset(index + side * half, order, True)

                moves.append(
                    (
                        2 * i + side,
                        lambda chip, core, index: index,
                        target,
                        put,
                        box((0, rows), shifted_span(shared, span[0])),
                        box((0, rows), shifted_span(shared, cols_span[0])),
                    )
                )
    arrays = [part for pair in zip(held[2:], other[2:]) for part in pair]
    large = route(moves, half, place, arrays, [(CHIPS, rows, width) for width in widths])
    expand, shrink, adapter = [part.reshape(CHIPS * rows, part.shape[2]) for part in large]
    adapter = in_core_order(adapter, core_swap(adapter), core, 1)
    return small, expand, shrink, adapter, extra


def even_edges(width, count):
    tiles = width // LANES
    edges = [LANES * ((tiles * i + count - 1) // count) for i in range(count + 1)]
    return [(edges[i], edges[i + 1]) for i in range(count)]


def turn(left_refs, turned):
    first = 0
    for left_ref in left_refs:
        rows = left_ref.shape[0]
        for start in range(0, left_ref.shape[1], LANES):
            lanes = slice(start, start + LANES)
            turned[lanes, first : first + rows] = left_ref[:, lanes].T
        first += rows


def slope_pack_kernel(orders, spans, place, *refs):
    first_lefts, second_lefts, (right_a, right_b, extra_ref) = refs[:2], refs[2:4], refs[4:7]
    outs, (turned, tile, sems) = refs[7:-3], refs[-3:]
    width = right_a.shape[1]
    step = pl.program_id(0)
    per_side = turned.shape[0] // width
    total = 2 * per_side + 1
    blocks, rows = tile.shape[1], tile.shape[2]
    group = blocks // 4
    chip = place[0] >> 1
    slot = step % 2

    def sent(which, wide):
        box_ref = tile.at[which, :, :, pl.ds(0, wide)]
        return pltpu.make_async_copy(box_ref, box_ref, sems.at[which])

    @pl.when(step >= 2)
    def _():
        sent(slot, width).wait()

    @pl.when(step == 0)
    def _():
        turn(first_lefts, turned)

    @pl.when(step == per_side)
    def _():
        turn(second_lefts, turned)

    def fill(right):
        for part in range(4):
            lines = slice(part * group * rows, (part + 1) * group * rows)
            value = jnp.dot(turned[lines, :], right[...], preferred_element_type=jnp.float32)
            tile[slot, part * group : (part + 1) * group] = value.astype(tile.dtype).reshape(
                group, rows, width
            )

    @pl.when(step < per_side)
    def _():
        fill(right_a)

    @pl.when((step >= per_side) & (step < 2 * per_side))
    def _():
        fill(right_b)

    last = extra_ref.shape[2]

    @pl.when(step == 2 * per_side)
    def _():
        tile[slot, :, :, 0:last] = extra_ref[...]

    for index in range(total):
        begin = index * width
        wide = width if index < 2 * per_side else last
        goal = [i for i, span in enumerate(spans) if span[0] <= begin < span[1]][0]
        cols = pl.ds(begin - spans[goal][0], wide)

        @pl.when(step == index)
        def _(goal=goal, cols=cols, wide=wide):
            def send(spot, carry):
                for side in range(2):
                    owner = chip ^ chip_offset(spot + side * (blocks // 2), orders[goal], True)
                    pltpu.make_async_copy(
                        tile.at[slot, owner, :, pl.ds(0, wide)],
                        outs[2 * goal + side].at[spot, :, cols],
                        sems.at[slot],
                    ).start()
                return carry

            lax.fori_loop(0, blocks // 2, send, 0)

    @pl.when(step == total - 1)
    def _():
        sent(1 - slot, width).wait()
        sent(slot, last).wait()


def packed_slopes(place, orders, spans, first_lefts, right_a, second_lefts, right_b, extra):
    channels = first_lefts[0].shape[1]
    depth, hidden = right_a.shape
    width = 384
    steps = hidden // width
    rows = channels // CHIPS
    extra = extra.reshape(CHIPS, rows, extra.shape[1])
    once = pl.Buffered(1)
    return pl.pallas_call(
        functools.partial(slope_pack_kernel, orders, spans),
        grid=(2 * steps + 1,),
        in_specs=[SCALARS]
        + [
            pl.BlockSpec(left.shape, lambda i: (0, 0), pipeline_mode=once)
            for left in (*first_lefts, *second_lefts)
        ]
        + [
            pl.BlockSpec((depth, width), lambda i: (0, jnp.minimum(i, steps - 1))),
            pl.BlockSpec((depth, width), lambda i: (0, jnp.clip(i - steps, 0, steps - 1))),
            pl.BlockSpec(extra.shape, lambda i: (0, 0, 0), pipeline_mode=once),
        ],
        out_specs=[pl.BlockSpec(memory_space=pl.ANY)] * (2 * len(spans)),
        out_shape=[
            jax.ShapeDtypeStruct((CHIPS // 2, rows, high - low), jnp.bfloat16)
            for low, high in spans
            for _ in range(2)
        ],
        scratch_shapes=[
            pltpu.VMEM((channels, depth), jnp.bfloat16),
            pltpu.VMEM((2, CHIPS, rows, width), jnp.bfloat16),
            pltpu.SemaphoreType.DMA((2,)),
        ],
        compiler_params=pltpu.CompilerParams(vmem_limit_bytes=40 * 1024 * 1024),
        cost_estimate=CHEAP,
    )(place, *first_lefts, *second_lefts, right_a, right_b, extra)


def unpacked_map_slopes(core, blocks, widths):
    block = jnp.concatenate(blocks, axis=1)
    own = own_half(block, core, 0)
    got = core_swap(own_half(block, core, 0, True).astype(jnp.bfloat16)).astype(jnp.float32)
    outs = []
    start = 0
    for width in widths:
        outs.append(
            in_core_order(own[:, start : start + width], got[:, start : start + width], core, 1)
        )
        start += width
    return outs


def row_sums(values):
    count = values.shape[0]
    pieces = lax.all_to_all(values, "dp", 0, 0, tiled=True)
    return jnp.sum(pieces.astype(jnp.float32), axis=0)


def row_copies(row):
    count = lax.axis_size("dp")
    return lax.all_to_all(jnp.broadcast_to(row[None], (count,) + row.shape), "dp", 0, 0, tiled=True)


def on_device(
    lowres_in,
    highres_in,
    image_sizes,
    attn_gain,
    query_weight,
    key_weight,
    value_weight,
    output_weight,
    mlp_gain,
    up_weight,
    down_weight,
    depth_kernel,
    conv_gain,
    expand_weight,
    shrink_weight,
    layer_scale,
    adapter_weight,
    adapter_kernel,
    gate_vector,
    out_cotangent,
    map_cotangent,
):
    device = lax.axis_index("dp")
    core = device & 1
    place = device.reshape(1).astype(jnp.int32)
    group_count = lax.axis_size("dp") // TILES
    position = (device + 2) % TILES
    group_id = (device + 2) // TILES % group_count
    model_half = lax.axis_index("mp")
    low_strip, _, grid_side, width = lowres_in.shape
    high_strip, _, high_side, channels = highres_in.shape
    own_width = adapter_kernel.shape[1]
    local_width = query_weight.shape[1]
    local_heads = local_width // HD
    scaling = HD ** (-0.5)
    token_count = low_strip * grid_side
    pixel_count = high_strip * high_side

    high_map = highres_in.reshape(high_strip, high_side, channels)
    table_ids = jnp.arange(image_sizes.shape[0])
    extent = jnp.sum(jnp.where(table_ids == group_id, image_sizes, 0))
    first_row = position * high_strip
    map_place = jnp.stack([first_row, extent]).astype(jnp.int32)
    token_low = lowres_in.reshape(token_count, width)
    local_grad_low = out_cotangent.reshape(low_strip, grid_side, own_width)
    backs = []
    depth = query_weight.shape[0]
    pickers = [row_picker(device, rotated(i), depth) for i in range(2)]

    def convolve(map_low, map_high):
        convolved = map_conv(map_place, high_map, map_low, map_high, depth_kernel)
        convolved = convolved.reshape(pixel_count, channels)
        (normed_low,) = norm([token_low], attn_gain)
        normed_first = matmul(normed_low, pickers[0]).astype(jnp.bfloat16)
        backs.extend([map_low, map_high, convolved])
        return [*norm([convolved], conv_gain), normed_low, normed_first]

    small, expand_full, shrink_full, adapter_full, extra = all_weights(
        place,
        core,
        (query_weight, key_weight, value_weight, output_weight.T, up_weight, down_weight.T),
        (expand_weight, shrink_weight.T, adapter_weight),
        list(halo_rows(high_map, RADIUS)),
        convolve,
    )
    map_low, map_high, convolved = backs
    normed_map_low, normed_low, normed_first = extra
    normed_map_given_low = core_swap(normed_map_low)
    normed_map_pair = jnp.concatenate([normed_map_low, normed_map_given_low], axis=0)
    triple = 3 * local_width
    quad = 4 * local_width
    hidden_width = up_weight.shape[1]
    hidden_half = hidden_width // 2

    def pieces(index, low, high):
        return [part[:, low:high] for part in small[index]]

    qkv_parts = pieces(0, 0, triple)
    output_parts = pieces(0, triple, quad)
    up_parts = [pieces(0, quad, quad + hidden_half), pieces(1, 0, hidden_half)]
    down_parts = pieces(1, hidden_half, hidden_half + hidden_width)

    def picked(values, index):
        return matmul(values, pickers[index]).astype(jnp.bfloat16)

    def restored(values, index):
        return matmul_nt(values.astype(jnp.bfloat16), pickers[index])

    def into(values, parts):
        half = values.shape[1] // 2
        return matmul(values[:, :half], parts[0]) + matmul(values[:, half:], parts[1])

    def outof(values, parts):
        return jnp.concatenate([matmul_nt(values, part) for part in parts], axis=1)

    qkv_rows = into(normed_first, qkv_parts).astype(jnp.bfloat16)
    pair = qkv_rows[:, local_width:]
    pair_other, expand_full, shrink_full = together([pair_swap(pair), expand_full, shrink_full])
    pair = jnp.concatenate([pair, pair_other], axis=0)
    pair = jnp.concatenate([pair, core_swap(pair)], axis=0)
    attended_low = attend(qkv_rows, pair)
    hidden_own = restored(outof(attended_low, output_parts), 0).astype(jnp.bfloat16)
    hidden_rows, normed_two_low = norm([token_low, hidden_own, model_swap(hidden_own)], mlp_gain)
    normed_two_picked = [picked(normed_two_low, i) for i in range(2)]
    expanded = jnp.concatenate(
        [into(normed_two_picked[i], up_parts[i]) for i in range(2)], axis=1
    )
    activated_low, activated_slope = gelu_pair(expanded)
    result_own = restored(outof(activated_low, down_parts), 1).astype(jnp.bfloat16)
    result_rows, gating, lifted_grad_low = gate(
        hidden_rows,
        result_own,
        model_swap(result_own),
        gate_vector,
        local_grad_low.reshape(token_count, own_width),
    )

    result_grid = result_rows.reshape(low_strip, grid_side, width)
    gate_wide = gate_vector.astype(jnp.float32)
    gating = gating[:, :1].reshape(low_strip, grid_side, 1)
    out_grad = local_grad_low.astype(jnp.float32)
    grid_shape = (low_strip, grid_side, channels)
    pooled_own = matmul_nt(lifted_grad_low, adapter_full).astype(jnp.bfloat16).reshape(grid_shape)
    pooled_other = model_swap(pooled_own)

    widened = matmul(normed_map_pair, expand_full)
    widened_low, widened_slope = gelu_pair(widened)
    widened_low = after(widened_low, pooled_own)
    narrowed_part, narrowed_given = dense([widened_low], shrink_full, True, halves=True)
    narrowed_part = narrowed_part + core_swap(narrowed_given).astype(jnp.float32)
    map_shape = (high_strip, high_side, channels)
    narrowed_own = narrowed_part.astype(jnp.bfloat16).reshape(map_shape)
    narrowed_own, pooled_other = together([narrowed_own, pooled_other])
    narrowed_other = model_swap(narrowed_own)

    map_grad, narrowed_grad_low = spread_map(
        map_place, pooled_own, pooled_other, map_cotangent.reshape(map_shape), layer_scale[None]
    )
    narrowed_grad_low = narrowed_grad_low.reshape(pixel_count, channels)
    narrowed_grad_pair = [narrowed_grad_low, core_swap(narrowed_grad_low)]
    (widened_grad_low,) = dense(narrowed_grad_pair, shrink_full, False, widened_slope)
    normed_map_part, normed_map_given = dense([widened_grad_low], expand_full, True, halves=True)
    normed_map_given, narrowed_other = together([normed_map_given, narrowed_other])
    normed_map_part = normed_map_part + core_swap(normed_map_given).astype(jnp.float32)
    normed_map_own = normed_map_part.astype(jnp.bfloat16)

    mapped, pooled_low, layer_scale_slope = blend_map(
        map_place, narrowed_own, narrowed_other, high_map, layer_scale[None], map_grad
    )
    pooled_low = pooled_low.reshape(token_count, channels)
    lifted = matmul(pooled_low, adapter_full).reshape(low_strip, grid_side, own_width)

    own_result = lax.dynamic_slice_in_dim(result_grid, model_half * own_width, own_width, 2)
    own_result_low = own_result.astype(jnp.bfloat16)
    both_low = jnp.concatenate([own_result_low, local_grad_low], axis=2)
    both_edges = halo_rows(after(both_low, widened_grad_low), 1)
    mix_place = jnp.stack([position * low_strip, TILES * low_strip]).astype(jnp.int32)
    local_mix, local_back, adapter_kernel_slope = mix(
        mix_place, both_low, *both_edges, adapter_kernel
    )
    blended = own_result + local_mix + gating * lifted

    gate_part = jnp.sum(out_grad * lifted, axis=-1, keepdims=True)
    gate_grad = exchange(gate_part)
    adapter_slope = matmul_tn(pooled_low, lifted_grad_low)
    adapter_slope = own_half(adapter_slope, core, 1) + core_swap(
        own_half(adapter_slope, core, 1, True).astype(jnp.bfloat16)
    ).astype(jnp.float32)
    own_grad = out_grad + local_back
    own_grad_low = own_grad.astype(jnp.bfloat16)
    other_grad = model_swap(own_grad_low)
    result_grad = in_core_order(own_grad_low, other_grad, model_half, 2).astype(jnp.float32)
    gate_slope = gate_grad * gating * (1.0 - gating)
    gate_vector_slope = jnp.sum((gate_slope * result_grid).reshape(token_count, width), axis=0)
    result_grad = (result_grad + gate_slope * gate_wide).reshape(token_count, width)

    result_low = after(result_grad.astype(jnp.bfloat16), widened_grad_low)
    result_picked = picked(result_low, 1)
    activated_grad = into(result_picked, down_parts)
    expanded_grad_low = (activated_grad * activated_slope.astype(jnp.float32)).astype(jnp.bfloat16)
    expanded_grad_parts = [expanded_grad_low[:, :hidden_half], expanded_grad_low[:, hidden_half:]]
    second_slopes = split_rows(
        paired_slopes(
            (normed_two_picked[1], result_picked), (expanded_grad_parts[1], activated_low)
        )
    )
    normed_two_own = sum(
        restored(outof(expanded_grad_parts[i], up_parts[i]), i) for i in range(2)
    ).astype(jnp.bfloat16)
    normed_two_other = model_swap(normed_two_own)
    normed_two_other, normed_map_own, *second_slopes = together(
        [normed_two_other, normed_map_own, *second_slopes]
    )
    second_far = core_swap(second_slopes[1])
    normed_map_other = model_swap(normed_map_own)
    mlp_gain_slope, hidden_grad, hidden_low = norm_back(
        hidden_rows,
        normed_two_own,
        normed_two_other,
        mlp_gain,
        (jnp.float32, jnp.bfloat16),
        result_grad,
    )
    hidden_picked = picked(hidden_low, 0)
    attended_grad_low = into(hidden_picked, output_parts).astype(jnp.bfloat16)
    query_grad_rows, key_grad_all, value_grad_all = attend_back(qkv_rows, pair, attended_grad_low)
    pair_back = jnp.concatenate(
        [key_grad_all, value_grad_all], axis=1
    )
    pair_back = pair_back[: 2 * token_count] + core_swap(
        pair_back[2 * token_count :].astype(jnp.bfloat16)
    ).astype(jnp.float32)
    pair_given, late_place = together([pair_back[token_count:].astype(jnp.bfloat16), place])
    pair_other = pair_swap(pair_given)
    map_widths = (widened_low.shape[1], widened_low.shape[1], adapter_slope.shape[1])
    map_slopes_packed = packed_slopes(
        late_place,
        [rotated(i) for i in range(2, 5)],
        even_edges(sum(map_widths), 3),
        [normed_map_low, normed_map_given_low],
        widened_grad_low,
        narrowed_grad_pair,
        widened_low,
        adapter_slope.astype(jnp.bfloat16),
    )
    second_near = split_sum(second_slopes[0], second_far)
    pair_other, normed_map_other, *rest = together(
        [pair_other, normed_map_other, *second_near, *map_slopes_packed]
    )
    second_near, map_slopes_packed = rest[:2], rest[2:]
    pair_back = pair_back[:token_count] + pair_other.astype(jnp.float32)
    qkv_grad = jnp.concatenate([query_grad_rows, pair_back.astype(jnp.bfloat16)], axis=1)
    normed_own = restored(outof(qkv_grad, qkv_parts), 0).astype(jnp.bfloat16)
    normed_other = model_swap(normed_own)
    conv_gain_slope, convolved_grad_low = norm_back(
        convolved, normed_map_own, normed_map_other, conv_gain, (jnp.bfloat16,)
    )
    convolved_grad_low = convolved_grad_low.reshape(map_shape)
    convolved_grad_low, qkv_grad = together([convolved_grad_low, qkv_grad])
    grad_low, grad_high = halo_rows(convolved_grad_low, RADIUS)
    first_slopes = split_rows(
        paired_slopes(
            (normed_first, hidden_picked, normed_two_picked[0]),
            (qkv_grad, attended_low, expanded_grad_parts[0]),
        )
    )
    first_far = core_swap(first_slopes[1])
    grad_low, grad_high, *map_slopes_packed = together(
        [grad_low, grad_high, *map_slopes_packed]
    )
    near = [split_sum(first_slopes[0], first_far), second_near]
    scatter = Scatter(
        [low for low, _ in near] + list(map_slopes_packed[0::2]),
        [high for _, high in near] + list(map_slopes_packed[1::2]),
        [rotated(i)[::-1] for i in range(5)],
    )

    depth_kernel_slope = map_slopes(map_place, high_map, map_low, map_high, convolved_grad_low)
    highres_grad = map_conv(
        map_place, convolved_grad_low, grad_low, grad_high, depth_kernel, map_grad
    )
    attn_gain_slope, lowres_grad = norm_back(
        token_low, normed_own, normed_other, attn_gain, (jnp.float32,), hidden_grad
    )
    lowres_grad = lowres_grad.reshape(low_strip, 1, grid_side, width)

    def as_rows(values):
        return jnp.pad(values, ((0, 0), (0, channels - values.shape[1])))

    minor_rows = jnp.concatenate(
        [
            depth_kernel_slope,
            conv_gain_slope,
            layer_scale_slope,
            as_rows(
                jnp.concatenate([attn_gain_slope, mlp_gain_slope, gate_vector_slope[None]], axis=0)
            ),
            as_rows(adapter_kernel_slope),
        ],
        axis=0,
    )
    lines = channels // LANES
    block_rows = -(-lines // 16) * 16
    minor = jnp.pad(
        minor_rows.astype(jnp.bfloat16).reshape(minor_rows.shape[0], lines, LANES),
        ((0, 2 * CHIPS - minor_rows.shape[0]), (0, block_rows - lines), (0, 0)),
    )
    minor_own = row_sums(minor).astype(jnp.bfloat16)
    highres_grad, minor_own = scatter.advance(highres_grad, minor_own)
    minor_copies = row_copies(minor_own)
    (minor_copies,) = scatter.advance(minor_copies)
    minor_all = (
        minor_copies[:, :lines].reshape(2 * CHIPS, channels).astype(jnp.float32)
    )
    while scatter.step < len(RINGS):
        scatter.advance()
    first_own, second_own, *map_blocks = scatter.result()
    up_own = jnp.concatenate([first_own[:, quad:], second_own[:, :hidden_half]], axis=1)
    down_own = second_own[:, hidden_half:]
    expand_own, shrink_own, adapter_own = unpacked_map_slopes(
        core,
        map_blocks,
        map_widths,
    )
    firsts = [first_own[:, i * local_width : (i + 1) * local_width] for i in range(4)]
    taps = depth_kernel.shape[0]
    side_taps = adapter_kernel.shape[0]
    return (
        blended.astype(jnp.bfloat16)[:, None],
        mapped[:, None],
        lowres_grad,
        highres_grad[:, None],
        minor_all[taps + 2, :width],
        firsts[0],
        firsts[1],
        firsts[2],
        firsts[3].T,
        minor_all[taps + 3, :width],
        up_own,
        down_own.T,
        minor_all[:taps],
        minor_all[taps],
        expand_own,
        shrink_own.T,
        minor_all[taps + 1],
        adapter_own,
        minor_all[taps + 5 : taps + 5 + side_taps, :own_width],
        minor_all[taps + 4, :width],
    )


def solution(mesh):
    in_specs = (
        P("dp", None, None, None),
        P("dp", None, None, None),
        P(),
        P(),
        P("dp", "mp"),
        P("dp", "mp"),
        P("dp", "mp"),
        P("mp", "dp"),
        P(),
        P("dp", "mp"),
        P("mp", "dp"),
        P(),
        P(),
        P("dp", "mp"),
        P("mp", "dp"),
        P(),
        P("dp", "mp"),
        P(None, "mp"),
        P(),
        P("dp", None, None, "mp"),
        P("dp", None, None, None),
    )
    out_specs = (
        P("dp", None, None, "mp"),
        P("dp", None, None, None),
        P("dp", None, None, None),
        P("dp", None, None, None),
        P(),
        P("dp", "mp"),
        P("dp", "mp"),
        P("dp", "mp"),
        P("mp", "dp"),
        P(),
        P("dp", "mp"),
        P("mp", "dp"),
        P(),
        P(),
        P("dp", "mp"),
        P("mp", "dp"),
        P(),
        P("dp", "mp"),
        P(None, "mp"),
        P(),
    )
    return jax.shard_map(
        on_device, mesh=mesh, in_specs=in_specs, out_specs=out_specs, check_vma=False
    )
```
